512 devices in a mesh: wide: 32 (over x, z_lo), narrow: 16 (over z_hi, y, core).
Axes of the slice: x: 4, y: 4, z: 16 (z_hi: 2, z_lo: 8; z = z_hi * 8 + z_lo), core: 2. Of those that a mesh axis runs over, the one named last changes fastest.
Arguments:
- query_in: bfloat16 [32768, 4096], P(('wide', 'narrow')), may hold values from -100 to 100
- key_in: bfloat16 [32768, 4096], P(('wide', 'narrow')), may hold values from -20 to 20
- value_in: bfloat16 [32768, 4096], P(('wide', 'narrow')), may hold values from -3 to 3
- grad_out: bfloat16 [32768, 4096], P(('wide', 'narrow')), may hold values from -6 to 6
- row_start: int32 [32], replicated, may hold values from 0 to 1023
- col_start: int32 [8], replicated, may hold values from 0 to 31
Outputs:
- grad_query: bfloat16 [32768, 4096], P(('wide', 'narrow'))
- grad_key: bfloat16 [32768, 4096], P(('wide', 'narrow'))
- grad_value: bfloat16 [32768, 4096], P(('wide', 'narrow'))
The draws below stay inside these ranges and needn't reach their ends.
All inputs are finite; a program needn't handle non-finite values.
Results may differ from the reference program's by a relative error of at most 0.01055.
Values may be sent and summed in bfloat16 or wider, within the bound.
No kernel may reach another device: no remote copies, remote signals or barrier semaphores. Data moves between devices by JAX's collectives and lax.ppermute only.
A program may use at most 128 MiB of HBM per device.

```python
import jax
import jax.numpy as jnp
from jax import lax

HEADS = 32
HEAD = 128
COLS = 1024
CB = 128
ROWS = 32
TOKENS = 32768


def shared_keys(key):
    return jax.random.truncated_normal(jax.random.fold_in(key, 17), -4.0, 4.0, (TOKENS, HEADS * HEAD), jnp.float32)


def draw_key_in(key, part):
    shared = shared_keys(key)
    return shared.astype(jnp.bfloat16)


def draw_query_in(key, part):
    key = jax.random.fold_in(key, 5)
    own_part = jax.random.truncated_normal(key, -4.0, 4.0, (TOKENS, HEADS * HEAD), jnp.float32)
    return own_part.astype(jnp.bfloat16)


def set_ends(entries, rng, low, largest):
    longest = entries.shape.index(max(entries.shape))
    spots = []
    for shift in (0, 1):
        where = [jax.random.randint(jax.random.fold_in(rng, axis), (), 0, length) for axis, length in enumerate(entries.shape)]
        where[longest] = (where[longest] + shift) % entries.shape[longest]
        spots.append(tuple(where))
    return entries.at[spots[0]].set(low).at[spots[1]].set(largest)


def shard_levels(own_key, extent, pieces, low, high):
    def one(dim, parts):
        draws = jax.random.uniform(jax.random.fold_in(jax.random.fold_in(own_key, 6), dim), (parts,), jnp.float32, low / len(pieces), high / len(pieces))
        return jnp.repeat(jnp.exp(draws), extent[dim] // parts).reshape((-1,) + (1,) * (len(extent) - dim - 1))

    level = one(*pieces[0])
    for cut in pieces[1:]:
        level = level * one(*cut)
    return level


def scatter_about(key, dims, deviation, reach, shards=(), kind=jnp.bfloat16):
    values = jax.random.normal(key, dims, jnp.float32) * deviation
    if len(shards) > 0:
        values = shard_levels(key, dims, shards, -0.22, 0.18) * values
    return jnp.clip(values, min=-reach, max=reach).astype(kind)


def setup_inputs(seed: int = 0) -> dict:
    streams_of = jax.random.split(jax.random.key(seed), 7)
    query_in = draw_query_in(jax.random.fold_in(streams_of[6], 71), 0)
    key_in = draw_key_in(jax.random.fold_in(streams_of[6], 71), 0)
    value_in = scatter_about(streams_of[2], (TOKENS, HEADS * HEAD), 0.5, 3.0, ((0, 512),))
    grad_out = scatter_about(streams_of[3], (TOKENS, HEADS * HEAD), 1.0, 6.0, ((0, 512),))
    row_start = set_ends(jax.random.randint(streams_of[4], (ROWS,), 0, COLS), jax.random.fold_in(streams_of[4], 1), 0, COLS - 1).astype(jnp.int32)
    col_start = set_ends(jax.random.randint(streams_of[5], (COLS // CB,), 0, ROWS), jax.random.fold_in(streams_of[5], 1), 0, ROWS - 1).astype(jnp.int32)
    return dict(query_in=query_in, key_in=key_in, value_in=value_in, grad_out=grad_out, row_start=row_start, col_start=col_start)


masked_low = -1e30


def rounded(values):
    return lax.optimization_barrier(values.astype(jnp.bfloat16)).astype(jnp.float32)


def head_grads(inputs, row_start, col_start):
    queries, keys_in, values, grads = inputs
    score_scale = 1.0 / (HEAD ** 0.5)
    exact = lax.Precision.HIGHEST
    columns = jnp.arange(COLS, dtype=jnp.int32)
    row_ids = jnp.arange(ROWS, dtype=jnp.int32)
    row_mask = (columns[None, None, :] <= columns[None, :, None]) & ((columns[None, None, :] >= row_start[:, None, None]) | (columns[None, None, :] == columns[None, :, None]))
    col_first = col_start[columns // CB]
    col_mask = (row_ids[None, None, :] < row_ids[None, :, None]) & (row_ids[None, None, :] >= col_first[:, None, None])
    row_scores = jnp.einsum('rcd,red->rce', queries, keys_in, precision=exact) * score_scale
    col_scores = jnp.einsum('rcd,scd->crs', queries, keys_in, precision=exact) * score_scale
    maxima = jnp.maximum(jnp.max(jnp.where(row_mask, row_scores, masked_low), -1), jnp.max(jnp.where(col_mask, col_scores, masked_low), -1).T)
    totals = jnp.sum(jnp.where(row_mask, jnp.exp(row_scores - maxima[..., None]), 0.0), -1)
    totals = totals + jnp.sum(jnp.where(col_mask, jnp.exp(col_scores - maxima.T[..., None]), 0.0), -1).T
    log_norm = maxima + jnp.log(totals)
    row_probs = jnp.where(row_mask, jnp.exp(row_scores - log_norm[..., None]), 0.0)
    col_probs = jnp.where(col_mask, jnp.exp(col_scores - log_norm.T[..., None]), 0.0)
    row_dprob = jnp.einsum('rcd,red->rce', grads, values, precision=exact)
    col_dprob = jnp.einsum('rcd,scd->crs', grads, values, precision=exact)
    delta = jnp.sum(row_probs * row_dprob, -1) + jnp.sum(col_probs * col_dprob, -1).T
    row_dscore = rounded(row_probs * (row_dprob - delta[..., None]))
    col_dscore = rounded(col_probs * (col_dprob - delta.T[..., None]))
    row_weights = rounded(row_probs)
    col_weights = rounded(col_probs)
    grad_q = (jnp.einsum('rce,red->rcd', row_dscore, keys_in, precision=exact) + jnp.einsum('crs,scd->rcd', col_dscore, keys_in, precision=exact)) * score_scale
    grad_k = (jnp.einsum('rce,rcd->red', row_dscore, queries, precision=exact) + jnp.einsum('crs,rcd->scd', col_dscore, queries, precision=exact)) * score_scale
    grad_v = jnp.einsum('rce,rcd->red', row_weights, grads, precision=exact) + jnp.einsum('crs,rcd->scd', col_weights, grads, precision=exact)
    return grad_q, grad_k, grad_v


def split_heads(array):
    return array.astype(jnp.float32).reshape(ROWS, COLS, HEADS, HEAD).transpose(2, 0, 1, 3)


def join_heads(array):
    return array.transpose(1, 2, 0, 3).reshape(ROWS * COLS, HEADS * HEAD).astype(jnp.bfloat16)


def reference(query_in, key_in, value_in, grad_out, row_start, col_start):
    results = lax.map(lambda inputs: head_grads(inputs, row_start, col_start), (split_heads(query_in), split_heads(key_in), split_heads(value_in), split_heads(grad_out)))
    return join_heads(results[0]), join_heads(results[1]), join_heads(results[2])
```

```python
import math

import jax
import jax.numpy as jnp
from jax import lax
from jax.experimental import pallas as pl
from jax.experimental.pallas import tpu as pltpu
from jax.sharding import PartitionSpec as P

HEAD = 128
CB = 128
HALVES = 2

masked_low = -1e30
f32 = jnp.float32
bf16 = jnp.bfloat16
QI, GI, KI, VI = 2, 3, 0, 1


def dot_nt(a, b):
    return lax.dot_general(a, b, (((1,), (1,)), ((), ())), preferred_element_type=f32)


def dot_nn(a, b):
    return lax.dot_general(a, b, (((1,), (0,)), ((), ())), preferred_element_type=f32)


def dot_tn(a, b):
    return lax.dot_general(a, b, (((0,), (0,)), ((), ())), preferred_element_type=f32)


def params(n_axes=1):
    return pltpu.CompilerParams(
        dimension_semantics=("arbitrary",) * n_axes, vmem_limit_bytes=48 * 1024 * 1024
    )


def cost(units):
    return pl.CostEstimate(
        flops=units * 10 * 512 * 512 * 128, bytes_accessed=4 << 20, transcendentals=units * 512 * 512
    )


def pack_body(k_ref, v_ref, q_ref, g_ref, out_ref):
    _, subs, _, cols, _ = out_ref.shape
    for a, ref in enumerate((k_ref, v_ref, q_ref, g_ref)):
        for s in range(subs):
            out_ref[0, s, a] = ref[s * cols : (s + 1) * cols, :]


def pack(k, v, q, g, groups, subs, cols):
    tokens, feats = k.shape
    wide_feats = feats // groups
    return pl.pallas_call(
        pack_body,
        grid=(groups,),
        in_specs=[pl.BlockSpec((tokens, wide_feats), lambda j: (0, j))] * 4,
        out_specs=pl.BlockSpec((1, subs, 4, cols, wide_feats), lambda j: (j, 0, 0, 0, 0)),
        out_shape=jax.ShapeDtypeStruct((groups, subs, 4, cols, wide_feats), bf16),
        compiler_params=params(),
        name="pack",
    )(k, v, q, g)


def unpack_body(in_ref, q_ref, k_ref, v_ref):
    _, subs, _, cols, _ = in_ref.shape
    for a, ref in enumerate((q_ref, k_ref, v_ref)):
        for s in range(subs):
            ref[s * cols : (s + 1) * cols, :] = in_ref[0, s, a]


def unpack(arr, tokens, feats):
    groups, subs, _, cols, wide_feats = arr.shape
    out = jax.ShapeDtypeStruct((tokens, feats), bf16)
    return pl.pallas_call(
        unpack_body,
        grid=(groups,),
        in_specs=[pl.BlockSpec((1, subs, 3, cols, wide_feats), lambda j: (j, 0, 0, 0, 0))],
        out_specs=[pl.BlockSpec((tokens, wide_feats), lambda j: (0, j))] * 3,
        out_shape=[out] * 3,
        compiler_params=params(),
        name="unpack",
    )(arr)


def flat(ref, index):
    block = ref[:, index]
    return block.reshape(block.shape[0] * block.shape[1], block.shape[2])


def row_masks(scal_ref, n):
    first = scal_ref[1] - scal_ref[0] * n
    u = lax.broadcasted_iota(jnp.int32, (n, n), 0)
    t = lax.broadcasted_iota(jnp.int32, (n, n), 1)
    return (u == t) | ((u < t) & (u >= first))


def off_mask(scal_ref, n):
    u = lax.broadcasted_iota(jnp.int32, (n, n), 0)
    return u >= scal_ref[1]


def col_mask(scal_ref, n, cols):
    u = lax.broadcasted_iota(jnp.int32, (n, n), 0)
    t = lax.broadcasted_iota(jnp.int32, (n, n), 1)
    same = (u & (cols - 1)) == (t & (cols - 1))
    return same & (u < t) & (u >= scal_ref[2] * cols)


def partial_stats(k, v, q, g, mask, scale):
    s = jnp.where(mask, dot_nt(k, q) * scale, masked_low)
    m = jnp.max(s, axis=0, keepdims=True)
    e = jnp.where(mask, jnp.exp(s - m), 0.0)
    total = jnp.sum(e, axis=0, keepdims=True)
    weighted = jnp.sum(e * dot_nt(v, g), axis=0, keepdims=True)
    some = total > 0.0
    total = jnp.where(some, total, 1.0)
    return jnp.where(some, m + jnp.log(total), masked_low), weighted / total


def merge(lse_a, delta_a, lse_b, delta_b):
    top = jnp.maximum(lse_a, lse_b)
    a = jnp.exp(lse_a - top)
    b = jnp.exp(lse_b - top)
    total = a + b
    return top + jnp.log(total), (a * delta_a + b * delta_b) / total


def row_stats_body(scale, scal_ref, t_ref, far_ref, out_ref):
    k, v, q, g = (flat(t_ref, i) for i in range(4))
    n = k.shape[0]
    lse, delta = partial_stats(k, v, q, g, row_masks(scal_ref, n), scale)
    out_ref[0, 0:1] = lse
    out_ref[0, 1:2] = delta

    @pl.when(scal_ref[0] == 1)
    def _():
        lse_f, delta_f = partial_stats(
            flat(far_ref, 0), flat(far_ref, 1), q, g, off_mask(scal_ref, n), scale
        )
        lse_m, delta_m = merge(lse, delta, lse_f, delta_f)
        out_ref[0, 0:1] = lse_m
        out_ref[0, 1:2] = delta_m


def col_stats_body(scale, scal_ref, t_ref, out_ref):
    k, v, q, g = (flat(t_ref, i) for i in range(4))
    n = k.shape[0]
    lse, delta = partial_stats(k, v, q, g, col_mask(scal_ref, n, t_ref.shape[2]), scale)
    out_ref[0, 0:1] = lse
    out_ref[0, 1:2] = delta


def smem():
    return pl.BlockSpec(memory_space=pltpu.SMEM)


def head_block(arr):
    a, b, c, _ = arr.shape
    return pl.BlockSpec((a, b, c, HEAD), lambda h: (0, 0, 0, h))


def stats_call(body, scale, scal, arrays, name, units):
    heads = arrays[0].shape[3] // HEAD
    n = arrays[0].shape[0] * arrays[0].shape[2]
    return pl.pallas_call(
        lambda *refs: body(scale, *refs),
        grid=(heads,),
        in_specs=[smem()] + [head_block(a) for a in arrays],
        out_specs=pl.BlockSpec((1, 2, n), lambda h: (h, 0, 0)),
        out_shape=jax.ShapeDtypeStruct((heads, 2, n), f32),
        compiler_params=params(),
        cost_estimate=cost(units),
        name=name,
    )(scal, *arrays)


def block_grads(k, v, q, g, mask, lse, delta, scale):
    p = jnp.where(mask, jnp.exp(dot_nt(k, q) * scale - lse), 0.0)
    ds = (p * (dot_nt(v, g) - delta)).astype(bf16)
    dv = dot_nn(p.astype(bf16), g)
    dk = dot_nn(ds, q) * scale
    dq = dot_tn(ds, k) * scale
    return dq, dk, dv


def row_grads_body(scale, scal_ref, t_ref, far_ref, stat_ref, out_ref, back_ref):
    k, v, q, g = (flat(t_ref, i) for i in range(4))
    n = k.shape[0]
    lse, delta = stat_ref[0, 0:1], stat_ref[0, 1:2]
    dq, dk, dv = block_grads(k, v, q, g, row_masks(scal_ref, n), lse, delta, scale)
    out_ref[0] = dq
    out_ref[1] = dk
    out_ref[2] = dv

    @pl.when(scal_ref[0] == 1)
    def _():
        dq_f, dk_f, dv_f = block_grads(
            flat(far_ref, 0), flat(far_ref, 1), q, g, off_mask(scal_ref, n), lse, delta, scale
        )
        out_ref[0] += dq_f
        back_ref[0] = dk_f.astype(bf16)
        back_ref[1] = dv_f.astype(bf16)


def col_grads_body(scale, scal_ref, t_ref, stat_ref, out_ref):
    k, v, q, g = (flat(t_ref, i) for i in range(4))
    n = k.shape[0]
    lse, delta = stat_ref[0, 0:1], stat_ref[0, 1:2]
    grads = block_grads(k, v, q, g, col_mask(scal_ref, n, t_ref.shape[2]), lse, delta, scale)
    for a, d in enumerate(grads):
        out_ref[:, a] = d.astype(bf16).reshape(out_ref.shape[0], out_ref.shape[2], HEAD)


def row_grads(scale, scal, t, far, stats):
    rows, _, cols, feats = t.shape
    n = rows * cols
    return pl.pallas_call(
        lambda *refs: row_grads_body(scale, *refs),
        grid=(feats // HEAD,),
        in_specs=[smem(), head_block(t), head_block(far), pl.BlockSpec((1, 2, n), lambda h: (h, 0, 0))],
        out_specs=[
            pl.BlockSpec((3, n, HEAD), lambda h: (0, 0, h)),
            pl.BlockSpec((2, n, HEAD), lambda h: (0, 0, h)),
        ],
        out_shape=[
            jax.ShapeDtypeStruct((3, n, feats), f32),
            jax.ShapeDtypeStruct((2, n, feats), bf16),
        ],
        compiler_params=params(),
        cost_estimate=cost(16),
        name="row_grads",
    )(scal, t, far, stats)


def col_grads(scale, scal, t, stats):
    rows, _, cols, feats = t.shape
    n = rows * cols
    return pl.pallas_call(
        lambda *refs: col_grads_body(scale, *refs),
        grid=(feats // HEAD,),
        in_specs=[smem(), head_block(t), pl.BlockSpec((1, 2, n), lambda h: (h, 0, 0))],
        out_specs=pl.BlockSpec((rows, 3, cols, HEAD), lambda h: (0, 0, 0, h)),
        out_shape=jax.ShapeDtypeStruct((rows, 3, cols, feats), bf16),
        compiler_params=params(),
        cost_estimate=cost(8),
        name="col_grads",
    )(scal, t, stats)


def join_body(row_ref, col_ref, far_ref, out_ref):
    for a in range(3):
        total = row_ref[a] + col_ref[:, a].astype(f32).reshape(row_ref.shape[1:])
        if a > 0:
            total = total + far_ref[a - 1].astype(f32)
        out_ref[:, a] = total.astype(bf16).reshape(out_ref.shape[0], *out_ref.shape[2:])


def join(row, col, far):
    rows, _, cols, feats = col.shape
    steps = 4
    part = rows // steps
    n = part * cols
    return pl.pallas_call(
        join_body,
        grid=(steps,),
        in_specs=[
            pl.BlockSpec((3, n, feats), lambda i: (0, i, 0)),
            pl.BlockSpec((part, 3, cols, feats), lambda i: (i, 0, 0, 0)),
            pl.BlockSpec((2, n, feats), lambda i: (0, i, 0)),
        ],
        out_specs=pl.BlockSpec((part, 3, cols, feats), lambda i: (i, 0, 0, 0)),
        out_shape=jax.ShapeDtypeStruct(col.shape, bf16),
        compiler_params=params(),
        name="join",
    )(row, col, far)


def body(query_in, key_in, value_in, grad_out, row_start, col_start):
    scale = 1.0 / math.sqrt(HEAD)
    tokens, feats = query_in.shape
    lanes = lax.axis_size("wide")
    narrow = lax.axis_size("narrow")
    groups = narrow // HALVES
    half_cols = tokens * groups
    cols = half_cols // lanes
    subs = tokens // cols
    near = [[half * groups + j for j in range(groups)] for half in range(HALVES)]

    def exchange_near(arr):
        return lax.all_to_all(
            arr, "narrow", split_axis=0, concat_axis=0, axis_index_groups=near, tiled=True
        )

    def exchange_wide(arr):
        return lax.all_to_all(arr, "wide", split_axis=0, concat_axis=0, tiled=True)

    wide_index = lax.axis_index("wide")
    half = lax.axis_index("narrow") // groups
    first_col = lax.dynamic_index_in_dim(row_start, wide_index, keepdims=False)
    block_id = (half * half_cols + wide_index * cols) // CB
    first_row = lax.dynamic_index_in_dim(col_start, block_id, keepdims=False)
    scal = jnp.stack([half, first_col, first_row]).astype(jnp.int32)

    packed = pack(key_in, value_in, query_in, grad_out, groups, subs, cols)
    near_feats = feats // groups
    t = exchange_near(packed).reshape(lanes, 4, cols, near_feats)
    far = lax.ppermute(t[:, :2], "narrow", [(j, j + groups) for j in range(groups)])
    by_col = exchange_wide(t)
    heads = near_feats // HEAD
    row_part = stats_call(row_stats_body, scale, scal, (t, far), "row_stats", 6)
    col_part = stats_call(col_stats_body, scale, scal, (by_col,), "col_stats", 4)

    both = jnp.stack([row_part, col_part]).reshape(4 * heads, lanes, cols)
    sent = both.transpose(1, 0, 2).reshape(lanes, (4 * heads * cols) // HEAD, HEAD)
    got = exchange_wide(sent).reshape(lanes, 4 * heads, cols).transpose(1, 0, 2)
    got = got.reshape(2, heads, 2, lanes * cols)
    row_lse, row_delta = merge(row_part[:, 0], row_part[:, 1], got[1, :, 0], got[1, :, 1])
    col_lse, col_delta = merge(col_part[:, 0], col_part[:, 1], got[0, :, 0], got[0, :, 1])
    row_full = jnp.stack([row_lse, row_delta], axis=1)
    col_full = jnp.stack([col_lse, col_delta], axis=1)

    from_col = exchange_wide(col_grads(scale, scal, by_col, col_full))
    row_terms, far_terms = row_grads(scale, scal, t, far, row_full)
    far_back = lax.ppermute(far_terms, "narrow", [(j + groups, j) for j in range(groups)])
    joined = join(row_terms, from_col, far_back)
    out = exchange_near(joined.reshape(groups, subs, 3, cols, near_feats))
    return unpack(out, tokens, feats)


def solution(mesh):
    placed = P(("wide", "narrow"), None)
    return jax.shard_map(
        body,
        mesh=mesh,
        in_specs=(placed,) * 4 + (P(), P()),
        out_specs=(placed,) * 3,
        check_vma=False,
    )
```

```python
import math

import jax
import jax.numpy as jnp
from jax import lax
from jax.experimental import pallas as pl
from jax.experimental.pallas import tpu as pltpu
from jax.sharding import PartitionSpec as P

HEAD = 128
CB = 128
HALVES = 2

masked_low = -1e30
f32 = jnp.float32
bf16 = jnp.bfloat16
QI, GI, KI, VI = 2, 3, 0, 1


def dot_nt(a, b):
    return lax.dot_general(a, b, (((1,), (1,)), ((), ())), preferred_element_type=f32)


def dot_nn(a, b):
    return lax.dot_general(a, b, (((1,), (0,)), ((), ())), preferred_element_type=f32)


def dot_tn(a, b):
    return lax.dot_general(a, b, (((0,), (0,)), ((), ())), preferred_element_type=f32)


def params(n_axes=1):
    return pltpu.CompilerParams(
        dimension_semantics=("arbitrary",) * n_axes, vmem_limit_bytes=48 * 1024 * 1024
    )


def cost(units):
    return pl.CostEstimate(
        flops=units * 10 * 512 * 512 * 128, bytes_accessed=4 << 20, transcendentals=units * 512 * 512
    )


def pack_body(k_ref, v_ref, q_ref, g_ref, out_ref, qg_ref):
    _, subs, _, cols, _ = out_ref.shape
    for a, ref in enumerate((k_ref, v_ref, q_ref, g_ref)):
        for s in range(subs):
            out_ref[0, s, a] = ref[s * cols : (s + 1) * cols, :]
            if a >= QI:
                qg_ref[0, s, a - QI] = ref[s * cols : (s + 1) * cols, :]


def pack(k, v, q, g, groups, subs, cols):
    tokens, feats = k.shape
    wide_feats = feats // groups
    return pl.pallas_call(
        pack_body,
        grid=(groups,),
        in_specs=[pl.BlockSpec((tokens, wide_feats), lambda j: (0, j))] * 4,
        out_specs=[
            pl.BlockSpec((1, subs, n, cols, wide_feats), lambda j: (j, 0, 0, 0, 0)) for n in (4, 2)
        ],
        out_shape=[
            jax.ShapeDtypeStruct((groups, subs, n, cols, wide_feats), bf16) for n in (4, 2)
        ],
        compiler_params=params(),
        name="pack",
    )(k, v, q, g)


def unpack_body(in_ref, q_ref, k_ref, v_ref):
    _, subs, _, cols, _ = in_ref.shape
    for a, ref in enumerate((q_ref, k_ref, v_ref)):
        for s in range(subs):
            ref[s * cols : (s + 1) * cols, :] = in_ref[0, s, a]


def unpack(arr, tokens, feats):
    groups, subs, _, cols, wide_feats = arr.shape
    out = jax.ShapeDtypeStruct((tokens, feats), bf16)
    return pl.pallas_call(
        unpack_body,
        grid=(groups,),
        in_specs=[pl.BlockSpec((1, subs, 3, cols, wide_feats), lambda j: (j, 0, 0, 0, 0))],
        out_specs=[pl.BlockSpec((tokens, wide_feats), lambda j: (0, j))] * 3,
        out_shape=[out] * 3,
        compiler_params=params(),
        name="unpack",
    )(arr)


def flat(ref, index):
    block = ref[:, index]
    return block.reshape(block.shape[0] * block.shape[1], block.shape[2])


def row_masks(scal_ref, n):
    first = scal_ref[1] - scal_ref[0] * n
    u = lax.broadcasted_iota(jnp.int32, (n, n), 0)
    t = lax.broadcasted_iota(jnp.int32, (n, n), 1)
    return (u == t) | ((u < t) & (u >= first))


def off_mask(scal_ref, n):
    u = lax.broadcasted_iota(jnp.int32, (n, n), 0)
    return u >= scal_ref[1]


def col_mask(scal_ref, n, cols):
    u = lax.broadcasted_iota(jnp.int32, (n, n), 0)
    t = lax.broadcasted_iota(jnp.int32, (n, n), 1)
    same = (u & (cols - 1)) == (t & (cols - 1))
    return same & (u < t) & (u >= scal_ref[2] * cols)


def partial_stats(k, v, q, g, mask, scale):
    s = jnp.where(mask, dot_nt(k, q) * scale, masked_low)
    m = jnp.max(s, axis=0, keepdims=True)
    e = jnp.where(mask, jnp.exp(s - m), 0.0)
    total = jnp.sum(e, axis=0, keepdims=True)
    weighted = jnp.sum(e * dot_nt(v, g), axis=0, keepdims=True)
    some = total > 0.0
    total = jnp.where(some, total, 1.0)
    return jnp.where(some, m + jnp.log(total), masked_low), weighted / total


def merge(lse_a, delta_a, lse_b, delta_b):
    top = jnp.maximum(lse_a, lse_b)
    a = jnp.exp(lse_a - top)
    b = jnp.exp(lse_b - top)
    total = a + b
    return top + jnp.log(total), (a * delta_a + b * delta_b) / total


def row_stats_body(scale, scal_ref, t_ref, out_ref):
    k, v, q, g = (flat(t_ref, i) for i in range(4))
    lse, delta = partial_stats(k, v, q, g, row_masks(scal_ref, k.shape[0]), scale)
    out_ref[0, 0:1] = lse
    out_ref[0, 1:2] = delta


def gather_far(scal_ref, piece_refs, q_buf, g_buf):
    for i, ref in enumerate(piece_refs):
        place = scal_ref[3] ^ i
        q_buf[place] = flat(ref, 0)
        g_buf[place] = flat(ref, 1)
    return (b[...].reshape(b.shape[0] * b.shape[1], HEAD) for b in (q_buf, g_buf))


def off_stats_body(scale, scal_ref, t_ref, *refs):
    *piece_refs, out_ref, q_buf, g_buf = refs

    @pl.when(scal_ref[0] == 0)
    def _():
        q, g = gather_far(scal_ref, piece_refs, q_buf, g_buf)
        k, v = flat(t_ref, KI), flat(t_ref, VI)
        lse, delta = partial_stats(k, v, q, g, off_mask(scal_ref, k.shape[0]), scale)
        out_ref[0, 0:1] = lse
        out_ref[0, 1:2] = delta

    @pl.when(scal_ref[0] != 0)
    def _():
        out_ref[...] = jnp.zeros_like(out_ref)


def col_stats_body(scale, scal_ref, t_ref, out_ref):
    k, v, q, g = (flat(t_ref, i) for i in range(4))
    n = k.shape[0]
    lse, delta = partial_stats(k, v, q, g, col_mask(scal_ref, n, t_ref.shape[2]), scale)
    out_ref[0, 0:1] = lse
    out_ref[0, 1:2] = delta


def smem():
    return pl.BlockSpec(memory_space=pltpu.SMEM)


def head_block(arr):
    a, b, c, _ = arr.shape
    return pl.BlockSpec((a, b, c, HEAD), lambda h: (0, 0, 0, h))


def far_scratch(pieces):
    _, _, cols, _ = pieces[0].shape
    tokens = pieces[0].shape[0] * cols
    return [pltpu.VMEM((len(pieces), tokens, HEAD), bf16)] * 2


def stats_call(body, scale, scal, arrays, name, units, scratch=()):
    heads = arrays[0].shape[3] // HEAD
    n = arrays[0].shape[0] * arrays[0].shape[2]
    return pl.pallas_call(
        lambda *refs: body(scale, *refs),
        grid=(heads,),
        in_specs=[smem()] + [head_block(a) for a in arrays],
        out_specs=pl.BlockSpec((1, 2, n), lambda h: (h, 0, 0)),
        out_shape=jax.ShapeDtypeStruct((heads, 2, n), f32),
        scratch_shapes=list(scratch),
        compiler_params=params(),
        cost_estimate=cost(units),
        name=name,
    )(scal, *arrays)


def block_grads(k, v, q, g, mask, lse, delta, scale):
    p = jnp.where(mask, jnp.exp(dot_nt(k, q) * scale - lse), 0.0)
    ds = (p * (dot_nt(v, g) - delta)).astype(bf16)
    dv = dot_nn(p.astype(bf16), g)
    dk = dot_nn(ds, q) * scale
    dq = dot_tn(ds, k) * scale
    return dq, dk, dv


def row_grads_body(scale, scal_ref, t_ref, stat_ref, far_stat_ref, *refs):
    *piece_refs, out_ref, back_ref, q_buf, g_buf = refs
    k, v, q, g = (flat(t_ref, i) for i in range(4))
    n = k.shape[0]
    dq, dk, dv = block_grads(
        k, v, q, g, row_masks(scal_ref, n), stat_ref[0, 0:1], stat_ref[0, 1:2], scale
    )
    out_ref[0] = dq
    out_ref[1] = dk
    out_ref[2] = dv

    @pl.when(scal_ref[0] == 0)
    def _():
        q_f, g_f = gather_far(scal_ref, piece_refs, q_buf, g_buf)
        dq_f, dk_f, dv_f = block_grads(
            k, v, q_f, g_f, off_mask(scal_ref, n), far_stat_ref[0, 0:1], far_stat_ref[0, 1:2], scale
        )
        out_ref[1] += dk_f
        out_ref[2] += dv_f
        back_ref[...] = dq_f.astype(bf16)


def col_grads_body(scale, scal_ref, t_ref, stat_ref, out_ref):
    k, v, q, g = (flat(t_ref, i) for i in range(4))
    n = k.shape[0]
    lse, delta = stat_ref[0, 0:1], stat_ref[0, 1:2]
    grads = block_grads(k, v, q, g, col_mask(scal_ref, n, t_ref.shape[2]), lse, delta, scale)
    for a, d in enumerate(grads):
        out_ref[:, a] = d.astype(bf16).reshape(out_ref.shape[0], out_ref.shape[2], HEAD)


def row_grads(scale, scal, t, stats, far_stats, pieces):
    rows, _, cols, feats = t.shape
    n = rows * cols
    stat_spec = pl.BlockSpec((1, 2, n), lambda h: (h, 0, 0))
    return pl.pallas_call(
        lambda *refs: row_grads_body(scale, *refs),
        grid=(feats // HEAD,),
        in_specs=[smem(), head_block(t), stat_spec, stat_spec] + [head_block(p) for p in pieces],
        out_specs=[
            pl.BlockSpec((3, n, HEAD), lambda h: (0, 0, h)),
            pl.BlockSpec((n, HEAD), lambda h: (0, h)),
        ],
        out_shape=[
            jax.ShapeDtypeStruct((3, n, feats), f32),
            jax.ShapeDtypeStruct((n, feats), bf16),
        ],
        scratch_shapes=far_scratch(pieces),
        compiler_params=params(),
        cost_estimate=cost(16),
        name="row_grads",
    )(scal, t, stats, far_stats, *pieces)


def col_grads(scale, scal, t, stats):
    rows, _, cols, feats = t.shape
    n = rows * cols
    return pl.pallas_call(
        lambda *refs: col_grads_body(scale, *refs),
        grid=(feats // HEAD,),
        in_specs=[smem(), head_block(t), pl.BlockSpec((1, 2, n), lambda h: (h, 0, 0))],
        out_specs=pl.BlockSpec((rows, 3, cols, HEAD), lambda h: (0, 0, 0, h)),
        out_shape=jax.ShapeDtypeStruct((rows, 3, cols, feats), bf16),
        compiler_params=params(),
        cost_estimate=cost(8),
        name="col_grads",
    )(scal, t, stats)


def join_body(row_ref, col_ref, far_ref, out_ref):
    for a in range(3):
        total = row_ref[a] + col_ref[:, a].astype(f32).reshape(row_ref.shape[1:])
        if a == 0:
            total = total + far_ref[...].astype(f32)
        out_ref[:, a] = total.astype(bf16).reshape(out_ref.shape[0], *out_ref.shape[2:])


def join(row, col, far):
    rows, _, cols, feats = col.shape
    steps = 4
    part = rows // steps
    n = part * cols
    return pl.pallas_call(
        join_body,
        grid=(steps,),
        in_specs=[
            pl.BlockSpec((3, n, feats), lambda i: (0, i, 0)),
            pl.BlockSpec((part, 3, cols, feats), lambda i: (i, 0, 0, 0)),
            pl.BlockSpec((n, feats), lambda i: (i, 0)),
        ],
        out_specs=pl.BlockSpec((part, 3, cols, feats), lambda i: (i, 0, 0, 0)),
        out_shape=jax.ShapeDtypeStruct(col.shape, bf16),
        compiler_params=params(),
        name="join",
    )(row, col, far)


def body(query_in, key_in, value_in, grad_out, row_start, col_start):
    scale = 1.0 / math.sqrt(HEAD)
    tokens, feats = query_in.shape
    lanes = lax.axis_size("wide")
    narrow = lax.axis_size("narrow")
    groups = narrow // HALVES
    half_cols = tokens * groups
    cols = half_cols // lanes
    subs = tokens // cols
    near = [[half * groups + j for j in range(groups)] for half in range(HALVES)]

    def exchange_near(arr):
        return lax.all_to_all(
            arr, "narrow", split_axis=0, concat_axis=0, axis_index_groups=near, tiled=True
        )

    def exchange_wide(arr):
        return lax.all_to_all(arr, "wide", split_axis=0, concat_axis=0, tiled=True)

    def shift(arr, source, target):
        pairs = [(source * groups + j, target * groups + j) for j in range(groups)]
        return lax.ppermute(arr, "narrow", pairs)

    def swap(arr, step):
        pairs = [(i, i ^ step) for i in range(narrow)]
        return lax.ppermute(arr, "narrow", pairs)

    wide_index = lax.axis_index("wide")
    narrow_index = lax.axis_index("narrow")
    half = narrow_index // groups
    near_index = narrow_index % groups
    first_col = lax.dynamic_index_in_dim(row_start, wide_index, keepdims=False)
    block_id = (half * half_cols + wide_index * cols) // CB
    first_row = lax.dynamic_index_in_dim(col_start, block_id, keepdims=False)
    scal = jnp.stack([half, first_col, first_row, near_index]).astype(jnp.int32)

    packed, packed_qg = pack(key_in, value_in, query_in, grad_out, groups, subs, cols)
    near_feats = feats // groups
    far = shift(packed_qg, 1, 0)
    t = exchange_near(packed).reshape(lanes, 4, cols, near_feats)
    by_col = exchange_wide(t)
    pieces = []
    for step in range(groups):
        piece = lax.dynamic_index_in_dim(far, near_index ^ step, keepdims=False)
        pieces.append(swap(piece, step) if step else piece)
    heads = near_feats // HEAD
    diag_part = stats_call(row_stats_body, scale, scal, (t,), "row_stats", 4)
    off_part = stats_call(
        off_stats_body, scale, scal, (t, *pieces), "off_stats", 4, far_scratch(pieces)
    )
    off_part = shift(off_part, 0, 1)
    lse, delta = merge(diag_part[:, 0], diag_part[:, 1], off_part[:, 0], off_part[:, 1])
    row_part = jnp.where(half == 1, jnp.stack([lse, delta], axis=1), diag_part)
    col_part = stats_call(col_stats_body, scale, scal, (by_col,), "col_stats", 4)

    both = jnp.stack([row_part, col_part]).reshape(4 * heads, lanes, cols)
    sent = both.transpose(1, 0, 2).reshape(lanes, (4 * heads * cols) // HEAD, HEAD)
    got = exchange_wide(sent).reshape(lanes, 4 * heads, cols).transpose(1, 0, 2)
    got = got.reshape(2, heads, 2, lanes * cols)
    row_lse, row_delta = merge(row_part[:, 0], row_part[:, 1], got[1, :, 0], got[1, :, 1])
    col_lse, col_delta = merge(col_part[:, 0], col_part[:, 1], got[0, :, 0], got[0, :, 1])
    row_full = jnp.stack([row_lse, row_delta], axis=1)
    col_full = jnp.stack([col_lse, col_delta], axis=1)

    from_col = exchange_wide(col_grads(scale, scal, by_col, col_full))
    far_full = shift(row_full, 1, 0)
    row_terms, far_terms = row_grads(scale, scal, t, row_full, far_full, pieces)
    far_back = shift(far_terms, 0, 1)
    joined = join(row_terms, from_col, far_back)
    out = exchange_near(joined.reshape(groups, subs, 3, cols, near_feats))
    return unpack(out, tokens, feats)


def solution(mesh):
    placed = P(("wide", "narrow"), None)
    return jax.shard_map(
        body,
        mesh=mesh,
        in_specs=(placed,) * 4 + (P(), P()),
        out_specs=(placed,) * 3,
        check_vma=False,
    )
```

```python
import math

import jax
import jax.numpy as jnp
from jax import lax
from jax.experimental import pallas as pl
from jax.experimental.pallas import tpu as pltpu
from jax.sharding import PartitionSpec as P

HEAD = 128
CB = 128
HALVES = 2

masked_low = -1e30
f32 = jnp.float32
bf16 = jnp.bfloat16
QI, GI, KI, VI = 2, 3, 0, 1


def dot_nt(a, b):
    return lax.dot_general(a, b, (((1,), (1,)), ((), ())), preferred_element_type=f32)


def dot_nn(a, b):
    return lax.dot_general(a, b, (((1,), (0,)), ((), ())), preferred_element_type=f32)


def dot_tn(a, b):
    return lax.dot_general(a, b, (((0,), (0,)), ((), ())), preferred_element_type=f32)


def params(n_axes=1):
    return pltpu.CompilerParams(
        dimension_semantics=("arbitrary",) * n_axes, vmem_limit_bytes=48 * 1024 * 1024
    )


def cost(units):
    return pl.CostEstimate(
        flops=units * 10 * 512 * 512 * 128, bytes_accessed=4 << 20, transcendentals=units * 512 * 512
    )


def pack_body(scal_ref, k_ref, v_ref, q_ref, g_ref, out_ref, far_ref):
    _, subs, _, cols, _ = out_ref.shape
    far_feats = far_ref.shape[-1]
    for a, ref in enumerate((k_ref, v_ref, q_ref, g_ref)):
        for s in range(subs):
            out_ref[0, s, a] = ref[s * cols : (s + 1) * cols, :]

    def fill(pair, feats):
        for a, ref in enumerate(pair):
            for s in range(subs):
                far_ref[0, s, a] = ref[s * cols : (s + 1) * cols, feats]

    @pl.when(scal_ref[0] == 0)
    def _():
        fill((k_ref, v_ref), slice(far_feats, 2 * far_feats))

    @pl.when(scal_ref[0] != 0)
    def _():
        fill((q_ref, g_ref), slice(0, far_feats))


def pack(scal, k, v, q, g, groups, subs, cols):
    tokens, feats = k.shape
    near_feats = feats // groups
    shapes = [(subs, 4, cols, near_feats), (subs, 2, cols, near_feats // HALVES)]
    return pl.pallas_call(
        pack_body,
        grid=(groups,),
        in_specs=[smem()] + [pl.BlockSpec((tokens, near_feats), lambda j: (0, j))] * 4,
        out_specs=[pl.BlockSpec((1, *shape), lambda j: (j, 0, 0, 0, 0)) for shape in shapes],
        out_shape=[jax.ShapeDtypeStruct((groups, *shape), bf16) for shape in shapes],
        compiler_params=params(),
        name="pack",
    )(scal, k, v, q, g)


def unpack_body(scal_ref, in_ref, far_ref, q_ref, k_ref, v_ref):
    _, subs, _, cols, _ = in_ref.shape
    far_feats = far_ref.shape[-1]
    for a, ref in enumerate((q_ref, k_ref, v_ref)):
        for s in range(subs):
            ref[s * cols : (s + 1) * cols, :] = in_ref[0, s, a]

    def add(ref, terms, feats):
        ref[:, feats] = (ref[:, feats].astype(f32) + terms.astype(f32)).astype(bf16)

    @pl.when(scal_ref[0] == 0)
    def _():
        upper = slice(far_feats, 2 * far_feats)
        add(k_ref, far_ref[0, 0], upper)
        add(v_ref, far_ref[0, 1], upper)

    @pl.when(scal_ref[0] != 0)
    def _():
        add(q_ref, far_ref[0, 0], slice(0, far_feats))


def unpack(scal, arr, far, tokens, feats):
    groups, subs, _, cols, near_feats = arr.shape
    out = jax.ShapeDtypeStruct((tokens, feats), bf16)
    far_spec = pl.BlockSpec((1, *far.shape[1:]), lambda j, scal_ref: (j ^ scal_ref[3], 0, 0, 0))
    return pl.pallas_call(
        unpack_body,
        grid_spec=pltpu.PrefetchScalarGridSpec(
            num_scalar_prefetch=1,
            grid=(groups,),
            in_specs=[
                pl.BlockSpec((1, subs, 3, cols, near_feats), lambda j, scal_ref: (j, 0, 0, 0, 0)),
                far_spec,
            ],
            out_specs=[pl.BlockSpec((tokens, near_feats), lambda j, scal_ref: (0, j))] * 3,
        ),
        out_shape=[out] * 3,
        compiler_params=params(),
        name="unpack",
    )(scal, arr, far)


def flat(ref, index):
    block = ref[:, index]
    return block.reshape(block.shape[0] * block.shape[1], block.shape[2])


def row_masks(scal_ref, n):
    first = scal_ref[1] - scal_ref[0] * n
    u = lax.broadcasted_iota(jnp.int32, (n, n), 0)
    t = lax.broadcasted_iota(jnp.int32, (n, n), 1)
    return (u == t) | ((u < t) & (u >= first))


def off_mask(scal_ref, n):
    u = lax.broadcasted_iota(jnp.int32, (n, n), 0)
    return u >= scal_ref[1]


def col_mask(scal_ref, n, cols):
    u = lax.broadcasted_iota(jnp.int32, (n, n), 0)
    t = lax.broadcasted_iota(jnp.int32, (n, n), 1)
    same = (u & (cols - 1)) == (t & (cols - 1))
    return same & (u < t) & (u >= scal_ref[2] * cols)


def partial_stats(k, v, q, g, mask, scale):
    s = jnp.where(mask, dot_nt(k, q) * scale, masked_low)
    m = jnp.max(s, axis=0, keepdims=True)
    e = jnp.where(mask, jnp.exp(s - m), 0.0)
    total = jnp.sum(e, axis=0, keepdims=True)
    weighted = jnp.sum(e * dot_nt(v, g), axis=0, keepdims=True)
    some = total > 0.0
    total = jnp.where(some, total, 1.0)
    return jnp.where(some, m + jnp.log(total), masked_low), weighted / total


def merge(lse_a, delta_a, lse_b, delta_b):
    top = jnp.maximum(lse_a, lse_b)
    a = jnp.exp(lse_a - top)
    b = jnp.exp(lse_b - top)
    total = a + b
    return top + jnp.log(total), (a * delta_a + b * delta_b) / total


def row_stats_body(scale, scal_ref, t_ref, out_ref):
    k, v, q, g = (flat(t_ref, i) for i in range(4))
    lse, delta = partial_stats(k, v, q, g, row_masks(scal_ref, k.shape[0]), scale)
    out_ref[0, 0:1] = lse
    out_ref[0, 1:2] = delta


def gather_far(scal_ref, piece_refs, buf):
    for i, ref in enumerate(piece_refs):
        for a in range(2):
            buf[a, scal_ref[3] ^ i] = flat(ref, a)
    return (buf[a].reshape(buf.shape[1] * buf.shape[2], HEAD) for a in range(2))


def off_stats_body(scale, scal_ref, t_ref, *refs):
    *piece_refs, out_ref, buf = refs
    far_a, far_b = gather_far(scal_ref, piece_refs, buf)

    def run(k, v, q, g):
        lse, delta = partial_stats(k, v, q, g, off_mask(scal_ref, k.shape[0]), scale)
        out_ref[0, 0:1] = lse
        out_ref[0, 1:2] = delta

    @pl.when(scal_ref[0] == 0)
    def _():
        run(flat(t_ref, KI), flat(t_ref, VI), far_a, far_b)

    @pl.when(scal_ref[0] != 0)
    def _():
        run(far_a, far_b, flat(t_ref, QI), flat(t_ref, GI))


def col_stats_body(scale, scal_ref, t_ref, out_ref):
    k, v, q, g = (flat(t_ref, i) for i in range(4))
    n = k.shape[0]
    lse, delta = partial_stats(k, v, q, g, col_mask(scal_ref, n, t_ref.shape[2]), scale)
    out_ref[0, 0:1] = lse
    out_ref[0, 1:2] = delta


def smem():
    return pl.BlockSpec(memory_space=pltpu.SMEM)


def head_block(arr):
    a, b, c, _ = arr.shape
    return pl.BlockSpec((a, b, c, HEAD), lambda h: (0, 0, 0, h))


def off_block(arr, heads):
    a, b, c, _ = arr.shape
    return pl.BlockSpec((a, b, c, HEAD), lambda h, scal_ref: (0, 0, 0, h + scal_ref[0] * heads))


def off_call(body, scale, scal, t, extra, pieces, out_specs, out_shape, units, name):
    heads = pieces[0].shape[3] // HEAD
    tokens = pieces[0].shape[0] * pieces[0].shape[2]
    rows, _, cols, _ = t.shape
    stat_spec = pl.BlockSpec((1, 2, rows * cols), lambda h, scal_ref: (h, 0, 0))
    piece_specs = [
        pl.BlockSpec((*p.shape[:3], HEAD), lambda h, scal_ref: (0, 0, 0, h)) for p in pieces
    ]
    return pl.pallas_call(
        lambda *refs: body(scale, *refs),
        grid_spec=pltpu.PrefetchScalarGridSpec(
            num_scalar_prefetch=1,
            grid=(heads,),
            in_specs=[off_block(t, heads)] + [stat_spec] * len(extra) + piece_specs,
            out_specs=out_specs,
            scratch_shapes=[pltpu.VMEM((2, len(pieces), tokens, HEAD), bf16)],
        ),
        out_shape=out_shape,
        compiler_params=params(),
        cost_estimate=cost(units),
        name=name,
    )(scal, t, *extra, *pieces)


def off_stats(scale, scal, t, pieces):
    heads = pieces[0].shape[3] // HEAD
    n = t.shape[0] * t.shape[2]
    return off_call(
        off_stats_body, scale, scal, t, (), pieces,
        pl.BlockSpec((1, 2, n), lambda h, scal_ref: (h, 0, 0)),
        jax.ShapeDtypeStruct((heads, 2, n), f32), 2, "off_stats",
    )


def off_grads_body(scale, scal_ref, t_ref, stat_ref, *refs):
    *piece_refs, near_ref, far_ref, buf = refs
    far_a, far_b = gather_far(scal_ref, piece_refs, buf)
    lse, delta = stat_ref[0, 0:1], stat_ref[0, 1:2]

    def run(k, v, q, g):
        return block_grads(k, v, q, g, off_mask(scal_ref, k.shape[0]), lse, delta, scale)

    @pl.when(scal_ref[0] == 0)
    def _():
        dq, dk, dv = run(flat(t_ref, KI), flat(t_ref, VI), far_a, far_b)
        near_ref[0] = dk
        near_ref[1] = dv
        far_ref[:, 0] = dq.astype(bf16).reshape(far_ref.shape[0], far_ref.shape[2], HEAD)

    @pl.when(scal_ref[0] != 0)
    def _():
        dq, dk, dv = run(far_a, far_b, flat(t_ref, QI), flat(t_ref, GI))
        near_ref[0] = dq
        for a, d in enumerate((dk, dv)):
            far_ref[:, a] = d.astype(bf16).reshape(far_ref.shape[0], far_ref.shape[2], HEAD)


def off_grads(scale, scal, t, stats, pieces):
    n = t.shape[0] * t.shape[2]
    feats = pieces[0].shape[3]
    far_shape = (len(pieces), 2, n // len(pieces), feats)
    return off_call(
        off_grads_body, scale, scal, t, (stats,), pieces,
        [
            pl.BlockSpec((2, n, HEAD), lambda h, scal_ref: (0, 0, h)),
            pl.BlockSpec((*far_shape[:3], HEAD), lambda h, scal_ref: (0, 0, 0, h)),
        ],
        [jax.ShapeDtypeStruct((2, n, feats), f32), jax.ShapeDtypeStruct(far_shape, bf16)],
        5,
        "off_grads",
    )


def stats_call(body, scale, scal, arrays, name, units):
    heads = arrays[0].shape[3] // HEAD
    n = arrays[0].shape[0] * arrays[0].shape[2]
    return pl.pallas_call(
        lambda *refs: body(scale, *refs),
        grid=(heads,),
        in_specs=[smem()] + [head_block(a) for a in arrays],
        out_specs=pl.BlockSpec((1, 2, n), lambda h: (h, 0, 0)),
        out_shape=jax.ShapeDtypeStruct((heads, 2, n), f32),
        compiler_params=params(),
        cost_estimate=cost(units),
        name=name,
    )(scal, *arrays)


def block_grads(k, v, q, g, mask, lse, delta, scale):
    p = jnp.where(mask, jnp.exp(dot_nt(k, q) * scale - lse), 0.0)
    ds = (p * (dot_nt(v, g) - delta)).astype(bf16)
    dv = dot_nn(p.astype(bf16), g)
    dk = dot_nn(ds, q) * scale
    dq = dot_tn(ds, k) * scale
    return dq, dk, dv


def row_grads_body(scale, scal_ref, t_ref, stat_ref, out_ref):
    k, v, q, g = (flat(t_ref, i) for i in range(4))
    mask = row_masks(scal_ref, k.shape[0])
    grads = block_grads(k, v, q, g, mask, stat_ref[0, 0:1], stat_ref[0, 1:2], scale)
    for a, d in enumerate(grads):
        out_ref[a] = d


def col_grads_body(scale, scal_ref, t_ref, stat_ref, out_ref):
    k, v, q, g = (flat(t_ref, i) for i in range(4))
    n = k.shape[0]
    lse, delta = stat_ref[0, 0:1], stat_ref[0, 1:2]
    grads = block_grads(k, v, q, g, col_mask(scal_ref, n, t_ref.shape[2]), lse, delta, scale)
    for a, d in enumerate(grads):
        out_ref[:, a] = d.astype(bf16).reshape(out_ref.shape[0], out_ref.shape[2], HEAD)


def row_grads(scale, scal, t, stats):
    rows, _, cols, feats = t.shape
    n = rows * cols
    return pl.pallas_call(
        lambda *refs: row_grads_body(scale, *refs),
        grid=(feats // HEAD,),
        in_specs=[smem(), head_block(t), pl.BlockSpec((1, 2, n), lambda h: (h, 0, 0))],
        out_specs=pl.BlockSpec((3, n, HEAD), lambda h: (0, 0, h)),
        out_shape=jax.ShapeDtypeStruct((3, n, feats), f32),
        compiler_params=params(),
        cost_estimate=cost(8),
        name="row_grads",
    )(scal, t, stats)


def col_grads(scale, scal, t, stats):
    rows, _, cols, feats = t.shape
    n = rows * cols
    return pl.pallas_call(
        lambda *refs: col_grads_body(scale, *refs),
        grid=(feats // HEAD,),
        in_specs=[smem(), head_block(t), pl.BlockSpec((1, 2, n), lambda h: (h, 0, 0))],
        out_specs=pl.BlockSpec((rows, 3, cols, HEAD), lambda h: (0, 0, 0, h)),
        out_shape=jax.ShapeDtypeStruct((rows, 3, cols, feats), bf16),
        compiler_params=params(),
        cost_estimate=cost(8),
        name="col_grads",
    )(scal, t, stats)


def join_body(scal_ref, row_ref, off_ref, col_ref, out_ref, total_ref):
    half_feats = off_ref.shape[2]
    for a in range(3):
        total_ref[a] = row_ref[a] + col_ref[:, a].astype(f32).reshape(row_ref.shape[1:])

    @pl.when(scal_ref[0] == 0)
    def _():
        for a in range(2):
            total_ref[a + 1, :, :half_feats] += off_ref[a]

    @pl.when(scal_ref[0] != 0)
    def _():
        total_ref[0, :, half_feats:] += off_ref[0]

    for a in range(3):
        out_ref[:, a] = total_ref[a].astype(bf16).reshape(out_ref.shape[0], *out_ref.shape[2:])


def join(scal, row, off, col):
    rows, _, cols, feats = col.shape
    steps = 4
    part = rows // steps
    n = part * cols
    return pl.pallas_call(
        join_body,
        grid=(steps,),
        in_specs=[
            smem(),
            pl.BlockSpec((3, n, feats), lambda i: (0, i, 0)),
            pl.BlockSpec((2, n, off.shape[2]), lambda i: (0, i, 0)),
            pl.BlockSpec((part, 3, cols, feats), lambda i: (i, 0, 0, 0)),
        ],
        out_specs=pl.BlockSpec((part, 3, cols, feats), lambda i: (i, 0, 0, 0)),
        out_shape=jax.ShapeDtypeStruct(col.shape, bf16),
        scratch_shapes=[pltpu.VMEM((3, n, feats), f32)],
        compiler_params=params(),
        name="join",
    )(scal, row, off, col)


def body(query_in, key_in, value_in, grad_out, row_start, col_start):
    scale = 1.0 / math.sqrt(HEAD)
    tokens, feats = query_in.shape
    lanes = lax.axis_size("wide")
    narrow = lax.axis_size("narrow")
    groups = narrow // HALVES
    half_cols = tokens * groups
    cols = half_cols // lanes
    subs = tokens // cols
    near = [[half * groups + j for j in range(groups)] for half in range(HALVES)]

    def exchange_near(arr):
        return lax.all_to_all(
            arr, "narrow", split_axis=0, concat_axis=0, axis_index_groups=near, tiled=True
        )

    def exchange_wide(arr):
        return lax.all_to_all(arr, "wide", split_axis=0, concat_axis=0, tiled=True)

    def shift(arr, source, target):
        pairs = [(source * groups + j, target * groups + j) for j in range(groups)]
        return lax.ppermute(arr, "narrow", pairs)

    def swap(arr, step):
        pairs = [(i, i ^ step) for i in range(narrow)]
        return lax.ppermute(arr, "narrow", pairs)

    def spread(arr):
        pieces = []
        for step in range(groups):
            piece = lax.dynamic_index_in_dim(arr, near_index ^ step, keepdims=False)
            pieces.append(swap(piece, step) if step else piece)
        return pieces

    wide_index = lax.axis_index("wide")
    narrow_index = lax.axis_index("narrow")
    half = narrow_index // groups
    near_index = narrow_index % groups
    first_col = lax.dynamic_index_in_dim(row_start, wide_index, keepdims=False)
    block_id = (half * half_cols + wide_index * cols) // CB
    first_row = lax.dynamic_index_in_dim(col_start, block_id, keepdims=False)
    scal = jnp.stack([half, first_col, first_row, near_index]).astype(jnp.int32)

    packed, packed_far = pack(scal, key_in, value_in, query_in, grad_out, groups, subs, cols)
    near_feats = feats // groups
    heads = near_feats // HEAD
    near_heads = heads // HALVES
    far = swap(packed_far, groups)
    t = exchange_near(packed).reshape(lanes, 4, cols, near_feats)
    t, far = lax.optimization_barrier((t, far))
    by_col = exchange_wide(t)
    pieces = spread(far)
    diag_part = stats_call(row_stats_body, scale, scal, (t,), "row_stats", 4)
    own_off = off_stats(scale, scal, t, pieces)
    off_part = jnp.concatenate([shift(own_off, 0, 1), own_off])
    lse, delta = merge(diag_part[:, 0], diag_part[:, 1], off_part[:, 0], off_part[:, 1])
    row_part = jnp.where(half == 1, jnp.stack([lse, delta], axis=1), diag_part)
    col_part = stats_call(col_stats_body, scale, scal, (by_col,), "col_stats", 4)

    both = jnp.stack([row_part, col_part]).reshape(4 * heads, lanes, cols)
    sent = both.transpose(1, 0, 2).reshape(lanes, (4 * heads * cols) // HEAD, HEAD)
    got = exchange_wide(sent).reshape(lanes, 4 * heads, cols).transpose(1, 0, 2)
    got = got.reshape(2, heads, 2, lanes * cols)
    row_lse, row_delta = merge(row_part[:, 0], row_part[:, 1], got[1, :, 0], got[1, :, 1])
    col_lse, col_delta = merge(col_part[:, 0], col_part[:, 1], got[0, :, 0], got[0, :, 1])
    row_full = jnp.stack([row_lse, row_delta], axis=1)
    col_full = jnp.stack([col_lse, col_delta], axis=1)

    far_full = shift(row_full[:near_heads], 1, 0)
    col_terms = col_grads(scale, scal, by_col, col_full)
    col_terms, far_full = lax.optimization_barrier((col_terms, far_full))
    from_col = exchange_wide(col_terms)
    row_terms = row_grads(scale, scal, t, row_full)
    off_full = jnp.where(half == 1, row_full[near_heads:], far_full)
    off_terms, far_terms = off_grads(scale, scal, t, off_full, pieces)
    far_terms = jnp.stack(spread(far_terms))
    from_col, far_terms = lax.optimization_barrier((from_col, far_terms))
    back = swap(far_terms, groups)
    joined = join(scal, row_terms, off_terms, from_col)
    out = exchange_near(joined.reshape(groups, subs, 3, cols, near_feats))
    return unpack(scal, out, back, tokens, feats)


def solution(mesh):
    placed = P(("wide", "narrow"), None)
    return jax.shard_map(
        body,
        mesh=mesh,
        in_specs=(placed,) * 4 + (P(), P()),
        out_specs=(placed,) * 3,
        check_vma=False,
    )
```

```python
import math

import jax
import jax.numpy as jnp
from jax import lax
from jax.experimental import pallas as pl
from jax.experimental.pallas import tpu as pltpu
from jax.sharding import PartitionSpec as P

HEAD = 128
CB = 128
HALVES = 2
VMEM_BYTES = 16 * 1024 * 1024

masked_low = -1e30
f32 = jnp.float32
bf16 = jnp.bfloat16
QI, GI, KI, VI = 2, 3, 0, 1


def dot_nt(a, b):
    return lax.dot_general(a, b, (((1,), (1,)), ((), ())), preferred_element_type=f32)


def dot_nn(a, b):
    return lax.dot_general(a, b, (((1,), (0,)), ((), ())), preferred_element_type=f32)


def dot_tn(a, b):
    return lax.dot_general(a, b, (((0,), (0,)), ((), ())), preferred_element_type=f32)


def params(n_axes=1):
    return pltpu.CompilerParams(
        dimension_semantics=("arbitrary",) * n_axes, vmem_limit_bytes=VMEM_BYTES
    )


def cost(units):
    return pl.CostEstimate(
        flops=units * 10 * 512 * 512 * 128, bytes_accessed=4 << 20, transcendentals=units * 512 * 512
    )


def pack_body(k_ref, v_ref, q_ref, g_ref, far_a_ref, far_b_ref, out_ref, near_sem, far_sem):
    groups, feats, far_feats = out_ref.shape[0], out_ref.shape[-1], far_a_ref.shape[-1]
    lower = lax.axis_index("narrow") < groups

    def far_copies(pair, first):
        for ref, far_ref in zip(pair, (far_a_ref, far_b_ref)):
            for j in range(groups):
                src = ref.at[:, :, pl.ds(j * feats + first, far_feats)]
                yield pltpu.make_async_copy(src, far_ref.at[j], far_sem)

    def near_copies():
        for j in range(groups):
            for a, ref in enumerate((k_ref, v_ref, q_ref, g_ref)):
                src = ref.at[:, :, pl.ds(j * feats, feats)]
                yield pltpu.make_async_copy(src, out_ref.at[j, :, a], near_sem)

    @pl.when(lower)
    def _():
        for copy in far_copies((k_ref, v_ref), far_feats):
            copy.start()

    @pl.when(jnp.logical_not(lower))
    def _():
        for copy in far_copies((q_ref, g_ref), 0):
            copy.start()

    for copy in near_copies():
        copy.start()
    for copy in far_copies((k_ref, v_ref), 0):
        copy.wait()
    for copy in near_copies():
        copy.wait()


def pack(k, v, q, g, groups, subs, cols):
    near_feats = k.shape[1] // groups
    far = (subs, cols, near_feats // HALVES)
    shapes = [far, far, (subs, 4, cols, near_feats)]
    split = [a.reshape(subs, cols, a.shape[1]) for a in (k, v, q, g)]
    return pl.pallas_call(
        pack_body,
        in_specs=[pl.BlockSpec(memory_space=pltpu.HBM)] * 4,
        out_specs=[pl.BlockSpec(memory_space=pltpu.VMEM)] * 3,
        out_shape=[jax.ShapeDtypeStruct((groups, *shape), bf16) for shape in shapes],
        scratch_shapes=[pltpu.SemaphoreType.DMA, pltpu.SemaphoreType.DMA],
        compiler_params=pltpu.CompilerParams(vmem_limit_bytes=VMEM_BYTES),
        name="pack",
    )(*split)


LONG = pl.CostEstimate(flops=200_000_000_000, bytes_accessed=400 << 20, transcendentals=0)


def hold_body(in_ref, out_ref):
    out_ref[...] = in_ref[...]


def hold(arr):
    return pl.pallas_call(
        hold_body,
        in_specs=[pl.BlockSpec(memory_space=pltpu.VMEM)],
        out_specs=pl.BlockSpec(memory_space=pltpu.VMEM),
        out_shape=jax.ShapeDtypeStruct(arr.shape, arr.dtype),
        compiler_params=pltpu.CompilerParams(vmem_limit_bytes=VMEM_BYTES),
        cost_estimate=LONG,
        name="hold",
    )(arr)


def split_body(a_ref, b_ref, *out_refs):
    groups = len(out_refs)
    near = lax.rem(lax.axis_index("narrow"), groups)
    for step, ref in enumerate(out_refs):
        for i, far_ref in enumerate((a_ref, b_ref)):
            ref[:, i] = far_ref[near ^ step]


def split(far_a, far_b):
    groups, subs, cols, feats = far_a.shape
    whole = pl.BlockSpec(memory_space=pltpu.VMEM)
    return pl.pallas_call(
        split_body,
        in_specs=[whole] * 2,
        out_specs=[whole] * groups,
        out_shape=[jax.ShapeDtypeStruct((subs, 2, cols, feats), bf16)] * groups,
        compiler_params=pltpu.CompilerParams(vmem_limit_bytes=VMEM_BYTES),
        cost_estimate=LONG,
        name="split",
    )(far_a, far_b)


def unpack_body(scal_ref, in_ref, far_ref, q_ref, k_ref, v_ref):
    _, subs, _, cols, _ = in_ref.shape
    far_feats = far_ref.shape[-1]
    for a, ref in enumerate((q_ref, k_ref, v_ref)):
        for s in range(subs):
            ref[s * cols : (s + 1) * cols, :] = in_ref[0, s, a]

    def add(ref, terms, feats):
        ref[:, feats] = (ref[:, feats].astype(f32) + terms.astype(f32)).astype(bf16)

    @pl.when(scal_ref[0] == 0)
    def _():
        upper = slice(far_feats, 2 * far_feats)
        add(k_ref, far_ref[0, 0], upper)
        add(v_ref, far_ref[0, 1], upper)

    @pl.when(scal_ref[0] != 0)
    def _():
        add(q_ref, far_ref[0, 0], slice(0, far_feats))


def unpack(scal, arr, far, tokens, feats):
    groups, subs, _, cols, near_feats = arr.shape
    out = jax.ShapeDtypeStruct((tokens, feats), bf16)
    far_spec = pl.BlockSpec((1, *far.shape[1:]), lambda j, scal_ref: (j ^ scal_ref[3], 0, 0, 0))
    return pl.pallas_call(
        unpack_body,
        grid_spec=pltpu.PrefetchScalarGridSpec(
            num_scalar_prefetch=1,
            grid=(groups,),
            in_specs=[
                pl.BlockSpec((1, subs, 3, cols, near_feats), lambda j, scal_ref: (j, 0, 0, 0, 0)),
                far_spec,
            ],
            out_specs=[pl.BlockSpec((tokens, near_feats), lambda j, scal_ref: (0, j))] * 3,
        ),
        out_shape=[out] * 3,
        compiler_params=params(),
        name="unpack",
    )(scal, arr, far)


def flat(ref, index):
    block = ref[:, index]
    return block.reshape(block.shape[0] * block.shape[1], block.shape[2])


def row_masks(scal_ref, n):
    first = scal_ref[1] - scal_ref[0] * n
    u = lax.broadcasted_iota(jnp.int32, (n, n), 0)
    t = lax.broadcasted_iota(jnp.int32, (n, n), 1)
    return (u == t) | ((u < t) & (u >= first))


def off_mask(scal_ref, n):
    u = lax.broadcasted_iota(jnp.int32, (n, n), 0)
    return u >= scal_ref[1]


def col_mask(scal_ref, n, cols):
    u = lax.broadcasted_iota(jnp.int32, (n, n), 0)
    t = lax.broadcasted_iota(jnp.int32, (n, n), 1)
    same = (u & (cols - 1)) == (t & (cols - 1))
    return same & (u < t) & (u >= scal_ref[2] * cols)


def partial_stats(k, v, q, g, mask, scale):
    s = jnp.where(mask, dot_nt(k, q) * scale, masked_low)
    m = jnp.max(s, axis=0, keepdims=True)
    e = jnp.where(mask, jnp.exp(s - m), 0.0)
    total = jnp.sum(e, axis=0, keepdims=True)
    weighted = jnp.sum(e * dot_nt(v, g), axis=0, keepdims=True)
    some = total > 0.0
    total = jnp.where(some, total, 1.0)
    return jnp.where(some, m + jnp.log(total), masked_low), weighted / total


def merge(lse_a, delta_a, lse_b, delta_b):
    top = jnp.maximum(lse_a, lse_b)
    a = jnp.exp(lse_a - top)
    b = jnp.exp(lse_b - top)
    total = a + b
    return top + jnp.log(total), (a * delta_a + b * delta_b) / total


def row_stats_body(scale, scal_ref, t_ref, out_ref):
    k, v, q, g = (flat(t_ref, i) for i in range(4))
    lse, delta = partial_stats(k, v, q, g, row_masks(scal_ref, k.shape[0]), scale)
    out_ref[0, 0:1] = lse
    out_ref[0, 1:2] = delta


def gather_far(scal_ref, piece_refs, buf):
    for i, ref in enumerate(piece_refs):
        for a in range(2):
            buf[a, scal_ref[3] ^ i] = flat(ref, a)
    return (buf[a].reshape(buf.shape[1] * buf.shape[2], HEAD) for a in range(2))


def off_stats_body(scale, scal_ref, t_ref, *refs):
    *piece_refs, out_ref, buf = refs
    far_a, far_b = gather_far(scal_ref, piece_refs, buf)

    def run(k, v, q, g):
        lse, delta = partial_stats(k, v, q, g, off_mask(scal_ref, k.shape[0]), scale)
        out_ref[0, 0:1] = lse
        out_ref[0, 1:2] = delta

    @pl.when(scal_ref[0] == 0)
    def _():
        run(flat(t_ref, KI), flat(t_ref, VI), far_a, far_b)

    @pl.when(scal_ref[0] != 0)
    def _():
        run(far_a, far_b, flat(t_ref, QI), flat(t_ref, GI))


def col_stats_body(scale, scal_ref, t_ref, out_ref):
    k, v, q, g = (flat(t_ref, i) for i in range(4))
    n = k.shape[0]
    lse, delta = partial_stats(k, v, q, g, col_mask(scal_ref, n, t_ref.shape[2]), scale)
    out_ref[0, 0:1] = lse
    out_ref[0, 1:2] = delta


def smem():
    return pl.BlockSpec(memory_space=pltpu.SMEM)


def head_block(arr):
    a, b, c, _ = arr.shape
    return pl.BlockSpec((a, b, c, HEAD), lambda h: (0, 0, 0, h))


def off_block(arr, heads):
    a, b, c, _ = arr.shape
    return pl.BlockSpec((a, b, c, HEAD), lambda h, scal_ref: (0, 0, 0, h + scal_ref[0] * heads))


def off_call(body, scale, scal, t, extra, pieces, out_specs, out_shape, units, name):
    heads = pieces[0].shape[3] // HEAD
    tokens = pieces[0].shape[0] * pieces[0].shape[2]
    rows, _, cols, _ = t.shape
    stat_spec = pl.BlockSpec((1, 2, rows * cols), lambda h, scal_ref: (h, 0, 0))
    piece_specs = [
        pl.BlockSpec((*p.shape[:3], HEAD), lambda h, scal_ref: (0, 0, 0, h)) for p in pieces
    ]
    return pl.pallas_call(
        lambda *refs: body(scale, *refs),
        grid_spec=pltpu.PrefetchScalarGridSpec(
            num_scalar_prefetch=1,
            grid=(heads,),
            in_specs=[off_block(t, heads)] + [stat_spec] * len(extra) + piece_specs,
            out_specs=out_specs,
            scratch_shapes=[pltpu.VMEM((2, len(pieces), tokens, HEAD), bf16)],
        ),
        out_shape=out_shape,
        compiler_params=params(),
        cost_estimate=cost(units),
        name=name,
    )(scal, t, *extra, *pieces)


def off_stats(scale, scal, t, pieces):
    heads = pieces[0].shape[3] // HEAD
    n = t.shape[0] * t.shape[2]
    return off_call(
        off_stats_body, scale, scal, t, (), pieces,
        pl.BlockSpec((1, 2, n), lambda h, scal_ref: (h, 0, 0)),
        jax.ShapeDtypeStruct((heads, 2, n), f32), 2, "off_stats",
    )


def off_grads_body(scale, scal_ref, t_ref, stat_ref, *refs):
    *piece_refs, near_ref, far_ref, buf = refs
    far_a, far_b = gather_far(scal_ref, piece_refs, buf)
    lse, delta = stat_ref[0, 0:1], stat_ref[0, 1:2]

    def run(k, v, q, g):
        return block_grads(k, v, q, g, off_mask(scal_ref, k.shape[0]), lse, delta, scale)

    @pl.when(scal_ref[0] == 0)
    def _():
        dq, dk, dv = run(flat(t_ref, KI), flat(t_ref, VI), far_a, far_b)
        near_ref[0] = dk
        near_ref[1] = dv
        far_ref[:, 0] = dq.astype(bf16).reshape(far_ref.shape[0], far_ref.shape[2], HEAD)

    @pl.when(scal_ref[0] != 0)
    def _():
        dq, dk, dv = run(far_a, far_b, flat(t_ref, QI), flat(t_ref, GI))
        near_ref[0] = dq
        for a, d in enumerate((dk, dv)):
            far_ref[:, a] = d.astype(bf16).reshape(far_ref.shape[0], far_ref.shape[2], HEAD)


def off_grads(scale, scal, t, stats, pieces):
    n = t.shape[0] * t.shape[2]
    feats = pieces[0].shape[3]
    far_shape = (len(pieces), 2, n // len(pieces), feats)
    return off_call(
        off_grads_body, scale, scal, t, (stats,), pieces,
        [
            pl.BlockSpec((2, n, HEAD), lambda h, scal_ref: (0, 0, h)),
            pl.BlockSpec((*far_shape[:3], HEAD), lambda h, scal_ref: (0, 0, 0, h)),
        ],
        [jax.ShapeDtypeStruct((2, n, feats), f32), jax.ShapeDtypeStruct(far_shape, bf16)],
        5,
        "off_grads",
    )


def stats_call(body, scale, scal, arrays, name, units):
    heads = arrays[0].shape[3] // HEAD
    n = arrays[0].shape[0] * arrays[0].shape[2]
    return pl.pallas_call(
        lambda *refs: body(scale, *refs),
        grid=(heads,),
        in_specs=[smem()] + [head_block(a) for a in arrays],
        out_specs=pl.BlockSpec((1, 2, n), lambda h: (h, 0, 0)),
        out_shape=jax.ShapeDtypeStruct((heads, 2, n), f32),
        compiler_params=params(),
        cost_estimate=cost(units),
        name=name,
    )(scal, *arrays)


def block_grads(k, v, q, g, mask, lse, delta, scale):
    p = jnp.where(mask, jnp.exp(dot_nt(k, q) * scale - lse), 0.0)
    ds = (p * (dot_nt(v, g) - delta)).astype(bf16)
    dv = dot_nn(p.astype(bf16), g)
    dk = dot_nn(ds, q) * scale
    dq = dot_tn(ds, k) * scale
    return dq, dk, dv


def row_grads_body(scale, scal_ref, t_ref, stat_ref, off_ref, out_ref, sum_ref):
    k, v, q, g = (flat(t_ref, i) for i in range(4))
    mask = row_masks(scal_ref, k.shape[0])
    grads = block_grads(k, v, q, g, mask, stat_ref[0, 0:1], stat_ref[0, 1:2], scale)
    upper = scal_ref[0] != 0
    has_off = (pl.program_id(0) >= pl.num_programs(0) // HALVES) == upper
    for a, d in enumerate(grads):
        sum_ref[a] = d

    @pl.when(has_off & upper)
    def _():
        sum_ref[0] += off_ref[0]

    @pl.when(has_off & jnp.logical_not(upper))
    def _():
        sum_ref[1] += off_ref[0]
        sum_ref[2] += off_ref[1]

    for a in range(3):
        out_ref[:, a] = sum_ref[a].astype(bf16).reshape(out_ref.shape[0], out_ref.shape[2], HEAD)


def col_grads_body(scale, scal_ref, t_ref, stat_ref, out_ref):
    k, v, q, g = (flat(t_ref, i) for i in range(4))
    n = k.shape[0]
    lse, delta = stat_ref[0, 0:1], stat_ref[0, 1:2]
    grads = block_grads(k, v, q, g, col_mask(scal_ref, n, t_ref.shape[2]), lse, delta, scale)
    for a, d in enumerate(grads):
        out_ref[:, a] = d.astype(bf16).reshape(out_ref.shape[0], out_ref.shape[2], HEAD)


def row_grads(scale, scal, t, stats, off):
    rows, _, cols, feats = t.shape
    n = rows * cols
    near_heads = off.shape[2] // HEAD
    return pl.pallas_call(
        lambda *refs: row_grads_body(scale, *refs),
        grid=(feats // HEAD,),
        in_specs=[
            smem(),
            head_block(t),
            pl.BlockSpec((1, 2, n), lambda h: (h, 0, 0)),
            pl.BlockSpec((2, n, HEAD), lambda h: (0, 0, h % near_heads)),
        ],
        out_specs=pl.BlockSpec((rows, 3, cols, HEAD), lambda h: (0, 0, 0, h)),
        out_shape=jax.ShapeDtypeStruct((rows, 3, cols, feats), bf16),
        scratch_shapes=[pltpu.VMEM((3, n, HEAD), f32)],
        compiler_params=params(),
        cost_estimate=cost(8),
        name="row_grads",
    )(scal, t, stats, off)


def col_grads(scale, scal, t, stats):
    rows, _, cols, feats = t.shape
    n = rows * cols
    return pl.pallas_call(
        lambda *refs: col_grads_body(scale, *refs),
        grid=(feats // HEAD,),
        in_specs=[smem(), head_block(t), pl.BlockSpec((1, 2, n), lambda h: (h, 0, 0))],
        out_specs=pl.BlockSpec((rows, 3, cols, HEAD), lambda h: (0, 0, 0, h)),
        out_shape=jax.ShapeDtypeStruct((rows, 3, cols, feats), bf16),
        compiler_params=params(),
        cost_estimate=cost(8),
        name="col_grads",
    )(scal, t, stats)


def join_body(row_ref, col_ref, out_ref):
    out_ref[...] = (row_ref[...].astype(f32) + col_ref[...].astype(f32)).astype(bf16)


def join(row, col):
    rows, arrays, cols, feats = col.shape
    steps = 4
    spec = pl.BlockSpec((rows // steps, arrays, cols, feats), lambda i: (i, 0, 0, 0))
    return pl.pallas_call(
        join_body,
        grid=(steps,),
        in_specs=[spec, spec],
        out_specs=spec,
        out_shape=jax.ShapeDtypeStruct(col.shape, bf16),
        compiler_params=params(),
        name="join",
    )(row, col)


def body(query_in, key_in, value_in, grad_out, row_start, col_start):
    scale = 1.0 / math.sqrt(HEAD)
    tokens, feats = query_in.shape
    lanes = lax.axis_size("wide")
    narrow = lax.axis_size("narrow")
    groups = narrow // HALVES
    half_cols = tokens * groups
    cols = half_cols // lanes
    subs = tokens // cols
    near = [[half * groups + j for j in range(groups)] for half in range(HALVES)]

    def exchange_near(arr):
        return lax.all_to_all(
            arr, "narrow", split_axis=0, concat_axis=0, axis_index_groups=near, tiled=True
        )

    def exchange_wide(arr):
        return lax.all_to_all(arr, "wide", split_axis=0, concat_axis=0, tiled=True)

    def shift(arr, source, target):
        pairs = [(source * groups + j, target * groups + j) for j in range(groups)]
        return lax.ppermute(arr, "narrow", pairs)

    def swap(arr, step):
        pairs = [(i, i ^ step) for i in range(narrow)]
        return lax.ppermute(arr, "narrow", pairs)

    def spread(pieces):
        return [swap(piece, step) if step else piece for step, piece in enumerate(pieces)]

    wide_index = lax.axis_index("wide")
    narrow_index = lax.axis_index("narrow")
    half = narrow_index // groups
    near_index = narrow_index % groups
    first_col = lax.dynamic_index_in_dim(row_start, wide_index, keepdims=False)
    block_id = (half * half_cols + wide_index * cols) // CB
    first_row = lax.dynamic_index_in_dim(col_start, block_id, keepdims=False)
    scal = jnp.stack([half, first_col, first_row, near_index]).astype(jnp.int32)

    far_a, far_b, packed = pack(key_in, value_in, query_in, grad_out, groups, subs, cols)
    near_feats = feats // groups
    heads = near_feats // HEAD
    near_heads = heads // HALVES
    far_a = hold(swap(far_a, groups))
    far_b = swap(far_b, groups)
    t = exchange_near(packed).reshape(lanes, 4, cols, near_feats)
    t, far_a = lax.optimization_barrier((t, far_a))
    by_col = exchange_wide(t)
    pieces = spread(split(far_a, far_b))
    diag_part = stats_call(row_stats_body, scale, scal, (t,), "row_stats", 4)
    own_off = off_stats(scale, scal, t, pieces)
    off_part = jnp.concatenate([shift(own_off, 0, 1), own_off])
    lse, delta = merge(diag_part[:, 0], diag_part[:, 1], off_part[:, 0], off_part[:, 1])
    row_part = jnp.where(half == 1, jnp.stack([lse, delta], axis=1), diag_part)
    col_part = stats_call(col_stats_body, scale, scal, (by_col,), "col_stats", 4)

    both = jnp.stack([row_part, col_part]).reshape(4 * heads, lanes, cols)
    sent = both.transpose(1, 0, 2).reshape(lanes, (4 * heads * cols) // HEAD, HEAD)
    got = exchange_wide(sent).reshape(lanes, 4 * heads, cols).transpose(1, 0, 2)
    got = got.reshape(2, heads, 2, lanes * cols)
    row_lse, row_delta = merge(row_part[:, 0], row_part[:, 1], got[1, :, 0], got[1, :, 1])
    col_lse, col_delta = merge(col_part[:, 0], col_part[:, 1], got[0, :, 0], got[0, :, 1])
    row_full = jnp.stack([row_lse, row_delta], axis=1)
    col_full = jnp.stack([col_lse, col_delta], axis=1)

    far_full = hold(shift(row_full[:near_heads], 1, 0))
    from_col = exchange_wide(col_grads(scale, scal, by_col, col_full))
    off_full = jnp.where(half == 1, row_full[near_heads:], far_full)
    off_terms, far_terms = off_grads(scale, scal, t, off_full, pieces)
    row_terms = row_grads(scale, scal, t, row_full, off_terms)
    by_step = [
        lax.dynamic_index_in_dim(far_terms, near_index ^ step, keepdims=False)
        for step in range(groups)
    ]
    far_terms = jnp.stack(spread(by_step))
    from_col, far_terms, row_terms = lax.optimization_barrier((from_col, far_terms, row_terms))
    back = hold(swap(far_terms, groups))
    joined = join(row_terms, from_col)
    out = exchange_near(joined.reshape(groups, subs, 3, cols, near_feats))
    return unpack(scal, out, back, tokens, feats)


def solution(mesh):
    placed = P(("wide", "narrow"), None)
    return jax.shard_map(
        body,
        mesh=mesh,
        in_specs=(placed,) * 4 + (P(), P()),
        out_specs=(placed,) * 3,
        check_vma=False,
    )
```

```python
import math

import jax
import jax.numpy as jnp
from jax import lax
from jax.experimental import pallas as pl
from jax.experimental.pallas import tpu as pltpu
from jax.sharding import PartitionSpec as P

HEAD = 128
CB = 128
HALVES = 2
VMEM_BYTES = 16 * 1024 * 1024
PACK_BYTES = 60 * 1024 * 1024

masked_low = -1e30
least_max = -1e29
score_scale = 1.0 / math.sqrt(HEAD)
f32 = jnp.float32
bf16 = jnp.bfloat16
QI, GI, KI, VI = 2, 3, 0, 1


def dot_nt(a, b):
    return lax.dot_general(a, b, (((1,), (1,)), ((), ())), preferred_element_type=f32)


def dot_nn(a, b):
    return lax.dot_general(a, b, (((1,), (0,)), ((), ())), preferred_element_type=f32)


def dot_tn(a, b):
    return lax.dot_general(a, b, (((0,), (0,)), ((), ())), preferred_element_type=f32)


def params(n_axes=1):
    return pltpu.CompilerParams(
        dimension_semantics=("arbitrary",) * n_axes, vmem_limit_bytes=VMEM_BYTES
    )


def cost(units):
    return pl.CostEstimate(
        flops=units * 10 * 512 * 512 * 128, bytes_accessed=4 << 20, transcendentals=units * 512 * 512
    )


def pack_body(k_ref, v_ref, q_ref, g_ref, far_a_ref, far_b_ref, out_ref, near_sem, far_sem):
    groups, feats, far_feats = out_ref.shape[0], out_ref.shape[-1], far_a_ref.shape[-1]
    lower = lax.axis_index("narrow") < groups

    def far_copies(pair, first):
        for ref, far_ref in zip(pair, (far_a_ref, far_b_ref)):
            for j in range(groups):
                src = ref.at[:, :, pl.ds(j * feats + first, far_feats)]
                yield pltpu.make_async_copy(src, far_ref.at[j], far_sem)

    def near_copies():
        for j in range(groups):
            for a, ref in enumerate((k_ref, v_ref, q_ref, g_ref)):
                src = ref.at[:, :, pl.ds(j * feats, feats)]
                yield pltpu.make_async_copy(src, out_ref.at[j, :, a], near_sem)

    @pl.when(lower)
    def _():
        for copy in far_copies((k_ref, v_ref), far_feats):
            copy.start()

    @pl.when(jnp.logical_not(lower))
    def _():
        for copy in far_copies((q_ref, g_ref), 0):
            copy.start()

    for copy in near_copies():
        copy.start()
    for copy in far_copies((k_ref, v_ref), 0):
        copy.wait()
    for copy in near_copies():
        copy.wait()


def pack(k, v, q, g, groups, subs, cols):
    near_feats = k.shape[1] // groups
    far = (subs, cols, near_feats // HALVES)
    shapes = [far, far, (subs, 4, cols, near_feats)]
    split = [a.reshape(subs, cols, a.shape[1]) for a in (k, v, q, g)]
    return pl.pallas_call(
        pack_body,
        in_specs=[pl.BlockSpec(memory_space=pltpu.HBM)] * 4,
        out_specs=[pl.BlockSpec(memory_space=pltpu.VMEM)] * 3,
        out_shape=[jax.ShapeDtypeStruct((groups, *shape), bf16) for shape in shapes],
        scratch_shapes=[pltpu.SemaphoreType.DMA, pltpu.SemaphoreType.DMA],
        compiler_params=pltpu.CompilerParams(vmem_limit_bytes=PACK_BYTES),
        name="pack",
    )(*split)


LONG = pl.CostEstimate(flops=200_000_000_000, bytes_accessed=400 << 20, transcendentals=0)


def hold_body(in_ref, out_ref):
    out_ref[...] = jnp.zeros_like(out_ref)


def hold(arr):
    return pl.pallas_call(
        hold_body,
        in_specs=[pl.BlockSpec(memory_space=pl.ANY)],
        out_specs=pl.BlockSpec(memory_space=pltpu.VMEM),
        out_shape=jax.ShapeDtypeStruct((8, 128), f32),
        compiler_params=pltpu.CompilerParams(vmem_limit_bytes=1024 * 1024),
        cost_estimate=LONG,
        name="hold",
    )(arr)


def split_body(a_ref, b_ref, token_ref, *out_refs):
    groups = len(out_refs)
    near = lax.rem(lax.axis_index("narrow"), groups)
    for step, ref in enumerate(out_refs):
        for i, far_ref in enumerate((a_ref, b_ref)):
            ref[:, i] = far_ref[near ^ step]


def split(far_a, far_b, token):
    groups, subs, cols, feats = far_a.shape
    whole = pl.BlockSpec(memory_space=pltpu.VMEM)
    return pl.pallas_call(
        split_body,
        in_specs=[whole] * 2 + [pl.BlockSpec(memory_space=pl.ANY)],
        out_specs=[whole] * groups,
        out_shape=[jax.ShapeDtypeStruct((subs, 2, cols, feats), bf16)] * groups,
        compiler_params=pltpu.CompilerParams(vmem_limit_bytes=VMEM_BYTES),
        cost_estimate=LONG,
        name="split",
    )(far_a, far_b, token)


def unpack_body(scal_ref, in_ref, far_ref, token_ref, q_ref, k_ref, v_ref):
    members, subs, _, cols, feats = in_ref.shape
    far_feats = far_ref.shape[-1]
    for i in range(members):
        for a, ref in enumerate((q_ref, k_ref, v_ref)):
            for s in range(subs):
                ref[s * cols : (s + 1) * cols, i * feats : (i + 1) * feats] = in_ref[i, s, a]

    def add(ref, i, a, first):
        place = (pl.program_id(0) * members + i) ^ scal_ref[3]
        feat_cols = slice(i * feats + first, i * feats + first + far_feats)
        total = ref[:, feat_cols].astype(f32) + far_ref[place, a].astype(f32)
        ref[:, feat_cols] = total.astype(bf16)

    @pl.when(scal_ref[0] == 0)
    def _():
        for i in range(members):
            add(k_ref, i, 0, far_feats)
            add(v_ref, i, 1, far_feats)

    @pl.when(scal_ref[0] != 0)
    def _():
        for i in range(members):
            add(q_ref, i, 0, 0)


def unpack(scal, arr, far, token, tokens, feats):
    groups, subs, _, cols, near_feats = arr.shape
    members = 2
    out = jax.ShapeDtypeStruct((tokens, feats), bf16)
    return pl.pallas_call(
        unpack_body,
        grid=(groups // members,),
        in_specs=[
            smem(),
            pl.BlockSpec((members, subs, 3, cols, near_feats), lambda j: (j, 0, 0, 0, 0)),
            pl.BlockSpec(far.shape, lambda j: (0, 0, 0, 0)),
            pl.BlockSpec(memory_space=pl.ANY),
        ],
        out_specs=[pl.BlockSpec((tokens, members * near_feats), lambda j: (0, j))] * 3,
        out_shape=[out] * 3,
        compiler_params=params(),
        name="unpack",
    )(scal, arr, far, token)


def flat(ref, index):
    block = ref[:, index]
    return block.reshape(block.shape[0] * block.shape[1], block.shape[2])


def row_mask(scal_ref, n):
    first = scal_ref[1] - scal_ref[0] * n
    u = lax.broadcasted_iota(jnp.int32, (n, n), 0)
    t = lax.broadcasted_iota(jnp.int32, (n, n), 1)
    return (u == t) | ((u < t) & (u >= first))


def off_mask(scal_ref, n):
    return lax.broadcasted_iota(jnp.int32, (n, n), 0) >= scal_ref[1]


def col_mask(scal_ref, n, cols):
    u = lax.broadcasted_iota(jnp.int32, (n, n), 0)
    t = lax.broadcasted_iota(jnp.int32, (n, n), 1)
    same = (u & (cols - 1)) == (t & (cols - 1))
    return same & (u < t) & (u >= scal_ref[2] * cols)


def fill_bias(bias_ref, mask):
    @pl.when(pl.program_id(0) == 0)
    def _():
        bias_ref[...] = jnp.where(mask(bias_ref.shape[0]), 0.0, masked_low)


def partial_stats(k, v, q, g, bias, scale):
    s = dot_nt(k, q) * scale + bias
    m = jnp.maximum(jnp.max(s, axis=0, keepdims=True), least_max)
    e = jnp.exp2(s - m)
    total = jnp.sum(e, axis=0, keepdims=True)
    weighted = jnp.sum(e * dot_nt(v, g), axis=0, keepdims=True)
    some = total > 0.0
    total = jnp.where(some, total, 1.0)
    return jnp.where(some, m + jnp.log2(total), masked_low), weighted / total


def merge(lse_a, delta_a, lse_b, delta_b):
    top = jnp.maximum(lse_a, lse_b)
    a = jnp.exp2(lse_a - top)
    b = jnp.exp2(lse_b - top)
    total = a + b
    return top + jnp.log2(total), (a * delta_a + b * delta_b) / total


def row_stats_body(scale, scal_ref, t_ref, out_ref, bias_ref):
    fill_bias(bias_ref, lambda n: row_mask(scal_ref, n))
    k, v, q, g = (flat(t_ref, i) for i in range(4))
    lse, delta = partial_stats(k, v, q, g, bias_ref[...], scale)
    out_ref[0, 0:1] = lse
    out_ref[0, 1:2] = delta


def gather_far(scal_ref, piece_refs, buf):
    for i, ref in enumerate(piece_refs):
        for a in range(2):
            buf[a, scal_ref[3] ^ i] = flat(ref, a)
    return (buf[a].reshape(buf.shape[1] * buf.shape[2], HEAD) for a in range(2))


def off_stats_body(scale, scal_ref, t_ref, *refs):
    *piece_refs, out_ref, buf, bias_ref = refs
    fill_bias(bias_ref, lambda n: off_mask(scal_ref, n))
    far_a, far_b = gather_far(scal_ref, piece_refs, buf)

    def run(k, v, q, g):
        lse, delta = partial_stats(k, v, q, g, bias_ref[...], scale)
        out_ref[0, 0:1] = lse
        out_ref[0, 1:2] = delta

    @pl.when(scal_ref[0] == 0)
    def _():
        run(flat(t_ref, KI), flat(t_ref, VI), far_a, far_b)

    @pl.when(scal_ref[0] != 0)
    def _():
        run(far_a, far_b, flat(t_ref, QI), flat(t_ref, GI))


def col_blocks(n):
    step = n
    return [slice(i, i + step) for i in range(0, n, step)]


def col_stats_body(scale, scal_ref, t_ref, out_ref, bias_ref):
    fill_bias(bias_ref, lambda n: col_mask(scal_ref, n, t_ref.shape[2]))
    k, v, q, g = (flat(t_ref, i) for i in range(4))
    for part in col_blocks(k.shape[0]):
        upto = slice(0, part.stop)
        lse, delta = partial_stats(k[upto], v[upto], q[part], g[part], bias_ref[upto, part], scale)
        out_ref[0, 0:1, part] = lse
        out_ref[0, 1:2, part] = delta


def smem():
    return pl.BlockSpec(memory_space=pltpu.SMEM)


def head_block(arr):
    a, b, c, _ = arr.shape
    return pl.BlockSpec((a, b, c, HEAD), lambda h: (0, 0, 0, h))


def off_block(arr, heads):
    a, b, c, _ = arr.shape
    return pl.BlockSpec((a, b, c, HEAD), lambda h, scal_ref: (0, 0, 0, h + scal_ref[0] * heads))


def off_call(body, scale, scal, t, extra, extra_specs, pieces, out_specs, out_shape, units, name):
    heads = pieces[0].shape[3] // HEAD
    tokens = pieces[0].shape[0] * pieces[0].shape[2]
    rows, _, cols, _ = t.shape
    stat_spec = pl.BlockSpec((1, 2, rows * cols), lambda h, scal_ref: (h, 0, 0))
    piece_specs = [
        pl.BlockSpec((*p.shape[:3], HEAD), lambda h, scal_ref: (0, 0, 0, h)) for p in pieces
    ]
    return pl.pallas_call(
        lambda *refs: body(scale, *refs),
        grid_spec=pltpu.PrefetchScalarGridSpec(
            num_scalar_prefetch=1,
            grid=(heads,),
            in_specs=[off_block(t, heads)] + [spec or stat_spec for spec in extra_specs] + piece_specs,
            out_specs=out_specs,
            scratch_shapes=[
                pltpu.VMEM((2, len(pieces), tokens, HEAD), bf16),
                pltpu.VMEM((rows * cols, rows * cols), f32),
            ],
        ),
        out_shape=out_shape,
        compiler_params=params(),
        cost_estimate=cost(units),
        name=name,
    )(scal, t, *extra, *pieces)


def off_stats(scale, scal, t, pieces):
    heads = pieces[0].shape[3] // HEAD
    n = t.shape[0] * t.shape[2]
    return off_call(
        off_stats_body, scale, scal, t, (), (), pieces,
        pl.BlockSpec((1, 2, n), lambda h, scal_ref: (h, 0, 0)),
        jax.ShapeDtypeStruct((heads, 2, n), f32), 2, "off_stats",
    )


def off_grads_body(scale, scal_ref, t_ref, stat_ref, token_ref, *refs):
    *piece_refs, near_ref, far_ref, buf, bias_ref = refs
    fill_bias(bias_ref, lambda n: off_mask(scal_ref, n))
    far_a, far_b = gather_far(scal_ref, piece_refs, buf)
    lse, delta = stat_ref[0, 0:1], stat_ref[0, 1:2]

    def run(k, v, q, g):
        return block_grads(k, v, q, g, bias_ref[...], lse, delta, scale)

    @pl.when(scal_ref[0] == 0)
    def _():
        dq, dk, dv = run(flat(t_ref, KI), flat(t_ref, VI), far_a, far_b)
        near_ref[0] = dk
        near_ref[1] = dv
        far_ref[:, 0] = dq.astype(bf16).reshape(far_ref.shape[0], far_ref.shape[2], HEAD)

    @pl.when(scal_ref[0] != 0)
    def _():
        dq, dk, dv = run(far_a, far_b, flat(t_ref, QI), flat(t_ref, GI))
        near_ref[0] = dq
        for a, d in enumerate((dk, dv)):
            far_ref[:, a] = d.astype(bf16).reshape(far_ref.shape[0], far_ref.shape[2], HEAD)


def off_grads(scale, scal, t, stats, token, pieces):
    n = t.shape[0] * t.shape[2]
    feats = pieces[0].shape[3]
    far_shape = (len(pieces), 2, n // len(pieces), feats)
    return off_call(
        off_grads_body, scale, scal, t, (stats, token),
        (None, pl.BlockSpec(memory_space=pl.ANY)), pieces,
        [
            pl.BlockSpec((2, n, HEAD), lambda h, scal_ref: (0, 0, h)),
            pl.BlockSpec((*far_shape[:3], HEAD), lambda h, scal_ref: (0, 0, 0, h)),
        ],
        [jax.ShapeDtypeStruct((2, n, feats), f32), jax.ShapeDtypeStruct(far_shape, bf16)],
        5,
        "off_grads",
    )


def stats_call(body, scale, scal, arrays, name, units):
    heads = arrays[0].shape[3] // HEAD
    n = arrays[0].shape[0] * arrays[0].shape[2]
    return pl.pallas_call(
        lambda *refs: body(scale, *refs),
        grid=(heads,),
        in_specs=[smem()] + [head_block(a) for a in arrays],
        out_specs=pl.BlockSpec((1, 2, n), lambda h: (h, 0, 0)),
        out_shape=jax.ShapeDtypeStruct((heads, 2, n), f32),
        scratch_shapes=[pltpu.VMEM((n, n), f32)],
        compiler_params=params(),
        cost_estimate=cost(units),
        name=name,
    )(scal, *arrays)


def block_grads(k, v, q, g, bias, lse, delta, scale):
    p = jnp.exp2(dot_nt(k, q) * scale + (bias - lse))
    ds = (p * (dot_nt(v, g) - delta)).astype(bf16)
    dv = dot_nn(p.astype(bf16), g)
    dk = dot_nn(ds, q) * score_scale
    dq = dot_tn(ds, k) * score_scale
    return dq, dk, dv


def row_grads_body(scale, scal_ref, t_ref, stat_ref, off_ref, out_ref, sum_ref, bias_ref):
    fill_bias(bias_ref, lambda n: row_mask(scal_ref, n))
    k, v, q, g = (flat(t_ref, i) for i in range(4))
    grads = block_grads(k, v, q, g, bias_ref[...], stat_ref[0, 0:1], stat_ref[0, 1:2], scale)
    upper = scal_ref[0] != 0
    has_off = (pl.program_id(0) >= pl.num_programs(0) // HALVES) == upper
    for a, d in enumerate(grads):
        sum_ref[a] = d

    @pl.when(has_off & upper)
    def _():
        sum_ref[0] += off_ref[0]

    @pl.when(has_off & jnp.logical_not(upper))
    def _():
        sum_ref[1] += off_ref[0]
        sum_ref[2] += off_ref[1]

    for a in range(3):
        out_ref[:, a] = sum_ref[a].astype(bf16).reshape(out_ref.shape[0], out_ref.shape[2], HEAD)


def col_grads_body(scale, scal_ref, t_ref, own_ref, got_ref, out_ref, sum_ref, bias_ref):
    fill_bias(bias_ref, lambda n: col_mask(scal_ref, n, t_ref.shape[2]))
    k, v, q, g = (flat(t_ref, i) for i in range(4))
    lse, delta = merge(own_ref[0, 0:1], own_ref[0, 1:2], got_ref[0, 0:1], got_ref[0, 1:2])
    blocks = col_blocks(k.shape[0])
    for i, part in enumerate(blocks):
        upto = slice(0, part.stop)
        dq, dk, dv = block_grads(
            k[upto], v[upto], q[part], g[part], bias_ref[upto, part], lse[:, part], delta[:, part], scale
        )
        sum_ref[0, part] = dq
        for a, d in ((1, dk), (2, dv)):
            if i:
                sum_ref[a, : part.start] += d[: part.start]
            sum_ref[a, part] = d[part.start :]
    for a in range(3):
        out_ref[:, a] = sum_ref[a].astype(bf16).reshape(out_ref.shape[0], out_ref.shape[2], HEAD)


def row_grads(scale, scal, t, stats, off):
    rows, _, cols, feats = t.shape
    n = rows * cols
    near_heads = off.shape[2] // HEAD
    return pl.pallas_call(
        lambda *refs: row_grads_body(scale, *refs),
        grid=(feats // HEAD,),
        in_specs=[
            smem(),
            head_block(t),
            pl.BlockSpec((1, 2, n), lambda h: (h, 0, 0)),
            pl.BlockSpec((2, n, HEAD), lambda h: (0, 0, h % near_heads)),
        ],
        out_specs=pl.BlockSpec((rows, 3, cols, HEAD), lambda h: (0, 0, 0, h)),
        out_shape=jax.ShapeDtypeStruct((rows, 3, cols, feats), bf16),
        scratch_shapes=[pltpu.VMEM((3, n, HEAD), f32), pltpu.VMEM((n, n), f32)],
        compiler_params=params(),
        cost_estimate=cost(8),
        name="row_grads",
    )(scal, t, stats, off)


def col_grads(scale, scal, t, own, got):
    rows, _, cols, feats = t.shape
    n = rows * cols
    stat_spec = pl.BlockSpec((1, 2, n), lambda h: (h, 0, 0))
    return pl.pallas_call(
        lambda *refs: col_grads_body(scale, *refs),
        grid=(feats // HEAD,),
        in_specs=[smem(), head_block(t), stat_spec, stat_spec],
        out_specs=pl.BlockSpec((rows, 3, cols, HEAD), lambda h: (0, 0, 0, h)),
        out_shape=jax.ShapeDtypeStruct((rows, 3, cols, feats), bf16),
        scratch_shapes=[pltpu.VMEM((3, n, HEAD), f32), pltpu.VMEM((n, n), f32)],
        compiler_params=params(),
        cost_estimate=cost(8),
        name="col_grads",
    )(scal, t, own, got)


def join_body(row_ref, col_ref, out_ref):
    out_ref[...] = (row_ref[...].astype(f32) + col_ref[...].astype(f32)).astype(bf16)


def join(row, col):
    rows, arrays, cols, feats = col.shape
    steps = 4
    spec = pl.BlockSpec((rows // steps, arrays, cols, feats), lambda i: (i, 0, 0, 0))
    return pl.pallas_call(
        join_body,
        grid=(steps,),
        in_specs=[spec, spec],
        out_specs=spec,
        out_shape=jax.ShapeDtypeStruct(col.shape, bf16),
        compiler_params=params(),
        name="join",
    )(row, col)


def body(query_in, key_in, value_in, grad_out, row_start, col_start):
    scale = score_scale * math.log2(math.e)
    tokens, feats = query_in.shape
    lanes = lax.axis_size("wide")
    narrow = lax.axis_size("narrow")
    groups = narrow // HALVES
    half_cols = tokens * groups
    cols = half_cols // lanes
    subs = tokens // cols
    near = [[half * groups + j for j in range(groups)] for half in range(HALVES)]

    def exchange_near(arr):
        return lax.all_to_all(
            arr, "narrow", split_axis=0, concat_axis=0, axis_index_groups=near, tiled=True
        )

    def exchange_wide(arr):
        return lax.all_to_all(arr, "wide", split_axis=0, concat_axis=0, tiled=True)

    def shift(arr, source, target):
        pairs = [(source * groups + j, target * groups + j) for j in range(groups)]
        return lax.ppermute(arr, "narrow", pairs)

    def swap(arr, step):
        pairs = [(i, i ^ step) for i in range(narrow)]
        return lax.ppermute(arr, "narrow", pairs)

    def spread(pieces):
        return [swap(piece, step) if step else piece for step, piece in enumerate(pieces)]

    wide_index = lax.axis_index("wide")
    narrow_index = lax.axis_index("narrow")
    half = narrow_index // groups
    near_index = narrow_index % groups
    first_col = lax.dynamic_index_in_dim(row_start, wide_index, keepdims=False)
    block_id = (half * half_cols + wide_index * cols) // CB
    first_row = lax.dynamic_index_in_dim(col_start, block_id, keepdims=False)
    scal = jnp.stack([half, first_col, first_row, near_index]).astype(jnp.int32)

    far_a, far_b, packed = pack(key_in, value_in, query_in, grad_out, groups, subs, cols)
    near_feats = feats // groups
    heads = near_feats // HEAD
    near_heads = heads // HALVES
    far_a = swap(far_a, groups)
    token = hold(far_a)
    far_b = swap(far_b, groups)
    t = exchange_near(packed).reshape(lanes, 4, cols, near_feats)
    t, token = lax.optimization_barrier((t, token))
    by_col = exchange_wide(t)
    pieces = spread(split(far_a, far_b, token))
    diag_part = stats_call(row_stats_body, scale, scal, (t,), "row_stats", 4)
    own_off = off_stats(scale, scal, t, pieces)
    off_part = jnp.concatenate([shift(own_off, 0, 1), own_off])
    lse, delta = merge(diag_part[:, 0], diag_part[:, 1], off_part[:, 0], off_part[:, 1])
    row_part = jnp.where(half == 1, jnp.stack([lse, delta], axis=1), diag_part)
    col_part = stats_call(col_stats_body, scale, scal, (by_col,), "col_stats", 4)

    both = jnp.stack([row_part, col_part]).reshape(4 * heads, lanes, cols)
    sent = both.transpose(1, 0, 2).reshape(lanes, (4 * heads * cols) // HEAD, HEAD)
    got = exchange_wide(sent).reshape(lanes, 4 * heads, cols).transpose(1, 0, 2)
    got = got.reshape(2, heads, 2, lanes * cols)
    row_lse, row_delta = merge(row_part[:, 0], row_part[:, 1], got[1, :, 0], got[1, :, 1])
    row_full = jnp.stack([row_lse, row_delta], axis=1)

    far_full = shift(row_full[:near_heads], 1, 0)
    token = hold(far_full)
    from_col = exchange_wide(col_grads(scale, scal, by_col, col_part, got[0]))
    off_full = jnp.where(half == 1, row_full[near_heads:], far_full)
    off_terms, far_terms = off_grads(scale, scal, t, off_full, token, pieces)
    row_terms = row_grads(scale, scal, t, row_full, off_terms)
    by_step = [
        lax.dynamic_index_in_dim(far_terms, near_index ^ step, keepdims=False)
        for step in range(groups)
    ]
    far_terms = jnp.stack(spread(by_step))
    from_col, far_terms, row_terms = lax.optimization_barrier((from_col, far_terms, row_terms))
    back = swap(far_terms, groups)
    token = hold(back)
    joined = join(row_terms, from_col)
    out = exchange_near(joined.reshape(groups, subs, 3, cols, near_feats))
    return unpack(scal, out, back, token, tokens, feats)


def solution(mesh):
    placed = P(("wide", "narrow"), None)
    return jax.shard_map(
        body,
        mesh=mesh,
        in_specs=(placed,) * 4 + (P(), P()),
        out_specs=(placed,) * 3,
        check_vma=False,
    )
```

```python
import math

import jax
import jax.numpy as jnp
from jax import lax
from jax.experimental import pallas as pl
from jax.experimental.pallas import tpu as pltpu
from jax.sharding import PartitionSpec as P

HEAD = 128
CB = 128
HALVES = 2
VMEM_BYTES = 16 * 1024 * 1024
PACK_BYTES = 60 * 1024 * 1024

masked_low = -1e30
least_max = -1e29
score_scale = 1.0 / math.sqrt(HEAD)
f32 = jnp.float32
bf16 = jnp.bfloat16
QI, GI, KI, VI = 2, 3, 0, 1


def dot_nt(a, b):
    return lax.dot_general(a, b, (((1,), (1,)), ((), ())), preferred_element_type=f32)


def dot_nn(a, b):
    return lax.dot_general(a, b, (((1,), (0,)), ((), ())), preferred_element_type=f32)


def params(n_axes=1):
    return pltpu.CompilerParams(
        dimension_semantics=("arbitrary",) * n_axes, vmem_limit_bytes=VMEM_BYTES
    )


def cost(units):
    return pl.CostEstimate(
        flops=units * 10 * 512 * 512 * 128, bytes_accessed=4 << 20, transcendentals=units * 512 * 512
    )


def pack_body(k_ref, v_ref, q_ref, g_ref, far_a_ref, far_b_ref, out_ref, near_sem, far_sem):
    groups, feats, far_feats = out_ref.shape[0], out_ref.shape[-1], far_a_ref.shape[-1]
    lower = lax.axis_index("narrow") < groups

    def far_copies(pair, first):
        for ref, far_ref in zip(pair, (far_a_ref, far_b_ref)):
            for j in range(groups):
                src = ref.at[:, :, pl.ds(j * feats + first, far_feats)]
                yield pltpu.make_async_copy(src, far_ref.at[j], far_sem)

    def near_copies():
        for j in range(groups):
            for a, ref in enumerate((k_ref, v_ref, q_ref, g_ref)):
                src = ref.at[:, :, pl.ds(j * feats, feats)]
                yield pltpu.make_async_copy(src, out_ref.at[j, :, a], near_sem)

    @pl.when(lower)
    def _():
        for copy in far_copies((k_ref, v_ref), far_feats):
            copy.start()

    @pl.when(jnp.logical_not(lower))
    def _():
        for copy in far_copies((q_ref, g_ref), 0):
            copy.start()

    for copy in near_copies():
        copy.start()
    for copy in far_copies((k_ref, v_ref), 0):
        copy.wait()
    for copy in near_copies():
        copy.wait()


def pack(k, v, q, g, groups, subs, cols):
    near_feats = k.shape[1] // groups
    far = (subs, cols, near_feats // HALVES)
    shapes = [far, far, (subs, 4, cols, near_feats)]
    split = [a.reshape(subs, cols, a.shape[1]) for a in (k, v, q, g)]
    return pl.pallas_call(
        pack_body,
        in_specs=[pl.BlockSpec(memory_space=pltpu.HBM)] * 4,
        out_specs=[pl.BlockSpec(memory_space=pltpu.VMEM)] * 3,
        out_shape=[jax.ShapeDtypeStruct((groups, *shape), bf16) for shape in shapes],
        scratch_shapes=[pltpu.SemaphoreType.DMA, pltpu.SemaphoreType.DMA],
        compiler_params=pltpu.CompilerParams(vmem_limit_bytes=PACK_BYTES),
        name="pack",
    )(*split)


STATS_STEP = 128
GRADS_STEP = 256
LONG = pl.CostEstimate(flops=200_000_000_000, bytes_accessed=400 << 20, transcendentals=0)


def hold_body(in_ref, out_ref):
    out_ref[...] = jnp.zeros_like(out_ref)


def hold(arr):
    return pl.pallas_call(
        hold_body,
        in_specs=[pl.BlockSpec(memory_space=pl.ANY)],
        out_specs=pl.BlockSpec(memory_space=pltpu.VMEM),
        out_shape=jax.ShapeDtypeStruct((8, 128), f32),
        compiler_params=pltpu.CompilerParams(vmem_limit_bytes=1024 * 1024),
        cost_estimate=LONG,
        name="hold",
    )(arr)


def split_body(a_ref, b_ref, token_ref, *out_refs):
    groups = len(out_refs)
    near = lax.rem(lax.axis_index("narrow"), groups)
    for step, ref in enumerate(out_refs):
        for i, far_ref in enumerate((a_ref, b_ref)):
            ref[:, i] = far_ref[near ^ step]


def split(far_a, far_b, token):
    groups, subs, cols, feats = far_a.shape
    whole = pl.BlockSpec(memory_space=pltpu.VMEM)
    return pl.pallas_call(
        split_body,
        in_specs=[whole] * 2 + [pl.BlockSpec(memory_space=pl.ANY)],
        out_specs=[whole] * groups,
        out_shape=[jax.ShapeDtypeStruct((subs, 2, cols, feats), bf16)] * groups,
        compiler_params=pltpu.CompilerParams(vmem_limit_bytes=VMEM_BYTES),
        cost_estimate=LONG,
        name="split",
    )(far_a, far_b, token)


def unpack_body(scal_ref, in_ref, far_ref, token_ref, q_ref, k_ref, v_ref):
    members, subs, _, cols, feats = in_ref.shape
    far_feats = far_ref.shape[-1]
    for i in range(members):
        for a, ref in enumerate((q_ref, k_ref, v_ref)):
            for s in range(subs):
                ref[s * cols : (s + 1) * cols, i * feats : (i + 1) * feats] = in_ref[i, s, a]

    def add(ref, i, a, first):
        place = (pl.program_id(0) * members + i) ^ scal_ref[3]
        feat_cols = slice(i * feats + first, i * feats + first + far_feats)
        total = ref[:, feat_cols].astype(f32) + far_ref[place, a].astype(f32)
        ref[:, feat_cols] = total.astype(bf16)

    @pl.when(scal_ref[0] == 0)
    def _():
        for i in range(members):
            add(k_ref, i, 0, far_feats)
            add(v_ref, i, 1, far_feats)

    @pl.when(scal_ref[0] != 0)
    def _():
        for i in range(members):
            add(q_ref, i, 0, 0)


def unpack(scal, arr, far, token, tokens, feats):
    groups, subs, _, cols, near_feats = arr.shape
    members = 2
    out = jax.ShapeDtypeStruct((tokens, feats), bf16)
    return pl.pallas_call(
        unpack_body,
        grid=(groups // members,),
        in_specs=[
            smem(),
            pl.BlockSpec((members, subs, 3, cols, near_feats), lambda j: (j, 0, 0, 0, 0)),
            pl.BlockSpec(far.shape, lambda j: (0, 0, 0, 0)),
            pl.BlockSpec(memory_space=pl.ANY),
        ],
        out_specs=[pl.BlockSpec((tokens, members * near_feats), lambda j: (0, j))] * 3,
        out_shape=[out] * 3,
        compiler_params=params(),
        name="unpack",
    )(scal, arr, far, token)


def flat(ref, index):
    block = ref[:, index]
    return block.reshape(block.shape[0] * block.shape[1], block.shape[2])


def row_mask(scal_ref, n):
    first = scal_ref[1] - scal_ref[0] * n
    u = lax.broadcasted_iota(jnp.int32, (n, n), 0)
    t = lax.broadcasted_iota(jnp.int32, (n, n), 1)
    return (u == t) | ((u < t) & (u >= first))


def off_mask(scal_ref, n):
    return lax.broadcasted_iota(jnp.int32, (n, n), 0) >= scal_ref[1]


def col_mask(scal_ref, n, cols):
    u = lax.broadcasted_iota(jnp.int32, (n, n), 0)
    t = lax.broadcasted_iota(jnp.int32, (n, n), 1)
    same = (u & (cols - 1)) == (t & (cols - 1))
    return same & (u < t) & (u >= scal_ref[2] * cols)


def fill_bias(bias_ref, mask):
    @pl.when(pl.program_id(0) == 0)
    def _():
        bias_ref[...] = jnp.where(mask(bias_ref.shape[0]), 0.0, masked_low)


def partial_stats(k, v, q, g, bias, scale):
    s = dot_nt(k, q) * scale + bias
    m = jnp.maximum(jnp.max(s, axis=0, keepdims=True), least_max)
    e = jnp.exp2(s - m)
    total = jnp.sum(e, axis=0, keepdims=True)
    weighted = jnp.sum(e * dot_nt(v, g), axis=0, keepdims=True)
    some = total > 0.0
    total = jnp.where(some, total, 1.0)
    return jnp.where(some, m + jnp.log2(total), masked_low), weighted / total


def merge(lse_a, delta_a, lse_b, delta_b):
    top = jnp.maximum(lse_a, lse_b)
    a = jnp.exp2(lse_a - top)
    b = jnp.exp2(lse_b - top)
    total = a + b
    return top + jnp.log2(total), (a * delta_a + b * delta_b) / total


def row_stats_body(scale, scal_ref, t_ref, out_ref, bias_ref):
    fill_bias(bias_ref, lambda n: row_mask(scal_ref, n))
    k, v, q, g = (flat(t_ref, i) for i in range(4))
    lse, delta = partial_stats(k, v, q, g, bias_ref[...], scale)
    out_ref[0, 0:1] = lse
    out_ref[0, 1:2] = delta


def gather_far(scal_ref, piece_refs, buf):
    for i, ref in enumerate(piece_refs):
        for a in range(2):
            buf[a, scal_ref[3] ^ i] = flat(ref, a)
    return (buf[a].reshape(buf.shape[1] * buf.shape[2], HEAD) for a in range(2))


def off_stats_body(scale, scal_ref, t_ref, *refs):
    *piece_refs, out_ref, buf, bias_ref = refs
    fill_bias(bias_ref, lambda n: off_mask(scal_ref, n))
    far_a, far_b = gather_far(scal_ref, piece_refs, buf)

    def run(k, v, q, g):
        lse, delta = partial_stats(k, v, q, g, bias_ref[...], scale)
        out_ref[0, 0:1] = lse
        out_ref[0, 1:2] = delta

    @pl.when(scal_ref[0] == 0)
    def _():
        run(flat(t_ref, KI), flat(t_ref, VI), far_a, far_b)

    @pl.when(scal_ref[0] != 0)
    def _():
        run(far_a, far_b, flat(t_ref, QI), flat(t_ref, GI))


def head_slices(ref, head):
    feats = slice(head * HEAD, (head + 1) * HEAD)
    blocks = (ref[:, i, :, feats] for i in range(ref.shape[1]))
    return (b.reshape(b.shape[0] * b.shape[1], HEAD) for b in blocks)


def col_stats_body(scale, scal_ref, t_ref, out_ref):
    rows, _, cols, _ = t_ref.shape
    bias = jnp.where(col_mask(scal_ref, rows * cols, cols), 0.0, masked_low)
    for head in range(out_ref.shape[0]):
        k, v, q, g = head_slices(t_ref, head)
        for start in range(0, rows * cols, STATS_STEP):
            part, upto = slice(start, start + STATS_STEP), slice(0, start + STATS_STEP)
            lse, delta = partial_stats(k[upto], v[upto], q[part], g[part], bias[upto, part], scale)
            out_ref[head, 0:1, part] = lse
            out_ref[head, 1:2, part] = delta


def col_stats(scale, scal, t):
    rows, _, cols, feats = t.shape
    whole = pl.BlockSpec(memory_space=pltpu.VMEM)
    return pl.pallas_call(
        lambda *refs: col_stats_body(scale, *refs),
        in_specs=[smem(), whole],
        out_specs=whole,
        out_shape=jax.ShapeDtypeStruct((feats // HEAD, 2, rows * cols), f32),
        compiler_params=pltpu.CompilerParams(vmem_limit_bytes=VMEM_BYTES),
        cost_estimate=cost(4),
        name="col_stats",
    )(scal, t)


def smem():
    return pl.BlockSpec(memory_space=pltpu.SMEM)


def head_block(arr):
    a, b, c, _ = arr.shape
    return pl.BlockSpec((a, b, c, HEAD), lambda h: (0, 0, 0, h))


def off_block(arr, heads):
    a, b, c, _ = arr.shape
    return pl.BlockSpec((a, b, c, HEAD), lambda h, scal_ref: (0, 0, 0, h + scal_ref[0] * heads))


def off_call(body, scale, scal, t, extra, extra_specs, pieces, out_specs, out_shape, units, name):
    heads = pieces[0].shape[3] // HEAD
    tokens = pieces[0].shape[0] * pieces[0].shape[2]
    rows, _, cols, _ = t.shape
    stat_spec = pl.BlockSpec((1, 2, rows * cols), lambda h, scal_ref: (h, 0, 0))
    piece_specs = [
        pl.BlockSpec((*p.shape[:3], HEAD), lambda h, scal_ref: (0, 0, 0, h)) for p in pieces
    ]
    return pl.pallas_call(
        lambda *refs: body(scale, *refs),
        grid_spec=pltpu.PrefetchScalarGridSpec(
            num_scalar_prefetch=1,
            grid=(heads,),
            in_specs=[off_block(t, heads)] + [spec or stat_spec for spec in extra_specs] + piece_specs,
            out_specs=out_specs,
            scratch_shapes=[
                pltpu.VMEM((2, len(pieces), tokens, HEAD), bf16),
                pltpu.VMEM((rows * cols, rows * cols), f32),
            ],
        ),
        out_shape=out_shape,
        compiler_params=params(),
        cost_estimate=cost(units),
        name=name,
    )(scal, t, *extra, *pieces)


def off_stats(scale, scal, t, pieces):
    heads = pieces[0].shape[3] // HEAD
    n = t.shape[0] * t.shape[2]
    return off_call(
        off_stats_body, scale, scal, t, (), (), pieces,
        pl.BlockSpec((1, 2, n), lambda h, scal_ref: (h, 0, 0)),
        jax.ShapeDtypeStruct((heads, 2, n), f32), 2, "off_stats",
    )


def off_grads_body(scale, scal_ref, t_ref, stat_ref, token_ref, *refs):
    *piece_refs, near_ref, far_ref, buf, bias_ref = refs
    fill_bias(bias_ref, lambda n: off_mask(scal_ref, n))
    far_a, far_b = gather_far(scal_ref, piece_refs, buf)
    lse, delta = stat_ref[0, 0:1], stat_ref[0, 1:2]

    def run(k, v, q, g):
        return block_grads(k, v, q, g, bias_ref[...], lse, delta, scale)

    @pl.when(scal_ref[0] == 0)
    def _():
        dq, dk, dv = run(flat(t_ref, KI), flat(t_ref, VI), far_a, far_b)
        near_ref[0] = dk
        near_ref[1] = dv
        far_ref[:, 0] = dq.astype(bf16).reshape(far_ref.shape[0], far_ref.shape[2], HEAD)

    @pl.when(scal_ref[0] != 0)
    def _():
        dq, dk, dv = run(far_a, far_b, flat(t_ref, QI), flat(t_ref, GI))
        near_ref[0] = dq
        for a, d in enumerate((dk, dv)):
            far_ref[:, a] = d.astype(bf16).reshape(far_ref.shape[0], far_ref.shape[2], HEAD)


def off_grads(scale, scal, t, stats, token, pieces):
    n = t.shape[0] * t.shape[2]
    feats = pieces[0].shape[3]
    far_shape = (len(pieces), 2, n // len(pieces), feats)
    return off_call(
        off_grads_body, scale, scal, t, (stats, token),
        (None, pl.BlockSpec(memory_space=pl.ANY)), pieces,
        [
            pl.BlockSpec((2, n, HEAD), lambda h, scal_ref: (0, 0, h)),
            pl.BlockSpec((*far_shape[:3], HEAD), lambda h, scal_ref: (0, 0, 0, h)),
        ],
        [jax.ShapeDtypeStruct((2, n, feats), f32), jax.ShapeDtypeStruct(far_shape, bf16)],
        5,
        "off_grads",
    )


def stats_call(body, scale, scal, arrays, name, units):
    heads = arrays[0].shape[3] // HEAD
    n = arrays[0].shape[0] * arrays[0].shape[2]
    return pl.pallas_call(
        lambda *refs: body(scale, *refs),
        grid=(heads,),
        in_specs=[smem()] + [head_block(a) for a in arrays],
        out_specs=pl.BlockSpec((1, 2, n), lambda h: (h, 0, 0)),
        out_shape=jax.ShapeDtypeStruct((heads, 2, n), f32),
        scratch_shapes=[pltpu.VMEM((n, n), f32)],
        compiler_params=params(),
        cost_estimate=cost(units),
        name=name,
    )(scal, *arrays)


def block_grads(k, v, q, g, bias, lse, delta, scale):
    p = jnp.exp2(dot_nt(k, q) * scale + (bias - lse))
    ds = (p * (dot_nt(v, g) - delta)).astype(bf16)
    dv = dot_nn(p.astype(bf16), g)
    dk = dot_nn(ds, q) * score_scale
    dq = dot_nn(k.T, ds).T * score_scale
    return dq, dk, dv


def row_grads_body(scale, scal_ref, t_ref, stat_ref, off_ref, out_ref, sum_ref, bias_ref):
    fill_bias(bias_ref, lambda n: row_mask(scal_ref, n))
    k, v, q, g = (flat(t_ref, i) for i in range(4))
    grads = block_grads(k, v, q, g, bias_ref[...], stat_ref[0, 0:1], stat_ref[0, 1:2], scale)
    upper = scal_ref[0] != 0
    has_off = (pl.program_id(0) >= pl.num_programs(0) // HALVES) == upper
    for a, d in enumerate(grads):
        sum_ref[a] = d

    @pl.when(has_off & upper)
    def _():
        sum_ref[0] += off_ref[0]

    @pl.when(has_off & jnp.logical_not(upper))
    def _():
        sum_ref[1] += off_ref[0]
        sum_ref[2] += off_ref[1]

    for a in range(3):
        out_ref[:, a] = sum_ref[a].astype(bf16).reshape(out_ref.shape[0], out_ref.shape[2], HEAD)


def col_grads_body(scale, scal_ref, t_ref, own_ref, got_ref, out_ref):
    rows, _, cols, _ = t_ref.shape
    bias = jnp.where(col_mask(scal_ref, rows * cols, cols), 0.0, masked_low)
    for head in range(own_ref.shape[0]):
        k, v, q, g = head_slices(t_ref, head)
        lse, delta = merge(
            own_ref[head, 0:1], own_ref[head, 1:2], got_ref[head, 0:1], got_ref[head, 1:2]
        )
        feats = slice(head * HEAD, (head + 1) * HEAD)

        def put(a, part, d):
            rows_here = slice(part.start // cols, part.stop // cols)
            out_ref[rows_here, a, :, feats] = d.astype(bf16).reshape(-1, cols, HEAD)

        n = rows * cols
        dk_sum = dv_sum = None
        for stop in range(n, 0, -GRADS_STEP):
            part, upto = slice(stop - GRADS_STEP, stop), slice(0, stop)
            dq, dk, dv = block_grads(
                k[upto], v[upto], q[part], g[part], bias[upto, part], lse[:, part], delta[:, part], scale
            )
            dk_sum = dk if dk_sum is None else dk_sum[upto] + dk
            dv_sum = dv if dv_sum is None else dv_sum[upto] + dv
            put(0, part, dq)
            put(1, part, dk_sum[part])
            put(2, part, dv_sum[part])


def row_grads(scale, scal, t, stats, off):
    rows, _, cols, feats = t.shape
    n = rows * cols
    near_heads = off.shape[2] // HEAD
    return pl.pallas_call(
        lambda *refs: row_grads_body(scale, *refs),
        grid=(feats // HEAD,),
        in_specs=[
            smem(),
            head_block(t),
            pl.BlockSpec((1, 2, n), lambda h: (h, 0, 0)),
            pl.BlockSpec((2, n, HEAD), lambda h: (0, 0, h % near_heads)),
        ],
        out_specs=pl.BlockSpec((rows, 3, cols, HEAD), lambda h: (0, 0, 0, h)),
        out_shape=jax.ShapeDtypeStruct((rows, 3, cols, feats), bf16),
        scratch_shapes=[pltpu.VMEM((3, n, HEAD), f32), pltpu.VMEM((n, n), f32)],
        compiler_params=params(),
        cost_estimate=cost(8),
        name="row_grads",
    )(scal, t, stats, off)


def col_grads(scale, scal, t, own, got):
    rows, _, cols, feats = t.shape
    whole = pl.BlockSpec(memory_space=pltpu.VMEM)
    return pl.pallas_call(
        lambda *refs: col_grads_body(scale, *refs),
        in_specs=[smem(), whole, whole, whole],
        out_specs=whole,
        out_shape=jax.ShapeDtypeStruct((rows, 3, cols, feats), bf16),
        compiler_params=pltpu.CompilerParams(vmem_limit_bytes=VMEM_BYTES),
        cost_estimate=cost(8),
        name="col_grads",
    )(scal, t, own, got)


def join_body(row_ref, col_ref, out_ref):
    out_ref[...] = (row_ref[...].astype(f32) + col_ref[...].astype(f32)).astype(bf16)


def join(row, col):
    rows, arrays, cols, feats = col.shape
    steps = 4
    spec = pl.BlockSpec((rows // steps, arrays, cols, feats), lambda i: (i, 0, 0, 0))
    return pl.pallas_call(
        join_body,
        grid=(steps,),
        in_specs=[spec, spec],
        out_specs=spec,
        out_shape=jax.ShapeDtypeStruct(col.shape, bf16),
        compiler_params=params(),
        name="join",
    )(row, col)


def body(query_in, key_in, value_in, grad_out, row_start, col_start):
    scale = score_scale * math.log2(math.e)
    tokens, feats = query_in.shape
    lanes = lax.axis_size("wide")
    narrow = lax.axis_size("narrow")
    groups = narrow // HALVES
    half_cols = tokens * groups
    cols = half_cols // lanes
    subs = tokens // cols
    near = [[half * groups + j for j in range(groups)] for half in range(HALVES)]

    def exchange_near(arr):
        return lax.all_to_all(
            arr, "narrow", split_axis=0, concat_axis=0, axis_index_groups=near, tiled=True
        )

    def exchange_wide(arr):
        return lax.all_to_all(arr, "wide", split_axis=0, concat_axis=0, tiled=True)

    def shift(arr, source, target):
        pairs = [(source * groups + j, target * groups + j) for j in range(groups)]
        return lax.ppermute(arr, "narrow", pairs)

    def swap(arr, step):
        pairs = [(i, i ^ step) for i in range(narrow)]
        return lax.ppermute(arr, "narrow", pairs)

    def spread(pieces):
        return [swap(piece, step) if step else piece for step, piece in enumerate(pieces)]

    wide_index = lax.axis_index("wide")
    narrow_index = lax.axis_index("narrow")
    half = narrow_index // groups
    near_index = narrow_index % groups
    first_col = lax.dynamic_index_in_dim(row_start, wide_index, keepdims=False)
    block_id = (half * half_cols + wide_index * cols) // CB
    first_row = lax.dynamic_index_in_dim(col_start, block_id, keepdims=False)
    scal = jnp.stack([half, first_col, first_row, near_index]).astype(jnp.int32)

    far_a, far_b, packed = pack(key_in, value_in, query_in, grad_out, groups, subs, cols)
    near_feats = feats // groups
    heads = near_feats // HEAD
    near_heads = heads // HALVES
    far_a = swap(far_a, groups)
    token = hold(far_a)
    far_b = swap(far_b, groups)
    t = exchange_near(packed).reshape(lanes, 4, cols, near_feats)
    t, token = lax.optimization_barrier((t, token))
    by_col = exchange_wide(t)
    pieces = spread(split(far_a, far_b, token))
    diag_part = stats_call(row_stats_body, scale, scal, (t,), "row_stats", 4)
    own_off = off_stats(scale, scal, t, pieces)
    off_part = jnp.concatenate([shift(own_off, 0, 1), own_off])
    lse, delta = merge(diag_part[:, 0], diag_part[:, 1], off_part[:, 0], off_part[:, 1])
    row_part = jnp.where(half == 1, jnp.stack([lse, delta], axis=1), diag_part)
    col_part = col_stats(scale, scal, by_col)

    both = jnp.stack([row_part, col_part]).reshape(4 * heads, lanes, cols)
    sent = both.transpose(1, 0, 2).reshape(lanes, (4 * heads * cols) // HEAD, HEAD)
    got = exchange_wide(sent).reshape(lanes, 4 * heads, cols).transpose(1, 0, 2)
    got = got.reshape(2, heads, 2, lanes * cols)
    row_lse, row_delta = merge(row_part[:, 0], row_part[:, 1], got[1, :, 0], got[1, :, 1])
    row_full = jnp.stack([row_lse, row_delta], axis=1)

    far_full = shift(row_full[:near_heads], 1, 0)
    token = hold(far_full)
    from_col = exchange_wide(col_grads(scale, scal, by_col, col_part, got[0]))
    off_full = jnp.where(half == 1, row_full[near_heads:], far_full)
    off_terms, far_terms = off_grads(scale, scal, t, off_full, token, pieces)
    row_terms = row_grads(scale, scal, t, row_full, off_terms)
    by_step = [
        lax.dynamic_index_in_dim(far_terms, near_index ^ step, keepdims=False)
        for step in range(groups)
    ]
    far_terms = jnp.stack(spread(by_step))
    from_col, far_terms, row_terms = lax.optimization_barrier((from_col, far_terms, row_terms))
    back = swap(far_terms, groups)
    token = hold(back)
    joined = join(row_terms, from_col)
    out = exchange_near(joined.reshape(groups, subs, 3, cols, near_feats))
    return unpack(scal, out, back, token, tokens, feats)


def solution(mesh):
    placed = P(("wide", "narrow"), None)
    return jax.shard_map(
        body,
        mesh=mesh,
        in_specs=(placed,) * 4 + (P(), P()),
        out_specs=(placed,) * 3,
        check_vma=False,
    )
```

```python
import math

import jax
import jax.numpy as jnp
from jax import lax
from jax.experimental import pallas as pl
from jax.experimental.pallas import tpu as pltpu
from jax.sharding import PartitionSpec as P

HEAD = 128
CB = 128
HALVES = 2
FIRST_SUBS = 1
FIRST_UNITS, SPLIT_UNITS, FULL_UNITS, BACK_UNITS = 40, 100, 40, 40
VMEM_BYTES = 16 * 1024 * 1024
PACK_BYTES = 60 * 1024 * 1024

masked_low = -1e30
least_max = -1e29
score_scale = 1.0 / math.sqrt(HEAD)
f32 = jnp.float32
bf16 = jnp.bfloat16
QI, GI, KI, VI = 2, 3, 0, 1


def dot_nt(a, b):
    return lax.dot_general(a, b, (((1,), (1,)), ((), ())), preferred_element_type=f32)


def dot_nn(a, b):
    return lax.dot_general(a, b, (((1,), (0,)), ((), ())), preferred_element_type=f32)


def params(n_axes=1):
    return pltpu.CompilerParams(
        dimension_semantics=("arbitrary",) * n_axes, vmem_limit_bytes=VMEM_BYTES
    )


def cost(units):
    return pl.CostEstimate(
        flops=units * 10 * 512 * 512 * 128, bytes_accessed=4 << 20, transcendentals=units * 512 * 512
    )


def pack_body(k_ref, v_ref, q_ref, g_ref, first_ref, second_ref, out_ref, near_sem, far_sem):
    groups, feats, far_feats = out_ref.shape[0], out_ref.shape[-1], first_ref.shape[-1]
    cut = first_ref.shape[1]
    lower = lax.axis_index("narrow") < groups

    def far_copies(pair, first):
        for a, ref in enumerate(pair):
            for j in range(groups):
                lanes = pl.ds(j * feats + first, far_feats)
                src = ref.at[:cut, :, lanes]
                yield pltpu.make_async_copy(src, first_ref.at[j, :, a], far_sem)
                src = ref.at[cut:, :, lanes]
                yield pltpu.make_async_copy(src, second_ref.at[j, :, a], far_sem)

    def near_copies():
        for j in range(groups):
            for a, ref in enumerate((k_ref, v_ref, q_ref, g_ref)):
                src = ref.at[:, :, pl.ds(j * feats, feats)]
                yield pltpu.make_async_copy(src, out_ref.at[j, :, a], near_sem)

    @pl.when(lower)
    def _():
        for copy in far_copies((k_ref, v_ref), far_feats):
            copy.start()

    @pl.when(jnp.logical_not(lower))
    def _():
        for copy in far_copies((q_ref, g_ref), 0):
            copy.start()

    for copy in near_copies():
        copy.start()
    for copy in far_copies((k_ref, v_ref), 0):
        copy.wait()
    for copy in near_copies():
        copy.wait()


def pack(k, v, q, g, groups, subs, cols):
    near_feats = k.shape[1] // groups
    far_feats = near_feats // HALVES
    shapes = [
        (FIRST_SUBS, 2, cols, far_feats),
        (subs - FIRST_SUBS, 2, cols, far_feats),
        (subs, 4, cols, near_feats),
    ]
    split = [a.reshape(subs, cols, a.shape[1]) for a in (k, v, q, g)]
    return pl.pallas_call(
        pack_body,
        in_specs=[pl.BlockSpec(memory_space=pltpu.HBM)] * 4,
        out_specs=[pl.BlockSpec(memory_space=pltpu.VMEM)] * 3,
        out_shape=[jax.ShapeDtypeStruct((groups, *shape), bf16) for shape in shapes],
        scratch_shapes=[pltpu.SemaphoreType.DMA, pltpu.SemaphoreType.DMA],
        compiler_params=pltpu.CompilerParams(vmem_limit_bytes=PACK_BYTES),
        name="pack",
    )(*split)


STATS_STEP = 128
GRADS_STEP = 256
def long(units):
    return pl.CostEstimate(flops=units * 10**9, bytes_accessed=units << 21, transcendentals=0)


def hold_body(in_ref, out_ref):
    out_ref[...] = jnp.zeros_like(out_ref)


def hold(arr, units):
    return pl.pallas_call(
        hold_body,
        in_specs=[pl.BlockSpec(memory_space=pl.ANY)],
        out_specs=pl.BlockSpec(memory_space=pltpu.VMEM),
        out_shape=jax.ShapeDtypeStruct((8, 128), f32),
        compiler_params=pltpu.CompilerParams(vmem_limit_bytes=1024 * 1024),
        cost_estimate=long(units),
        name="hold",
    )(arr)


def split_body(first_ref, second_ref, token_ref, *out_refs):
    groups = len(out_refs)
    near = lax.rem(lax.axis_index("narrow"), groups)
    for step, ref in enumerate(out_refs):
        cut = first_ref.shape[1]
        ref[:cut] = first_ref[near ^ step]
        ref[cut:] = second_ref[near ^ step]


def split(first, second, token):
    groups, _, arrays, cols, feats = first.shape
    subs = first.shape[1] + second.shape[1]
    whole = pl.BlockSpec(memory_space=pltpu.VMEM)
    return pl.pallas_call(
        split_body,
        in_specs=[whole, whole, pl.BlockSpec(memory_space=pl.ANY)],
        out_specs=[whole] * groups,
        out_shape=[jax.ShapeDtypeStruct((subs, arrays, cols, feats), bf16)] * groups,
        compiler_params=pltpu.CompilerParams(vmem_limit_bytes=VMEM_BYTES),
        cost_estimate=long(SPLIT_UNITS),
        name="split",
    )(first, second, token)


def unpack_body(scal_ref, in_ref, far_ref, token_ref, q_ref, k_ref, v_ref):
    members, subs, _, cols, feats = in_ref.shape
    far_feats = far_ref.shape[-1]
    for i in range(members):
        for a, ref in enumerate((q_ref, k_ref, v_ref)):
            for s in range(subs):
                ref[s * cols : (s + 1) * cols, i * feats : (i + 1) * feats] = in_ref[i, s, a]

    def add(ref, i, a, first):
        place = (pl.program_id(0) * members + i) ^ scal_ref[3]
        feat_cols = slice(i * feats + first, i * feats + first + far_feats)
        total = ref[:, feat_cols].astype(f32) + far_ref[place, a].astype(f32)
        ref[:, feat_cols] = total.astype(bf16)

    @pl.when(scal_ref[0] == 0)
    def _():
        for i in range(members):
            add(k_ref, i, 0, far_feats)
            add(v_ref, i, 1, far_feats)

    @pl.when(scal_ref[0] != 0)
    def _():
        for i in range(members):
            add(q_ref, i, 0, 0)


def unpack(scal, arr, far, token, tokens, feats):
    groups, subs, _, cols, near_feats = arr.shape
    members = 2
    out = jax.ShapeDtypeStruct((tokens, feats), bf16)
    return pl.pallas_call(
        unpack_body,
        grid=(groups // members,),
        in_specs=[
            smem(),
            pl.BlockSpec((members, subs, 3, cols, near_feats), lambda j: (j, 0, 0, 0, 0)),
            pl.BlockSpec(far.shape, lambda j: (0, 0, 0, 0)),
            pl.BlockSpec(memory_space=pl.ANY),
        ],
        out_specs=[pl.BlockSpec((tokens, members * near_feats), lambda j: (0, j))] * 3,
        out_shape=[out] * 3,
        compiler_params=params(),
        name="unpack",
    )(scal, arr, far, token)


def flat(ref, index):
    block = ref[:, index]
    return block.reshape(block.shape[0] * block.shape[1], block.shape[2])


def row_mask(scal_ref, n):
    first = scal_ref[1] - scal_ref[0] * n
    u = lax.broadcasted_iota(jnp.int32, (n, n), 0)
    t = lax.broadcasted_iota(jnp.int32, (n, n), 1)
    return (u == t) | ((u < t) & (u >= first))


def off_mask(scal_ref, n):
    return lax.broadcasted_iota(jnp.int32, (n, n), 0) >= scal_ref[1]


def col_mask(scal_ref, n, cols):
    u = lax.broadcasted_iota(jnp.int32, (n, n), 0)
    t = lax.broadcasted_iota(jnp.int32, (n, n), 1)
    same = (u & (cols - 1)) == (t & (cols - 1))
    return same & (u < t) & (u >= scal_ref[2] * cols)


def fill_bias(bias_ref, mask):
    @pl.when(pl.program_id(0) == 0)
    def _():
        bias_ref[...] = jnp.where(mask(bias_ref.shape[0]), 0.0, masked_low)


def partial_stats(k, v, q, g, bias, scale):
    s = dot_nt(k, q) * scale + bias
    m = jnp.maximum(jnp.max(s, axis=0, keepdims=True), least_max)
    e = jnp.exp2(s - m)
    total = jnp.sum(e, axis=0, keepdims=True)
    weighted = jnp.sum(e * dot_nt(v, g), axis=0, keepdims=True)
    some = total > 0.0
    total = jnp.where(some, total, 1.0)
    return jnp.where(some, m + jnp.log2(total), masked_low), weighted / total


def merge(lse_a, delta_a, lse_b, delta_b):
    top = jnp.maximum(lse_a, lse_b)
    a = jnp.exp2(lse_a - top)
    b = jnp.exp2(lse_b - top)
    total = a + b
    return top + jnp.log2(total), (a * delta_a + b * delta_b) / total


def row_stats_body(scale, scal_ref, t_ref, out_ref, bias_ref):
    fill_bias(bias_ref, lambda n: row_mask(scal_ref, n))
    k, v, q, g = (flat(t_ref, i) for i in range(4))
    lse, delta = partial_stats(k, v, q, g, bias_ref[...], scale)
    out_ref[0, 0:1] = lse
    out_ref[0, 1:2] = delta


def gather_far(scal_ref, piece_refs, buf):
    for i, ref in enumerate(piece_refs):
        for a in range(2):
            buf[a, scal_ref[3] ^ i] = flat(ref, a)
    return (buf[a].reshape(buf.shape[1] * buf.shape[2], HEAD) for a in range(2))


def off_stats_body(scale, scal_ref, t_ref, *refs):
    *piece_refs, out_ref, buf, bias_ref = refs
    fill_bias(bias_ref, lambda n: off_mask(scal_ref, n))
    far_a, far_b = gather_far(scal_ref, piece_refs, buf)

    def run(k, v, q, g):
        lse, delta = partial_stats(k, v, q, g, bias_ref[...], scale)
        out_ref[0, 0:1] = lse
        out_ref[0, 1:2] = delta

    @pl.when(scal_ref[0] == 0)
    def _():
        run(flat(t_ref, KI), flat(t_ref, VI), far_a, far_b)

    @pl.when(scal_ref[0] != 0)
    def _():
        run(far_a, far_b, flat(t_ref, QI), flat(t_ref, GI))


def head_slices(ref, head):
    feats = slice(head * HEAD, (head + 1) * HEAD)
    blocks = (ref[:, i, :, feats] for i in range(ref.shape[1]))
    return (b.reshape(b.shape[0] * b.shape[1], HEAD) for b in blocks)


def col_stats_body(scale, scal_ref, t_ref, out_ref):
    rows, _, cols, _ = t_ref.shape
    bias = jnp.where(col_mask(scal_ref, rows * cols, cols), 0.0, masked_low)
    for head in range(out_ref.shape[0]):
        k, v, q, g = head_slices(t_ref, head)
        for start in range(0, rows * cols, STATS_STEP):
            part, upto = slice(start, start + STATS_STEP), slice(0, start + STATS_STEP)
            lse, delta = partial_stats(k[upto], v[upto], q[part], g[part], bias[upto, part], scale)
            out_ref[head, 0:1, part] = lse
            out_ref[head, 1:2, part] = delta


def col_stats(scale, scal, t):
    rows, _, cols, feats = t.shape
    whole = pl.BlockSpec(memory_space=pltpu.VMEM)
    return pl.pallas_call(
        lambda *refs: col_stats_body(scale, *refs),
        in_specs=[smem(), whole],
        out_specs=whole,
        out_shape=jax.ShapeDtypeStruct((feats // HEAD, 2, rows * cols), f32),
        compiler_params=pltpu.CompilerParams(vmem_limit_bytes=VMEM_BYTES),
        cost_estimate=cost(4),
        name="col_stats",
    )(scal, t)


def smem():
    return pl.BlockSpec(memory_space=pltpu.SMEM)


def head_block(arr):
    a, b, c, _ = arr.shape
    return pl.BlockSpec((a, b, c, HEAD), lambda h: (0, 0, 0, h))


def off_block(arr, heads):
    a, b, c, _ = arr.shape
    return pl.BlockSpec((a, b, c, HEAD), lambda h, scal_ref: (0, 0, 0, h + scal_ref[0] * heads))


def off_call(body, scale, scal, t, extra, extra_specs, pieces, out_specs, out_shape, units, name):
    heads = pieces[0].shape[3] // HEAD
    tokens = pieces[0].shape[0] * pieces[0].shape[2]
    rows, _, cols, _ = t.shape
    stat_spec = pl.BlockSpec((1, 2, rows * cols), lambda h, scal_ref: (h, 0, 0))
    piece_specs = [
        pl.BlockSpec((*p.shape[:3], HEAD), lambda h, scal_ref: (0, 0, 0, h)) for p in pieces
    ]
    return pl.pallas_call(
        lambda *refs: body(scale, *refs),
        grid_spec=pltpu.PrefetchScalarGridSpec(
            num_scalar_prefetch=1,
            grid=(heads,),
            in_specs=[off_block(t, heads)] + [spec or stat_spec for spec in extra_specs] + piece_specs,
            out_specs=out_specs,
            scratch_shapes=[
                pltpu.VMEM((2, len(pieces), tokens, HEAD), bf16),
                pltpu.VMEM((rows * cols, rows * cols), f32),
            ],
        ),
        out_shape=out_shape,
        compiler_params=params(),
        cost_estimate=cost(units),
        name=name,
    )(scal, t, *extra, *pieces)


def off_stats(scale, scal, t, pieces):
    heads = pieces[0].shape[3] // HEAD
    n = t.shape[0] * t.shape[2]
    return off_call(
        off_stats_body, scale, scal, t, (), (), pieces,
        pl.BlockSpec((1, 2, n), lambda h, scal_ref: (h, 0, 0)),
        jax.ShapeDtypeStruct((heads, 2, n), f32), 2, "off_stats",
    )


def off_grads_body(scale, scal_ref, t_ref, stat_ref, token_ref, *refs):
    *piece_refs, near_ref, far_ref, buf, bias_ref = refs
    fill_bias(bias_ref, lambda n: off_mask(scal_ref, n))
    far_a, far_b = gather_far(scal_ref, piece_refs, buf)
    lse, delta = stat_ref[0, 0:1], stat_ref[0, 1:2]

    def run(k, v, q, g):
        return block_grads(k, v, q, g, bias_ref[...], lse, delta, scale)

    @pl.when(scal_ref[0] == 0)
    def _():
        dq, dk, dv = run(flat(t_ref, KI), flat(t_ref, VI), far_a, far_b)
        near_ref[0] = dk
        near_ref[1] = dv
        far_ref[:, 0] = dq.astype(bf16).reshape(far_ref.shape[0], far_ref.shape[2], HEAD)

    @pl.when(scal_ref[0] != 0)
    def _():
        dq, dk, dv = run(far_a, far_b, flat(t_ref, QI), flat(t_ref, GI))
        near_ref[0] = dq
        for a, d in enumerate((dk, dv)):
            far_ref[:, a] = d.astype(bf16).reshape(far_ref.shape[0], far_ref.shape[2], HEAD)


def off_grads(scale, scal, t, stats, token, pieces):
    n = t.shape[0] * t.shape[2]
    feats = pieces[0].shape[3]
    far_shape = (len(pieces), 2, n // len(pieces), feats)
    return off_call(
        off_grads_body, scale, scal, t, (stats, token),
        (None, pl.BlockSpec(memory_space=pl.ANY)), pieces,
        [
            pl.BlockSpec((2, n, HEAD), lambda h, scal_ref: (0, 0, h)),
            pl.BlockSpec((*far_shape[:3], HEAD), lambda h, scal_ref: (0, 0, 0, h)),
        ],
        [jax.ShapeDtypeStruct((2, n, feats), f32), jax.ShapeDtypeStruct(far_shape, bf16)],
        5,
        "off_grads",
    )


def stats_call(body, scale, scal, arrays, name, units):
    heads = arrays[0].shape[3] // HEAD
    n = arrays[0].shape[0] * arrays[0].shape[2]
    return pl.pallas_call(
        lambda *refs: body(scale, *refs),
        grid=(heads,),
        in_specs=[smem()] + [head_block(a) for a in arrays],
        out_specs=pl.BlockSpec((1, 2, n), lambda h: (h, 0, 0)),
        out_shape=jax.ShapeDtypeStruct((heads, 2, n), f32),
        scratch_shapes=[pltpu.VMEM((n, n), f32)],
        compiler_params=params(),
        cost_estimate=cost(units),
        name=name,
    )(scal, *arrays)


def block_grads(k, v, q, g, bias, lse, delta, scale):
    p = jnp.exp2(dot_nt(k, q) * scale + (bias - lse))
    ds = (p * (dot_nt(v, g) - delta)).astype(bf16)
    dv = dot_nn(p.astype(bf16), g)
    dk = dot_nn(ds, q) * score_scale
    dq = dot_nn(k.T, ds).T * score_scale
    return dq, dk, dv


def row_grads_body(scale, scal_ref, t_ref, stat_ref, off_ref, out_ref, sum_ref, bias_ref):
    fill_bias(bias_ref, lambda n: row_mask(scal_ref, n))
    k, v, q, g = (flat(t_ref, i) for i in range(4))
    grads = block_grads(k, v, q, g, bias_ref[...], stat_ref[0, 0:1], stat_ref[0, 1:2], scale)
    upper = scal_ref[0] != 0
    has_off = (pl.program_id(0) >= pl.num_programs(0) // HALVES) == upper
    for a, d in enumerate(grads):
        sum_ref[a] = d

    @pl.when(has_off & upper)
    def _():
        sum_ref[0] += off_ref[0]

    @pl.when(has_off & jnp.logical_not(upper))
    def _():
        sum_ref[1] += off_ref[0]
        sum_ref[2] += off_ref[1]

    for a in range(3):
        out_ref[:, a] = sum_ref[a].astype(bf16).reshape(out_ref.shape[0], out_ref.shape[2], HEAD)


def col_grads_body(scale, scal_ref, t_ref, own_ref, got_ref, out_ref):
    rows, _, cols, _ = t_ref.shape
    bias = jnp.where(col_mask(scal_ref, rows * cols, cols), 0.0, masked_low)
    for head in range(own_ref.shape[0]):
        k, v, q, g = head_slices(t_ref, head)
        lse, delta = merge(
            own_ref[head, 0:1], own_ref[head, 1:2], got_ref[head, 0:1], got_ref[head, 1:2]
        )
        feats = slice(head * HEAD, (head + 1) * HEAD)

        def put(a, part, d):
            rows_here = slice(part.start // cols, part.stop // cols)
            out_ref[rows_here, a, :, feats] = d.astype(bf16).reshape(-1, cols, HEAD)

        n = rows * cols
        dk_sum = dv_sum = None
        for stop in range(n, 0, -GRADS_STEP):
            part, upto = slice(stop - GRADS_STEP, stop), slice(0, stop)
            dq, dk, dv = block_grads(
                k[upto], v[upto], q[part], g[part], bias[upto, part], lse[:, part], delta[:, part], scale
            )
            dk_sum = dk if dk_sum is None else dk_sum[upto] + dk
            dv_sum = dv if dv_sum is None else dv_sum[upto] + dv
            put(0, part, dq)
            put(1, part, dk_sum[part])
            put(2, part, dv_sum[part])


def row_grads(scale, scal, t, stats, off):
    rows, _, cols, feats = t.shape
    n = rows * cols
    near_heads = off.shape[2] // HEAD
    return pl.pallas_call(
        lambda *refs: row_grads_body(scale, *refs),
        grid=(feats // HEAD,),
        in_specs=[
            smem(),
            head_block(t),
            pl.BlockSpec((1, 2, n), lambda h: (h, 0, 0)),
            pl.BlockSpec((2, n, HEAD), lambda h: (0, 0, h % near_heads)),
        ],
        out_specs=pl.BlockSpec((rows, 3, cols, HEAD), lambda h: (0, 0, 0, h)),
        out_shape=jax.ShapeDtypeStruct((rows, 3, cols, feats), bf16),
        scratch_shapes=[pltpu.VMEM((3, n, HEAD), f32), pltpu.VMEM((n, n), f32)],
        compiler_params=params(),
        cost_estimate=cost(8),
        name="row_grads",
    )(scal, t, stats, off)


def col_grads(scale, scal, t, own, got):
    rows, _, cols, feats = t.shape
    whole = pl.BlockSpec(memory_space=pltpu.VMEM)
    return pl.pallas_call(
        lambda *refs: col_grads_body(scale, *refs),
        in_specs=[smem(), whole, whole, whole],
        out_specs=whole,
        out_shape=jax.ShapeDtypeStruct((rows, 3, cols, feats), bf16),
        compiler_params=pltpu.CompilerParams(vmem_limit_bytes=VMEM_BYTES),
        cost_estimate=cost(8),
        name="col_grads",
    )(scal, t, own, got)


def join_body(row_ref, col_ref, out_ref):
    out_ref[...] = (row_ref[...].astype(f32) + col_ref[...].astype(f32)).astype(bf16)


def join(row, col):
    rows, arrays, cols, feats = col.shape
    steps = 4
    spec = pl.BlockSpec((rows // steps, arrays, cols, feats), lambda i: (i, 0, 0, 0))
    return pl.pallas_call(
        join_body,
        grid=(steps,),
        in_specs=[spec, spec],
        out_specs=spec,
        out_shape=jax.ShapeDtypeStruct(col.shape, bf16),
        compiler_params=params(),
        name="join",
    )(row, col)


def body(query_in, key_in, value_in, grad_out, row_start, col_start):
    scale = score_scale * math.log2(math.e)
    tokens, feats = query_in.shape
    lanes = lax.axis_size("wide")
    narrow = lax.axis_size("narrow")
    groups = narrow // HALVES
    half_cols = tokens * groups
    cols = half_cols // lanes
    subs = tokens // cols
    near = [[half * groups + j for j in range(groups)] for half in range(HALVES)]

    def exchange_near(arr):
        return lax.all_to_all(
            arr, "narrow", split_axis=0, concat_axis=0, axis_index_groups=near, tiled=True
        )

    def exchange_wide(arr):
        return lax.all_to_all(arr, "wide", split_axis=0, concat_axis=0, tiled=True)

    def shift(arr, source, target):
        pairs = [(source * groups + j, target * groups + j) for j in range(groups)]
        return lax.ppermute(arr, "narrow", pairs)

    def swap(arr, step):
        pairs = [(i, i ^ step) for i in range(narrow)]
        return lax.ppermute(arr, "narrow", pairs)

    def spread(pieces):
        return [swap(piece, step) if step else piece for step, piece in enumerate(pieces)]

    wide_index = lax.axis_index("wide")
    narrow_index = lax.axis_index("narrow")
    half = narrow_index // groups
    near_index = narrow_index % groups
    first_col = lax.dynamic_index_in_dim(row_start, wide_index, keepdims=False)
    block_id = (half * half_cols + wide_index * cols) // CB
    first_row = lax.dynamic_index_in_dim(col_start, block_id, keepdims=False)
    scal = jnp.stack([half, first_col, first_row, near_index]).astype(jnp.int32)

    far_first, far_second, packed = pack(key_in, value_in, query_in, grad_out, groups, subs, cols)
    near_feats = feats // groups
    heads = near_feats // HEAD
    near_heads = heads // HALVES
    far_first = swap(far_first, groups)
    token = hold(far_first, FIRST_UNITS)
    far_second = swap(far_second, groups)
    t = exchange_near(packed).reshape(lanes, 4, cols, near_feats)
    t, token = lax.optimization_barrier((t, token))
    by_col = exchange_wide(t)
    pieces = spread(split(far_first, far_second, token))
    diag_part = stats_call(row_stats_body, scale, scal, (t,), "row_stats", 4)
    own_off = off_stats(scale, scal, t, pieces)
    off_part = jnp.concatenate([shift(own_off, 0, 1), own_off])
    lse, delta = merge(diag_part[:, 0], diag_part[:, 1], off_part[:, 0], off_part[:, 1])
    row_part = jnp.where(half == 1, jnp.stack([lse, delta], axis=1), diag_part)
    col_part = col_stats(scale, scal, by_col)

    both = jnp.stack([row_part, col_part]).reshape(4 * heads, lanes, cols)
    sent = both.transpose(1, 0, 2).reshape(lanes, (4 * heads * cols) // HEAD, HEAD)
    got = exchange_wide(sent).reshape(lanes, 4 * heads, cols).transpose(1, 0, 2)
    got = got.reshape(2, heads, 2, lanes * cols)
    row_lse, row_delta = merge(row_part[:, 0], row_part[:, 1], got[1, :, 0], got[1, :, 1])
    row_full = jnp.stack([row_lse, row_delta], axis=1)

    far_full = shift(row_full[:near_heads], 1, 0)
    token = hold(far_full, FULL_UNITS)
    from_col = exchange_wide(col_grads(scale, scal, by_col, col_part, got[0]))
    off_full = jnp.where(half == 1, row_full[near_heads:], far_full)
    off_terms, far_terms = off_grads(scale, scal, t, off_full, token, pieces)
    row_terms = row_grads(scale, scal, t, row_full, off_terms)
    by_step = [
        lax.dynamic_index_in_dim(far_terms, near_index ^ step, keepdims=False)
        for step in range(groups)
    ]
    far_terms = jnp.stack(spread(by_step))
    from_col, far_terms, row_terms = lax.optimization_barrier((from_col, far_terms, row_terms))
    back = swap(far_terms, groups)
    token = hold(back, BACK_UNITS)
    joined = join(row_terms, from_col)
    out = exchange_near(joined.reshape(groups, subs, 3, cols, near_feats))
    return unpack(scal, out, back, token, tokens, feats)


def solution(mesh):
    placed = P(("wide", "narrow"), None)
    return jax.shard_map(
        body,
        mesh=mesh,
        in_specs=(placed,) * 4 + (P(), P()),
        out_specs=(placed,) * 3,
        check_vma=False,
    )
```

```python
import math

import jax
import jax.numpy as jnp
from jax import lax
from jax.experimental import pallas as pl
from jax.experimental.pallas import tpu as pltpu
from jax.sharding import PartitionSpec as P

HEAD = 128
CB = 128
HALVES = 2
FIRST_SUBS = 1
FIRST_UNITS, SPLIT_UNITS, FULL_UNITS, BACK_UNITS = 40, 100, 40, 40
VMEM_BYTES = 16 * 1024 * 1024
PACK_BYTES = 60 * 1024 * 1024

masked_low = -1e30
least_max = -1e29
score_scale = 1.0 / math.sqrt(HEAD)
f32 = jnp.float32
bf16 = jnp.bfloat16
QI, GI, KI, VI = 2, 3, 0, 1


def dot_nt(a, b):
    return lax.dot_general(a, b, (((1,), (1,)), ((), ())), preferred_element_type=f32)


def dot_nn(a, b):
    return lax.dot_general(a, b, (((1,), (0,)), ((), ())), preferred_element_type=f32)


def params(n_axes=1):
    return pltpu.CompilerParams(
        dimension_semantics=("arbitrary",) * n_axes, vmem_limit_bytes=VMEM_BYTES
    )


def cost(units):
    return pl.CostEstimate(
        flops=units * 10 * 512 * 512 * 128, bytes_accessed=4 << 20, transcendentals=units * 512 * 512
    )


def pack_body(k_ref, v_ref, q_ref, g_ref, first_ref, second_ref, out_ref, near_sem, far_sem):
    groups, feats, far_feats = out_ref.shape[0], out_ref.shape[-1], first_ref.shape[-1]
    cut = first_ref.shape[1]
    lower = lax.axis_index("narrow") < groups

    def far_copies(pair, first):
        for a, ref in enumerate(pair):
            for j in range(groups):
                lanes = pl.ds(j * feats + first, far_feats)
                src = ref.at[:cut, :, lanes]
                yield pltpu.make_async_copy(src, first_ref.at[j, :, a], far_sem)
                src = ref.at[cut:, :, lanes]
                yield pltpu.make_async_copy(src, second_ref.at[j, :, a], far_sem)

    def near_copies():
        for j in range(groups):
            for a, ref in enumerate((k_ref, v_ref, q_ref, g_ref)):
                src = ref.at[:, :, pl.ds(j * feats, feats)]
                yield pltpu.make_async_copy(src, out_ref.at[j, :, a], near_sem)

    @pl.when(lower)
    def _():
        for copy in far_copies((k_ref, v_ref), far_feats):
            copy.start()

    @pl.when(jnp.logical_not(lower))
    def _():
        for copy in far_copies((q_ref, g_ref), 0):
            copy.start()

    for copy in near_copies():
        copy.start()
    for copy in far_copies((k_ref, v_ref), 0):
        copy.wait()
    for copy in near_copies():
        copy.wait()


def pack(k, v, q, g, groups, subs, cols):
    near_feats = k.shape[1] // groups
    far_feats = near_feats // HALVES
    shapes = [
        (FIRST_SUBS, 2, cols, far_feats),
        (subs - FIRST_SUBS, 2, cols, far_feats),
        (subs, 4, cols, near_feats),
    ]
    split = [a.reshape(subs, cols, a.shape[1]) for a in (k, v, q, g)]
    return pl.pallas_call(
        pack_body,
        in_specs=[pl.BlockSpec(memory_space=pltpu.HBM)] * 4,
        out_specs=[pl.BlockSpec(memory_space=pltpu.VMEM)] * 3,
        out_shape=[jax.ShapeDtypeStruct((groups, *shape), bf16) for shape in shapes],
        scratch_shapes=[pltpu.SemaphoreType.DMA, pltpu.SemaphoreType.DMA],
        compiler_params=pltpu.CompilerParams(vmem_limit_bytes=PACK_BYTES),
        name="pack",
    )(*split)


STATS_STEP = 128
GRADS_STEP = 256
def long(units):
    return pl.CostEstimate(flops=units * 10**9, bytes_accessed=units << 21, transcendentals=0)


def hold_body(*refs):
    refs[-1][...] = jnp.zeros_like(refs[-1])


def hold(arrays, units):
    return pl.pallas_call(
        hold_body,
        in_specs=[pl.BlockSpec(memory_space=pl.ANY)] * len(arrays),
        out_specs=pl.BlockSpec(memory_space=pltpu.VMEM),
        out_shape=jax.ShapeDtypeStruct((8, 128), f32),
        compiler_params=pltpu.CompilerParams(vmem_limit_bytes=1024 * 1024),
        cost_estimate=long(units),
        name="hold",
    )(*arrays)


def split_body(first_ref, second_ref, token_ref, *out_refs):
    groups = len(out_refs)
    near = lax.rem(lax.axis_index("narrow"), groups)
    for step, ref in enumerate(out_refs):
        cut = first_ref.shape[1]
        ref[:cut] = first_ref[near ^ step]
        ref[cut:] = second_ref[near ^ step]


def split(first, second, token):
    groups, _, arrays, cols, feats = first.shape
    subs = first.shape[1] + second.shape[1]
    whole = pl.BlockSpec(memory_space=pltpu.VMEM)
    return pl.pallas_call(
        split_body,
        in_specs=[whole, whole, pl.BlockSpec(memory_space=pl.ANY)],
        out_specs=[whole] * groups,
        out_shape=[jax.ShapeDtypeStruct((subs, arrays, cols, feats), bf16)] * groups,
        compiler_params=pltpu.CompilerParams(vmem_limit_bytes=VMEM_BYTES),
        cost_estimate=long(SPLIT_UNITS),
        name="split",
    )(first, second, token)


def unpack_body(scal_ref, in_ref, far_ref, value_ref, token_ref, q_ref, k_ref, v_ref):
    members, subs, _, cols, feats = in_ref.shape
    far_feats = far_ref.shape[-1]
    for i in range(members):
        for a, ref in enumerate((q_ref, k_ref, v_ref)):
            for s in range(subs):
                ref[s * cols : (s + 1) * cols, i * feats : (i + 1) * feats] = in_ref[i, s, a]

    def add(ref, i, terms_ref, first):
        place = (pl.program_id(0) * members + i) ^ scal_ref[3]
        feat_cols = slice(i * feats + first, i * feats + first + far_feats)
        total = ref[:, feat_cols].astype(f32) + terms_ref[place].astype(f32)
        ref[:, feat_cols] = total.astype(bf16)

    @pl.when(scal_ref[0] == 0)
    def _():
        for i in range(members):
            add(k_ref, i, far_ref, far_feats)
            add(v_ref, i, value_ref, far_feats)

    @pl.when(scal_ref[0] != 0)
    def _():
        for i in range(members):
            add(q_ref, i, far_ref, 0)


def unpack(scal, arr, far, value, token, tokens, feats):
    groups, subs, _, cols, near_feats = arr.shape
    members = 2
    out = jax.ShapeDtypeStruct((tokens, feats), bf16)
    return pl.pallas_call(
        unpack_body,
        grid=(groups // members,),
        in_specs=[
            smem(),
            pl.BlockSpec((members, subs, 3, cols, near_feats), lambda j: (j, 0, 0, 0, 0)),
            pl.BlockSpec(far.shape, lambda j: (0, 0, 0)),
            pl.BlockSpec(far.shape, lambda j: (0, 0, 0)),
            pl.BlockSpec(memory_space=pl.ANY),
        ],
        out_specs=[pl.BlockSpec((tokens, members * near_feats), lambda j: (0, j))] * 3,
        out_shape=[out] * 3,
        compiler_params=params(),
        name="unpack",
    )(scal, arr, far, value, token)


def flat(ref, index):
    block = ref[:, index]
    return block.reshape(block.shape[0] * block.shape[1], block.shape[2])


def row_mask(scal_ref, n):
    first = scal_ref[1] - scal_ref[0] * n
    u = lax.broadcasted_iota(jnp.int32, (n, n), 0)
    t = lax.broadcasted_iota(jnp.int32, (n, n), 1)
    return (u == t) | ((u < t) & (u >= first))


def off_mask(scal_ref, n):
    return lax.broadcasted_iota(jnp.int32, (n, n), 0) >= scal_ref[1]


def col_mask(scal_ref, n, cols):
    u = lax.broadcasted_iota(jnp.int32, (n, n), 0)
    t = lax.broadcasted_iota(jnp.int32, (n, n), 1)
    same = (u & (cols - 1)) == (t & (cols - 1))
    return same & (u < t) & (u >= scal_ref[2] * cols)


def fill_bias(bias_ref, mask):
    @pl.when(pl.program_id(0) == 0)
    def _():
        bias_ref[...] = jnp.where(mask(bias_ref.shape[0]), 0.0, masked_low)


def partial_stats(k, v, q, g, bias, scale):
    s = dot_nt(k, q) * scale + bias
    m = jnp.maximum(jnp.max(s, axis=0, keepdims=True), least_max)
    e = jnp.exp2(s - m)
    total = jnp.sum(e, axis=0, keepdims=True)
    weighted = jnp.sum(e * dot_nt(v, g), axis=0, keepdims=True)
    some = total > 0.0
    total = jnp.where(some, total, 1.0)
    return jnp.where(some, m + jnp.log2(total), masked_low), weighted / total


def merge(lse_a, delta_a, lse_b, delta_b):
    top = jnp.maximum(lse_a, lse_b)
    a = jnp.exp2(lse_a - top)
    b = jnp.exp2(lse_b - top)
    total = a + b
    return top + jnp.log2(total), (a * delta_a + b * delta_b) / total


def row_stats_body(scale, scal_ref, t_ref, out_ref, bias_ref):
    fill_bias(bias_ref, lambda n: row_mask(scal_ref, n))
    k, v, q, g = (flat(t_ref, i) for i in range(4))
    lse, delta = partial_stats(k, v, q, g, bias_ref[...], scale)
    out_ref[0, 0:1] = lse
    out_ref[0, 1:2] = delta


def gather_far(scal_ref, piece_refs, buf):
    for i, ref in enumerate(piece_refs):
        for a in range(2):
            buf[a, scal_ref[3] ^ i] = flat(ref, a)
    return (buf[a].reshape(buf.shape[1] * buf.shape[2], HEAD) for a in range(2))


def off_stats_body(scale, scal_ref, t_ref, *refs):
    *piece_refs, out_ref, buf, bias_ref = refs
    fill_bias(bias_ref, lambda n: off_mask(scal_ref, n))
    far_a, far_b = gather_far(scal_ref, piece_refs, buf)

    def run(k, v, q, g):
        lse, delta = partial_stats(k, v, q, g, bias_ref[...], scale)
        out_ref[0, 0:1] = lse
        out_ref[0, 1:2] = delta

    @pl.when(scal_ref[0] == 0)
    def _():
        run(flat(t_ref, KI), flat(t_ref, VI), far_a, far_b)

    @pl.when(scal_ref[0] != 0)
    def _():
        run(far_a, far_b, flat(t_ref, QI), flat(t_ref, GI))


def head_slices(ref, head):
    feats = slice(head * HEAD, (head + 1) * HEAD)
    blocks = (ref[:, i, :, feats] for i in range(ref.shape[1]))
    return (b.reshape(b.shape[0] * b.shape[1], HEAD) for b in blocks)


def col_stats_body(scale, scal_ref, t_ref, out_ref):
    rows, _, cols, _ = t_ref.shape
    bias = jnp.where(col_mask(scal_ref, rows * cols, cols), 0.0, masked_low)
    for head in range(out_ref.shape[0]):
        k, v, q, g = head_slices(t_ref, head)
        for start in range(0, rows * cols, STATS_STEP):
            part, upto = slice(start, start + STATS_STEP), slice(0, start + STATS_STEP)
            lse, delta = partial_stats(k[upto], v[upto], q[part], g[part], bias[upto, part], scale)
            out_ref[head, 0:1, part] = lse
            out_ref[head, 1:2, part] = delta


def col_stats(scale, scal, t):
    rows, _, cols, feats = t.shape
    whole = pl.BlockSpec(memory_space=pltpu.VMEM)
    return pl.pallas_call(
        lambda *refs: col_stats_body(scale, *refs),
        in_specs=[smem(), whole],
        out_specs=whole,
        out_shape=jax.ShapeDtypeStruct((feats // HEAD, 2, rows * cols), f32),
        compiler_params=pltpu.CompilerParams(vmem_limit_bytes=VMEM_BYTES),
        cost_estimate=cost(4),
        name="col_stats",
    )(scal, t)


def smem():
    return pl.BlockSpec(memory_space=pltpu.SMEM)


def head_block(arr):
    a, b, c, _ = arr.shape
    return pl.BlockSpec((a, b, c, HEAD), lambda h: (0, 0, 0, h))


def off_block(arr, heads):
    a, b, c, _ = arr.shape
    return pl.BlockSpec((a, b, c, HEAD), lambda h, scal_ref: (0, 0, 0, h + scal_ref[0] * heads))


def off_call(body, scale, scal, t, extra, extra_specs, pieces, out_specs, out_shape, units, name):
    heads = pieces[0].shape[3] // HEAD
    tokens = pieces[0].shape[0] * pieces[0].shape[2]
    rows, _, cols, _ = t.shape
    stat_spec = pl.BlockSpec((1, 2, rows * cols), lambda h, scal_ref: (h, 0, 0))
    piece_specs = [
        pl.BlockSpec((*p.shape[:3], HEAD), lambda h, scal_ref: (0, 0, 0, h)) for p in pieces
    ]
    return pl.pallas_call(
        lambda *refs: body(scale, *refs),
        grid_spec=pltpu.PrefetchScalarGridSpec(
            num_scalar_prefetch=1,
            grid=(heads,),
            in_specs=[off_block(t, heads)] + [spec or stat_spec for spec in extra_specs] + piece_specs,
            out_specs=out_specs,
            scratch_shapes=[
                pltpu.VMEM((2, len(pieces), tokens, HEAD), bf16),
                pltpu.VMEM((rows * cols, rows * cols), f32),
            ],
        ),
        out_shape=out_shape,
        compiler_params=params(),
        cost_estimate=cost(units),
        name=name,
    )(scal, t, *extra, *pieces)


def off_stats(scale, scal, t, pieces):
    heads = pieces[0].shape[3] // HEAD
    n = t.shape[0] * t.shape[2]
    return off_call(
        off_stats_body, scale, scal, t, (), (), pieces,
        pl.BlockSpec((1, 2, n), lambda h, scal_ref: (h, 0, 0)),
        jax.ShapeDtypeStruct((heads, 2, n), f32), 2, "off_stats",
    )


def off_grads_body(scale, scal_ref, t_ref, stat_ref, token_ref, *refs):
    *piece_refs, near_ref, far_ref, buf, bias_ref = refs
    fill_bias(bias_ref, lambda n: off_mask(scal_ref, n))
    far_a, far_b = gather_far(scal_ref, piece_refs, buf)
    lse, delta = stat_ref[0, 0:1], stat_ref[0, 1:2]

    def run(k, v, q, g):
        return block_grads(k, v, q, g, bias_ref[...], lse, delta, scale)

    @pl.when(scal_ref[0] == 0)
    def _():
        dq, dk, dv = run(flat(t_ref, KI), flat(t_ref, VI), far_a, far_b)
        near_ref[0] = dk
        near_ref[1] = dv
        far_ref[:, 0] = dq.astype(bf16).reshape(far_ref.shape[0], far_ref.shape[2], HEAD)

    @pl.when(scal_ref[0] != 0)
    def _():
        dq, dk, dv = run(far_a, far_b, flat(t_ref, QI), flat(t_ref, GI))
        near_ref[0] = dq
        for a, d in enumerate((dk, dv)):
            far_ref[:, a] = d.astype(bf16).reshape(far_ref.shape[0], far_ref.shape[2], HEAD)


def off_grads(scale, scal, t, stats, token, pieces):
    n = t.shape[0] * t.shape[2]
    feats = pieces[0].shape[3]
    far_shape = (len(pieces), 2, n // len(pieces), feats)
    return off_call(
        off_grads_body, scale, scal, t, (stats, token),
        (None, pl.BlockSpec(memory_space=pl.ANY)), pieces,
        [
            pl.BlockSpec((2, n, HEAD), lambda h, scal_ref: (0, 0, h)),
            pl.BlockSpec((*far_shape[:3], HEAD), lambda h, scal_ref: (0, 0, 0, h)),
        ],
        [jax.ShapeDtypeStruct((2, n, feats), f32), jax.ShapeDtypeStruct(far_shape, bf16)],
        5,
        "off_grads",
    )


def stats_call(body, scale, scal, arrays, name, units):
    heads = arrays[0].shape[3] // HEAD
    n = arrays[0].shape[0] * arrays[0].shape[2]
    return pl.pallas_call(
        lambda *refs: body(scale, *refs),
        grid=(heads,),
        in_specs=[smem()] + [head_block(a) for a in arrays],
        out_specs=pl.BlockSpec((1, 2, n), lambda h: (h, 0, 0)),
        out_shape=jax.ShapeDtypeStruct((heads, 2, n), f32),
        scratch_shapes=[pltpu.VMEM((n, n), f32)],
        compiler_params=params(),
        cost_estimate=cost(units),
        name=name,
    )(scal, *arrays)


def block_grads(k, v, q, g, bias, lse, delta, scale):
    p = jnp.exp2(dot_nt(k, q) * scale + (bias - lse))
    ds = (p * (dot_nt(v, g) - delta)).astype(bf16)
    dv = dot_nn(p.astype(bf16), g)
    dk = dot_nn(ds, q) * score_scale
    dq = dot_nn(k.T, ds).T * score_scale
    return dq, dk, dv


def row_grads_body(scale, scal_ref, t_ref, stat_ref, off_ref, out_ref, sum_ref, bias_ref):
    fill_bias(bias_ref, lambda n: row_mask(scal_ref, n))
    k, v, q, g = (flat(t_ref, i) for i in range(4))
    grads = block_grads(k, v, q, g, bias_ref[...], stat_ref[0, 0:1], stat_ref[0, 1:2], scale)
    upper = scal_ref[0] != 0
    has_off = (pl.program_id(0) >= pl.num_programs(0) // HALVES) == upper
    for a, d in enumerate(grads):
        sum_ref[a] = d

    @pl.when(has_off & upper)
    def _():
        sum_ref[0] += off_ref[0]

    @pl.when(has_off & jnp.logical_not(upper))
    def _():
        sum_ref[1] += off_ref[0]
        sum_ref[2] += off_ref[1]

    for a in range(3):
        out_ref[:, a] = sum_ref[a].astype(bf16).reshape(out_ref.shape[0], out_ref.shape[2], HEAD)


def col_grads_body(scale, scal_ref, t_ref, own_ref, got_ref, out_ref):
    rows, _, cols, _ = t_ref.shape
    bias = jnp.where(col_mask(scal_ref, rows * cols, cols), 0.0, masked_low)
    for head in range(own_ref.shape[0]):
        k, v, q, g = head_slices(t_ref, head)
        lse, delta = merge(
            own_ref[head, 0:1], own_ref[head, 1:2], got_ref[head, 0:1], got_ref[head, 1:2]
        )
        feats = slice(head * HEAD, (head + 1) * HEAD)

        def put(a, part, d):
            rows_here = slice(part.start // cols, part.stop // cols)
            out_ref[rows_here, a, :, feats] = d.astype(bf16).reshape(-1, cols, HEAD)

        n = rows * cols
        dk_sum = dv_sum = None
        for stop in range(n, 0, -GRADS_STEP):
            part, upto = slice(stop - GRADS_STEP, stop), slice(0, stop)
            dq, dk, dv = block_grads(
                k[upto], v[upto], q[part], g[part], bias[upto, part], lse[:, part], delta[:, part], scale
            )
            dk_sum = dk if dk_sum is None else dk_sum[upto] + dk
            dv_sum = dv if dv_sum is None else dv_sum[upto] + dv
            put(0, part, dq)
            put(1, part, dk_sum[part])
            put(2, part, dv_sum[part])


def row_grads(scale, scal, t, stats, off):
    rows, _, cols, feats = t.shape
    n = rows * cols
    near_heads = off.shape[2] // HEAD
    return pl.pallas_call(
        lambda *refs: row_grads_body(scale, *refs),
        grid=(feats // HEAD,),
        in_specs=[
            smem(),
            head_block(t),
            pl.BlockSpec((1, 2, n), lambda h: (h, 0, 0)),
            pl.BlockSpec((2, n, HEAD), lambda h: (0, 0, h % near_heads)),
        ],
        out_specs=pl.BlockSpec((rows, 3, cols, HEAD), lambda h: (0, 0, 0, h)),
        out_shape=jax.ShapeDtypeStruct((rows, 3, cols, feats), bf16),
        scratch_shapes=[pltpu.VMEM((3, n, HEAD), f32), pltpu.VMEM((n, n), f32)],
        compiler_params=params(),
        cost_estimate=cost(8),
        name="row_grads",
    )(scal, t, stats, off)


def col_grads(scale, scal, t, own, got):
    rows, _, cols, feats = t.shape
    whole = pl.BlockSpec(memory_space=pltpu.VMEM)
    return pl.pallas_call(
        lambda *refs: col_grads_body(scale, *refs),
        in_specs=[smem(), whole, whole, whole],
        out_specs=whole,
        out_shape=jax.ShapeDtypeStruct((rows, 3, cols, feats), bf16),
        compiler_params=pltpu.CompilerParams(vmem_limit_bytes=VMEM_BYTES),
        cost_estimate=cost(8),
        name="col_grads",
    )(scal, t, own, got)


def join_body(row_ref, col_ref, out_ref):
    out_ref[...] = (row_ref[...].astype(f32) + col_ref[...].astype(f32)).astype(bf16)


def join(row, col):
    rows, arrays, cols, feats = col.shape
    steps = 4
    spec = pl.BlockSpec((rows // steps, arrays, cols, feats), lambda i: (i, 0, 0, 0))
    return pl.pallas_call(
        join_body,
        grid=(steps,),
        in_specs=[spec, spec],
        out_specs=spec,
        out_shape=jax.ShapeDtypeStruct(col.shape, bf16),
        compiler_params=params(),
        name="join",
    )(row, col)


def body(query_in, key_in, value_in, grad_out, row_start, col_start):
    scale = score_scale * math.log2(math.e)
    tokens, feats = query_in.shape
    lanes = lax.axis_size("wide")
    narrow = lax.axis_size("narrow")
    groups = narrow // HALVES
    half_cols = tokens * groups
    cols = half_cols // lanes
    subs = tokens // cols
    near = [[half * groups + j for j in range(groups)] for half in range(HALVES)]

    def exchange_near(arr):
        return lax.all_to_all(
            arr, "narrow", split_axis=0, concat_axis=0, axis_index_groups=near, tiled=True
        )

    def exchange_wide(arr):
        return lax.all_to_all(arr, "wide", split_axis=0, concat_axis=0, tiled=True)

    def shift(arr, source, target):
        pairs = [(source * groups + j, target * groups + j) for j in range(groups)]
        return lax.ppermute(arr, "narrow", pairs)

    def swap(arr, step):
        pairs = [(i, i ^ step) for i in range(narrow)]
        return lax.ppermute(arr, "narrow", pairs)

    def spread(pieces):
        return [swap(piece, step) if step else piece for step, piece in enumerate(pieces)]

    wide_index = lax.axis_index("wide")
    narrow_index = lax.axis_index("narrow")
    half = narrow_index // groups
    near_index = narrow_index % groups
    first_col = lax.dynamic_index_in_dim(row_start, wide_index, keepdims=False)
    block_id = (half * half_cols + wide_index * cols) // CB
    first_row = lax.dynamic_index_in_dim(col_start, block_id, keepdims=False)
    scal = jnp.stack([half, first_col, first_row, near_index]).astype(jnp.int32)

    far_first, far_second, packed = pack(key_in, value_in, query_in, grad_out, groups, subs, cols)
    near_feats = feats // groups
    heads = near_feats // HEAD
    near_heads = heads // HALVES
    far_first = swap(far_first, groups)
    token = hold([far_first], FIRST_UNITS)
    far_second = swap(far_second, groups)
    t = exchange_near(packed).reshape(lanes, 4, cols, near_feats)
    t, token = lax.optimization_barrier((t, token))
    by_col = exchange_wide(t)
    pieces = spread(split(far_first, far_second, token))
    diag_part = stats_call(row_stats_body, scale, scal, (t,), "row_stats", 4)
    own_off = off_stats(scale, scal, t, pieces)
    off_part = jnp.concatenate([shift(own_off, 0, 1), own_off])
    lse, delta = merge(diag_part[:, 0], diag_part[:, 1], off_part[:, 0], off_part[:, 1])
    row_part = jnp.where(half == 1, jnp.stack([lse, delta], axis=1), diag_part)
    col_part = col_stats(scale, scal, by_col)

    both = jnp.stack([row_part, col_part]).reshape(4 * heads, lanes, cols)
    sent = both.transpose(1, 0, 2).reshape(lanes, (4 * heads * cols) // HEAD, HEAD)
    got = exchange_wide(sent).reshape(lanes, 4 * heads, cols).transpose(1, 0, 2)
    got = got.reshape(2, heads, 2, lanes * cols)
    row_lse, row_delta = merge(row_part[:, 0], row_part[:, 1], got[1, :, 0], got[1, :, 1])
    row_full = jnp.stack([row_lse, row_delta], axis=1)

    far_full = shift(row_full[:near_heads], 1, 0)
    token = hold([far_full], FULL_UNITS)
    from_col = exchange_wide(col_grads(scale, scal, by_col, col_part, got[0]))
    off_full = jnp.where(half == 1, row_full[near_heads:], far_full)
    off_terms, far_terms = off_grads(scale, scal, t, off_full, token, pieces)
    row_terms = row_grads(scale, scal, t, row_full, off_terms)
    by_step = [
        lax.dynamic_index_in_dim(far_terms, near_index ^ step, keepdims=False)
        for step in range(groups)
    ]
    by_step = spread(by_step)
    far_terms, far_value = (jnp.stack([piece[a] for piece in by_step]) for a in range(2))
    from_col, far_terms, far_value, row_terms = lax.optimization_barrier(
        (from_col, far_terms, far_value, row_terms)
    )
    far_value = shift(far_value, 1, 0)
    far_terms = swap(far_terms, groups)
    token = hold([far_terms, far_value], BACK_UNITS)
    joined = join(row_terms, from_col)
    out = exchange_near(joined.reshape(groups, subs, 3, cols, near_feats))
    return unpack(scal, out, far_terms, far_value, token, tokens, feats)


def solution(mesh):
    placed = P(("wide", "narrow"), None)
    return jax.shard_map(
        body,
        mesh=mesh,
        in_specs=(placed,) * 4 + (P(), P()),
        out_specs=(placed,) * 3,
        check_vma=False,
    )
```

```python
import math

import jax
import jax.numpy as jnp
from jax import lax
from jax.experimental import pallas as pl
from jax.experimental.pallas import tpu as pltpu
from jax.sharding import PartitionSpec as P

HEAD = 128
CB = 128
HALVES = 2
FIRST_SUBS = 1
FIRST_UNITS, SPLIT_UNITS, FULL_UNITS, BACK_UNITS = 40, 100, 40, 40
VMEM_BYTES = 16 * 1024 * 1024
PACK_BYTES = 60 * 1024 * 1024

masked_low = -1e30
least_max = -1e29
score_scale = 1.0 / math.sqrt(HEAD)
f32 = jnp.float32
bf16 = jnp.bfloat16
QI, GI, KI, VI = 2, 3, 0, 1


def dot_nt(a, b):
    return lax.dot_general(a, b, (((1,), (1,)), ((), ())), preferred_element_type=f32)


def dot_nn(a, b):
    return lax.dot_general(a, b, (((1,), (0,)), ((), ())), preferred_element_type=f32)


def params(n_axes=1):
    return pltpu.CompilerParams(
        dimension_semantics=("arbitrary",) * n_axes, vmem_limit_bytes=VMEM_BYTES
    )


def cost(units):
    return pl.CostEstimate(
        flops=units * 10 * 512 * 512 * 128, bytes_accessed=4 << 20, transcendentals=units * 512 * 512
    )


def pack_body(k_ref, v_ref, q_ref, g_ref, first_ref, second_ref, out_ref, near_sem, far_sem):
    groups, feats, far_feats = out_ref.shape[0], out_ref.shape[-1], first_ref.shape[-1]
    cut = first_ref.shape[1]
    lower = lax.axis_index("narrow") < groups

    def far_copies(pair, first):
        for a, ref in enumerate(pair):
            for j in range(groups):
                lanes = pl.ds(j * feats + first, far_feats)
                src = ref.at[:cut, :, lanes]
                yield pltpu.make_async_copy(src, first_ref.at[j, :, a], far_sem)
                src = ref.at[cut:, :, lanes]
                yield pltpu.make_async_copy(src, second_ref.at[j, :, a], far_sem)

    def near_copies():
        for j in range(groups):
            for a, ref in enumerate((k_ref, v_ref, q_ref, g_ref)):
                src = ref.at[:, :, pl.ds(j * feats, feats)]
                yield pltpu.make_async_copy(src, out_ref.at[j, :, a], near_sem)

    @pl.when(lower)
    def _():
        for copy in far_copies((k_ref, v_ref), far_feats):
            copy.start()

    @pl.when(jnp.logical_not(lower))
    def _():
        for copy in far_copies((q_ref, g_ref), 0):
            copy.start()

    for copy in near_copies():
        copy.start()
    for copy in far_copies((k_ref, v_ref), 0):
        copy.wait()
    for copy in near_copies():
        copy.wait()


def pack(k, v, q, g, groups, subs, cols):
    near_feats = k.shape[1] // groups
    far_feats = near_feats // HALVES
    shapes = [
        (FIRST_SUBS, 2, cols, far_feats),
        (subs - FIRST_SUBS, 2, cols, far_feats),
        (subs, 4, cols, near_feats),
    ]
    split = [a.reshape(subs, cols, a.shape[1]) for a in (k, v, q, g)]
    return pl.pallas_call(
        pack_body,
        in_specs=[pl.BlockSpec(memory_space=pltpu.HBM)] * 4,
        out_specs=[pl.BlockSpec(memory_space=pltpu.VMEM)] * 3,
        out_shape=[jax.ShapeDtypeStruct((groups, *shape), bf16) for shape in shapes],
        scratch_shapes=[pltpu.SemaphoreType.DMA, pltpu.SemaphoreType.DMA],
        compiler_params=pltpu.CompilerParams(vmem_limit_bytes=PACK_BYTES),
        name="pack",
    )(*split)


STATS_STEP = 128
GRADS_STEP = 256
def long(units):
    return pl.CostEstimate(flops=units * 10**9, bytes_accessed=units << 21, transcendentals=0)


def hold_body(*refs):
    refs[-1][...] = jnp.zeros_like(refs[-1])


def hold(arrays, units):
    return pl.pallas_call(
        hold_body,
        in_specs=[pl.BlockSpec(memory_space=pl.ANY)] * len(arrays),
        out_specs=pl.BlockSpec(memory_space=pltpu.VMEM),
        out_shape=jax.ShapeDtypeStruct((8, 128), f32),
        compiler_params=pltpu.CompilerParams(vmem_limit_bytes=1024 * 1024),
        cost_estimate=long(units),
        name="hold",
    )(*arrays)


def split_body(first_ref, second_ref, token_ref, *out_refs):
    groups = len(out_refs)
    near = lax.rem(lax.axis_index("narrow"), groups)
    for step, ref in enumerate(out_refs):
        cut = first_ref.shape[1]
        ref[:cut] = first_ref[near ^ step]
        ref[cut:] = second_ref[near ^ step]


def split(first, second, token):
    groups, _, arrays, cols, feats = first.shape
    subs = first.shape[1] + second.shape[1]
    whole = pl.BlockSpec(memory_space=pltpu.VMEM)
    return pl.pallas_call(
        split_body,
        in_specs=[whole, whole, pl.BlockSpec(memory_space=pl.ANY)],
        out_specs=[whole] * groups,
        out_shape=[jax.ShapeDtypeStruct((subs, arrays, cols, feats), bf16)] * groups,
        compiler_params=pltpu.CompilerParams(vmem_limit_bytes=VMEM_BYTES),
        cost_estimate=long(SPLIT_UNITS),
        name="split",
    )(first, second, token)


def unpack_body(scal_ref, in_ref, far_ref, value_ref, token_ref, q_ref, k_ref, v_ref):
    members, subs, _, cols, feats = in_ref.shape
    far_feats = far_ref.shape[-1]
    for i in range(members):
        for a, ref in enumerate((q_ref, k_ref, v_ref)):
            for s in range(subs):
                ref[s * cols : (s + 1) * cols, i * feats : (i + 1) * feats] = in_ref[i, s, a]

    def add(ref, i, terms_ref, first):
        place = (pl.program_id(0) * members + i) ^ scal_ref[3]
        feat_cols = slice(i * feats + first, i * feats + first + far_feats)
        total = ref[:, feat_cols].astype(f32) + terms_ref[place].astype(f32)
        ref[:, feat_cols] = total.astype(bf16)

    @pl.when(scal_ref[0] == 0)
    def _():
        for i in range(members):
            add(k_ref, i, far_ref, far_feats)
            add(v_ref, i, value_ref, far_feats)

    @pl.when(scal_ref[0] != 0)
    def _():
        for i in range(members):
            add(q_ref, i, far_ref, 0)


def unpack(scal, arr, far, value, token, tokens, feats):
    groups, subs, _, cols, near_feats = arr.shape
    members = 4
    out = jax.ShapeDtypeStruct((tokens, feats), bf16)
    return pl.pallas_call(
        unpack_body,
        grid=(groups // members,),
        in_specs=[
            smem(),
            pl.BlockSpec((members, subs, 3, cols, near_feats), lambda j: (j, 0, 0, 0, 0)),
            pl.BlockSpec(far.shape, lambda j: (0, 0, 0)),
            pl.BlockSpec(far.shape, lambda j: (0, 0, 0)),
            pl.BlockSpec(memory_space=pl.ANY),
        ],
        out_specs=[pl.BlockSpec((tokens, members * near_feats), lambda j: (0, j))] * 3,
        out_shape=[out] * 3,
        compiler_params=params(),
        name="unpack",
    )(scal, arr, far, value, token)


def flat(ref, index):
    block = ref[:, index]
    return block.reshape(block.shape[0] * block.shape[1], block.shape[2])


def row_mask(scal_ref, n):
    first = scal_ref[1] - scal_ref[0] * n
    u = lax.broadcasted_iota(jnp.int32, (n, n), 0)
    t = lax.broadcasted_iota(jnp.int32, (n, n), 1)
    return (u == t) | ((u < t) & (u >= first))


def off_mask(scal_ref, n):
    return lax.broadcasted_iota(jnp.int32, (n, n), 0) >= scal_ref[1]


def col_mask(scal_ref, n, cols):
    u = lax.broadcasted_iota(jnp.int32, (n, n), 0)
    t = lax.broadcasted_iota(jnp.int32, (n, n), 1)
    same = (u & (cols - 1)) == (t & (cols - 1))
    return same & (u < t) & (u >= scal_ref[2] * cols)


def fill_bias(bias_ref, mask):
    @pl.when(pl.program_id(0) == 0)
    def _():
        bias_ref[...] = jnp.where(mask(bias_ref.shape[0]), 0.0, masked_low)


def partial_stats(k, v, q, g, bias, scale):
    s = dot_nt(k, q) * scale + bias
    m = jnp.maximum(jnp.max(s, axis=0, keepdims=True), least_max)
    e = jnp.exp2(s - m)
    total = jnp.sum(e, axis=0, keepdims=True)
    weighted = jnp.sum(e * dot_nt(v, g), axis=0, keepdims=True)
    some = total > 0.0
    total = jnp.where(some, total, 1.0)
    return jnp.where(some, m + jnp.log2(total), masked_low), weighted / total


def merge(lse_a, delta_a, lse_b, delta_b):
    top = jnp.maximum(lse_a, lse_b)
    a = jnp.exp2(lse_a - top)
    b = jnp.exp2(lse_b - top)
    total = a + b
    return top + jnp.log2(total), (a * delta_a + b * delta_b) / total


def row_stats_body(scale, scal_ref, t_ref, out_ref, bias_ref):
    fill_bias(bias_ref, lambda n: row_mask(scal_ref, n))
    k, v, q, g = (flat(t_ref, i) for i in range(4))
    lse, delta = partial_stats(k, v, q, g, bias_ref[...], scale)
    out_ref[0, 0:1] = lse
    out_ref[0, 1:2] = delta


def gather_far(scal_ref, piece_refs, buf):
    for i, ref in enumerate(piece_refs):
        for a in range(2):
            buf[a, scal_ref[3] ^ i] = flat(ref, a)
    return (buf[a].reshape(buf.shape[1] * buf.shape[2], HEAD) for a in range(2))


def off_stats_body(scale, scal_ref, t_ref, *refs):
    *piece_refs, out_ref, buf, bias_ref = refs
    fill_bias(bias_ref, lambda n: off_mask(scal_ref, n))
    far_a, far_b = gather_far(scal_ref, piece_refs, buf)

    def run(k, v, q, g):
        lse, delta = partial_stats(k, v, q, g, bias_ref[...], scale)
        out_ref[0, 0:1] = lse
        out_ref[0, 1:2] = delta

    @pl.when(scal_ref[0] == 0)
    def _():
        run(flat(t_ref, KI), flat(t_ref, VI), far_a, far_b)

    @pl.when(scal_ref[0] != 0)
    def _():
        run(far_a, far_b, flat(t_ref, QI), flat(t_ref, GI))


def head_slices(ref, head):
    feats = slice(head * HEAD, (head + 1) * HEAD)
    blocks = (ref[:, i, :, feats] for i in range(ref.shape[1]))
    return (b.reshape(b.shape[0] * b.shape[1], HEAD) for b in blocks)


def col_stats_body(scale, scal_ref, t_ref, out_ref):
    rows, _, cols, _ = t_ref.shape
    bias = jnp.where(col_mask(scal_ref, rows * cols, cols), 0.0, masked_low)
    for head in range(out_ref.shape[0]):
        k, v, q, g = head_slices(t_ref, head)
        for start in range(0, rows * cols, STATS_STEP):
            part, upto = slice(start, start + STATS_STEP), slice(0, start + STATS_STEP)
            lse, delta = partial_stats(k[upto], v[upto], q[part], g[part], bias[upto, part], scale)
            out_ref[head, 0:1, part] = lse
            out_ref[head, 1:2, part] = delta


def col_stats(scale, scal, t):
    rows, _, cols, feats = t.shape
    whole = pl.BlockSpec(memory_space=pltpu.VMEM)
    return pl.pallas_call(
        lambda *refs: col_stats_body(scale, *refs),
        in_specs=[smem(), whole],
        out_specs=whole,
        out_shape=jax.ShapeDtypeStruct((feats // HEAD, 2, rows * cols), f32),
        compiler_params=pltpu.CompilerParams(vmem_limit_bytes=VMEM_BYTES),
        cost_estimate=cost(4),
        name="col_stats",
    )(scal, t)


def smem():
    return pl.BlockSpec(memory_space=pltpu.SMEM)


def head_block(arr):
    a, b, c, _ = arr.shape
    return pl.BlockSpec((a, b, c, HEAD), lambda h: (0, 0, 0, h))


def off_block(arr, heads):
    a, b, c, _ = arr.shape
    return pl.BlockSpec((a, b, c, HEAD), lambda h, scal_ref: (0, 0, 0, h + scal_ref[0] * heads))


def off_call(body, scale, scal, t, extra, extra_specs, pieces, out_specs, out_shape, units, name):
    heads = pieces[0].shape[3] // HEAD
    tokens = pieces[0].shape[0] * pieces[0].shape[2]
    rows, _, cols, _ = t.shape
    stat_spec = pl.BlockSpec((1, 2, rows * cols), lambda h, scal_ref: (h, 0, 0))
    piece_specs = [
        pl.BlockSpec((*p.shape[:3], HEAD), lambda h, scal_ref: (0, 0, 0, h)) for p in pieces
    ]
    return pl.pallas_call(
        lambda *refs: body(scale, *refs),
        grid_spec=pltpu.PrefetchScalarGridSpec(
            num_scalar_prefetch=1,
            grid=(heads,),
            in_specs=[off_block(t, heads)] + [spec or stat_spec for spec in extra_specs] + piece_specs,
            out_specs=out_specs,
            scratch_shapes=[
                pltpu.VMEM((2, len(pieces), tokens, HEAD), bf16),
                pltpu.VMEM((rows * cols, rows * cols), f32),
            ],
        ),
        out_shape=out_shape,
        compiler_params=params(),
        cost_estimate=cost(units),
        name=name,
    )(scal, t, *extra, *pieces)


def off_stats(scale, scal, t, pieces):
    heads = pieces[0].shape[3] // HEAD
    n = t.shape[0] * t.shape[2]
    return off_call(
        off_stats_body, scale, scal, t, (), (), pieces,
        pl.BlockSpec((1, 2, n), lambda h, scal_ref: (h, 0, 0)),
        jax.ShapeDtypeStruct((heads, 2, n), f32), 2, "off_stats",
    )


def off_grads_body(scale, scal_ref, t_ref, stat_ref, token_ref, *refs):
    *piece_refs, near_ref, far_ref, buf, bias_ref = refs
    fill_bias(bias_ref, lambda n: off_mask(scal_ref, n))
    far_a, far_b = gather_far(scal_ref, piece_refs, buf)
    lse, delta = stat_ref[0, 0:1], stat_ref[0, 1:2]

    def run(k, v, q, g):
        return block_grads(k, v, q, g, bias_ref[...], lse, delta, scale)

    @pl.when(scal_ref[0] == 0)
    def _():
        dq, dk, dv = run(flat(t_ref, KI), flat(t_ref, VI), far_a, far_b)
        near_ref[0] = dk
        near_ref[1] = dv
        far_ref[:, 0] = dq.astype(bf16).reshape(far_ref.shape[0], far_ref.shape[2], HEAD)

    @pl.when(scal_ref[0] != 0)
    def _():
        dq, dk, dv = run(far_a, far_b, flat(t_ref, QI), flat(t_ref, GI))
        near_ref[0] = dq
        for a, d in enumerate((dk, dv)):
            far_ref[:, a] = d.astype(bf16).reshape(far_ref.shape[0], far_ref.shape[2], HEAD)


def off_grads(scale, scal, t, stats, token, pieces):
    n = t.shape[0] * t.shape[2]
    feats = pieces[0].shape[3]
    far_shape = (len(pieces), 2, n // len(pieces), feats)
    return off_call(
        off_grads_body, scale, scal, t, (stats, token),
        (None, pl.BlockSpec(memory_space=pl.ANY)), pieces,
        [
            pl.BlockSpec((2, n, HEAD), lambda h, scal_ref: (0, 0, h)),
            pl.BlockSpec((*far_shape[:3], HEAD), lambda h, scal_ref: (0, 0, 0, h)),
        ],
        [jax.ShapeDtypeStruct((2, n, feats), f32), jax.ShapeDtypeStruct(far_shape, bf16)],
        5,
        "off_grads",
    )


def stats_call(body, scale, scal, arrays, name, units):
    heads = arrays[0].shape[3] // HEAD
    n = arrays[0].shape[0] * arrays[0].shape[2]
    return pl.pallas_call(
        lambda *refs: body(scale, *refs),
        grid=(heads,),
        in_specs=[smem()] + [head_block(a) for a in arrays],
        out_specs=pl.BlockSpec((1, 2, n), lambda h: (h, 0, 0)),
        out_shape=jax.ShapeDtypeStruct((heads, 2, n), f32),
        scratch_shapes=[pltpu.VMEM((n, n), f32)],
        compiler_params=params(),
        cost_estimate=cost(units),
        name=name,
    )(scal, *arrays)


def block_grads(k, v, q, g, bias, lse, delta, scale):
    p = jnp.exp2(dot_nt(k, q) * scale + (bias - lse))
    ds = (p * (dot_nt(v, g) - delta)).astype(bf16)
    dv = dot_nn(p.astype(bf16), g)
    dk = dot_nn(ds, q) * score_scale
    dq = dot_nn(k.T, ds).T * score_scale
    return dq, dk, dv


def row_grads_body(scale, scal_ref, t_ref, stat_ref, off_ref, out_ref, sum_ref, bias_ref):
    fill_bias(bias_ref, lambda n: row_mask(scal_ref, n))
    k, v, q, g = (flat(t_ref, i) for i in range(4))
    grads = block_grads(k, v, q, g, bias_ref[...], stat_ref[0, 0:1], stat_ref[0, 1:2], scale)
    upper = scal_ref[0] != 0
    has_off = (pl.program_id(0) >= pl.num_programs(0) // HALVES) == upper
    for a, d in enumerate(grads):
        sum_ref[a] = d

    @pl.when(has_off & upper)
    def _():
        sum_ref[0] += off_ref[0]

    @pl.when(has_off & jnp.logical_not(upper))
    def _():
        sum_ref[1] += off_ref[0]
        sum_ref[2] += off_ref[1]

    for a in range(3):
        out_ref[:, a] = sum_ref[a].astype(bf16).reshape(out_ref.shape[0], out_ref.shape[2], HEAD)


def col_grads_body(scale, scal_ref, t_ref, own_ref, got_ref, out_ref):
    rows, _, cols, _ = t_ref.shape
    bias = jnp.where(col_mask(scal_ref, rows * cols, cols), 0.0, masked_low)
    for head in range(own_ref.shape[0]):
        k, v, q, g = head_slices(t_ref, head)
        lse, delta = merge(
            own_ref[head, 0:1], own_ref[head, 1:2], got_ref[head, 0:1], got_ref[head, 1:2]
        )
        feats = slice(head * HEAD, (head + 1) * HEAD)

        def put(a, part, d):
            rows_here = slice(part.start // cols, part.stop // cols)
            out_ref[rows_here, a, :, feats] = d.astype(bf16).reshape(-1, cols, HEAD)

        n = rows * cols
        dk_sum = dv_sum = None
        for stop in range(n, 0, -GRADS_STEP):
            part, upto = slice(stop - GRADS_STEP, stop), slice(0, stop)
            dq, dk, dv = block_grads(
                k[upto], v[upto], q[part], g[part], bias[upto, part], lse[:, part], delta[:, part], scale
            )
            dk_sum = dk if dk_sum is None else dk_sum[upto] + dk
            dv_sum = dv if dv_sum is None else dv_sum[upto] + dv
            put(0, part, dq)
            put(1, part, dk_sum[part])
            put(2, part, dv_sum[part])


def row_grads(scale, scal, t, stats, off):
    rows, _, cols, feats = t.shape
    n = rows * cols
    near_heads = off.shape[2] // HEAD
    return pl.pallas_call(
        lambda *refs: row_grads_body(scale, *refs),
        grid=(feats // HEAD,),
        in_specs=[
            smem(),
            head_block(t),
            pl.BlockSpec((1, 2, n), lambda h: (h, 0, 0)),
            pl.BlockSpec((2, n, HEAD), lambda h: (0, 0, h % near_heads)),
        ],
        out_specs=pl.BlockSpec((rows, 3, cols, HEAD), lambda h: (0, 0, 0, h)),
        out_shape=jax.ShapeDtypeStruct((rows, 3, cols, feats), bf16),
        scratch_shapes=[pltpu.VMEM((3, n, HEAD), f32), pltpu.VMEM((n, n), f32)],
        compiler_params=params(),
        cost_estimate=cost(8),
        name="row_grads",
    )(scal, t, stats, off)


def col_grads(scale, scal, t, own, got):
    rows, _, cols, feats = t.shape
    whole = pl.BlockSpec(memory_space=pltpu.VMEM)
    return pl.pallas_call(
        lambda *refs: col_grads_body(scale, *refs),
        in_specs=[smem(), whole, whole, whole],
        out_specs=whole,
        out_shape=jax.ShapeDtypeStruct((rows, 3, cols, feats), bf16),
        compiler_params=pltpu.CompilerParams(vmem_limit_bytes=VMEM_BYTES),
        cost_estimate=cost(8),
        name="col_grads",
    )(scal, t, own, got)


def join_body(row_ref, col_ref, out_ref):
    out_ref[...] = (row_ref[...].astype(f32) + col_ref[...].astype(f32)).astype(bf16)


def join(row, col):
    rows, arrays, cols, feats = col.shape
    steps = 4
    spec = pl.BlockSpec((rows // steps, arrays, cols, feats), lambda i: (i, 0, 0, 0))
    return pl.pallas_call(
        join_body,
        grid=(steps,),
        in_specs=[spec, spec],
        out_specs=spec,
        out_shape=jax.ShapeDtypeStruct(col.shape, bf16),
        compiler_params=params(),
        name="join",
    )(row, col)


def body(query_in, key_in, value_in, grad_out, row_start, col_start):
    scale = score_scale * math.log2(math.e)
    tokens, feats = query_in.shape
    lanes = lax.axis_size("wide")
    narrow = lax.axis_size("narrow")
    groups = narrow // HALVES
    half_cols = tokens * groups
    cols = half_cols // lanes
    subs = tokens // cols
    near = [[half * groups + j for j in range(groups)] for half in range(HALVES)]

    def exchange_near(arr):
        return lax.all_to_all(
            arr, "narrow", split_axis=0, concat_axis=0, axis_index_groups=near, tiled=True
        )

    def exchange_wide(arr):
        return lax.all_to_all(arr, "wide", split_axis=0, concat_axis=0, tiled=True)

    def shift(arr, source, target):
        pairs = [(source * groups + j, target * groups + j) for j in range(groups)]
        return lax.ppermute(arr, "narrow", pairs)

    def swap(arr, step):
        pairs = [(i, i ^ step) for i in range(narrow)]
        return lax.ppermute(arr, "narrow", pairs)

    def spread(pieces):
        return [swap(piece, step) if step else piece for step, piece in enumerate(pieces)]

    wide_index = lax.axis_index("wide")
    narrow_index = lax.axis_index("narrow")
    half = narrow_index // groups
    near_index = narrow_index % groups
    first_col = lax.dynamic_index_in_dim(row_start, wide_index, keepdims=False)
    block_id = (half * half_cols + wide_index * cols) // CB
    first_row = lax.dynamic_index_in_dim(col_start, block_id, keepdims=False)
    scal = jnp.stack([half, first_col, first_row, near_index]).astype(jnp.int32)

    far_first, far_second, packed = pack(key_in, value_in, query_in, grad_out, groups, subs, cols)
    near_feats = feats // groups
    heads = near_feats // HEAD
    near_heads = heads // HALVES
    far_first = swap(far_first, groups)
    token = hold([far_first], FIRST_UNITS)
    far_second = swap(far_second, groups)
    t = exchange_near(packed).reshape(lanes, 4, cols, near_feats)
    t, token = lax.optimization_barrier((t, token))
    by_col = exchange_wide(t)
    pieces = spread(split(far_first, far_second, token))
    diag_part = stats_call(row_stats_body, scale, scal, (t,), "row_stats", 4)
    own_off = off_stats(scale, scal, t, pieces)
    off_part = jnp.concatenate([shift(own_off, 0, 1), own_off])
    lse, delta = merge(diag_part[:, 0], diag_part[:, 1], off_part[:, 0], off_part[:, 1])
    row_part = jnp.where(half == 1, jnp.stack([lse, delta], axis=1), diag_part)
    col_part = col_stats(scale, scal, by_col)

    both = jnp.stack([row_part, col_part]).reshape(4 * heads, lanes, cols)
    sent = both.transpose(1, 0, 2).reshape(lanes, (4 * heads * cols) // HEAD, HEAD)
    got = exchange_wide(sent).reshape(lanes, 4 * heads, cols).transpose(1, 0, 2)
    got = got.reshape(2, heads, 2, lanes * cols)
    row_lse, row_delta = merge(row_part[:, 0], row_part[:, 1], got[1, :, 0], got[1, :, 1])
    row_full = jnp.stack([row_lse, row_delta], axis=1)

    far_full = shift(row_full[:near_heads], 1, 0)
    token = hold([far_full], FULL_UNITS)
    from_col = exchange_wide(col_grads(scale, scal, by_col, col_part, got[0]))
    off_full = jnp.where(half == 1, row_full[near_heads:], far_full)
    off_terms, far_terms = off_grads(scale, scal, t, off_full, token, pieces)
    row_terms = row_grads(scale, scal, t, row_full, off_terms)
    by_step = [
        lax.dynamic_index_in_dim(far_terms, near_index ^ step, keepdims=False)
        for step in range(groups)
    ]
    by_step = spread(by_step)
    far_terms, far_value = (jnp.stack([piece[a] for piece in by_step]) for a in range(2))
    from_col, far_terms, far_value, row_terms = lax.optimization_barrier(
        (from_col, far_terms, far_value, row_terms)
    )
    far_value = shift(far_value, 1, 0)
    far_terms = swap(far_terms, groups)
    token = hold([far_terms, far_value], BACK_UNITS)
    joined = join(row_terms, from_col)
    out = exchange_near(joined.reshape(groups, subs, 3, cols, near_feats))
    return unpack(scal, out, far_terms, far_value, token, tokens, feats)


def solution(mesh):
    placed = P(("wide", "narrow"), None)
    return jax.shard_map(
        body,
        mesh=mesh,
        in_specs=(placed,) * 4 + (P(), P()),
        out_specs=(placed,) * 3,
        check_vma=False,
    )
```
